32 devices in a mesh: rep: 2 (over x), shard: 16 (over z, y, core).
Axes of the slice: x: 2, y: 2, z: 4, core: 2. Of those that a mesh axis runs over, the one named last changes fastest.
Arguments:
- tokens: bfloat16 [4096, 768], P(('rep', 'shard')), may hold values from -6 to 6
- cotangent: bfloat16 [4096, 768], P(('rep', 'shard')), may hold values from -6 to 6
- lengths: int32 [32, 3], P(('rep', 'shard')), may hold values from 1 to 96, 128 in all within a row
- routes: int32 [4096, 1], P(('rep', 'shard')), may hold values from 0 to 1; in each aligned block of 128 rows (0 to 127, 128 to 255, ...) at most 80 rows name the same one
- bucket_ids: int32 [255], replicated, may hold values from 0 to 31
- attn_in: bfloat16 [3, 768, 768], P(None, 'shard'), may hold values from -0.21875 to 0.21875
- attn_out: bfloat16 [768, 768], P('shard'), may hold values from -0.875 to 0.875
- gains: bfloat16 [2, 768], P(None, 'shard'), may hold values from 0.25 to 1.75
- router: bfloat16 [768, 2], P('shard'), may hold values from -0.109375 to 0.109375
- rel_table: bfloat16 [32, 12], P('shard'), may hold values from -4 to 4
- expert_in: bfloat16 [2, 768, 3072], P(None, 'shard'), may hold values from -0.21875 to 0.21875
- expert_out: bfloat16 [2, 3072, 768], P(None, 'shard'), may hold values from -0.21875 to 0.21875
Outputs:
- layer_out: bfloat16 [4096, 768], P(('rep', 'shard'))
- input_grad: float32 [4096, 768], P(('rep', 'shard'))
- grad_attn_in: float32 [3, 768, 768], P(None, 'shard')
- grad_attn_out: float32 [768, 768], P('shard')
- grad_gains: float32 [2, 768], P(None, 'shard')
- grad_router: float32 [768, 2], P('shard')
- grad_rel_table: float32 [32, 12], P('shard')
- grad_expert_in: float32 [2, 768, 3072], P(None, 'shard')
- grad_expert_out: float32 [2, 3072, 768], P(None, 'shard')
The draws below stay inside these ranges and needn't reach their ends.
Inputs may be any that keep to these rules, and one draw needn't show every extreme that they name: Row b holds the lengths of the 3 sequences of device block b; they sum to 128, and some block has one of exactly 96. `routes`: within the 128 rows of one device no expert is named more than 80 times, and in every draw some device names some expert exactly 80 times.
All inputs are finite; a program needn't handle non-finite values.
Results may differ from the reference program's by a relative error of at most 0.012.
Values may be sent and summed in bfloat16 or wider, within the bound.
A program may use at most 192 MiB of HBM per device.

```python
import math
import jax
import jax.numpy as jnp
import numpy as np
from jax import lax

D = 768
H = 12
HD = 64
FF = 3072
BUCKETS = 32
E = 2
SEQ_DEV = 3
TOK_DEV = 128
CAP = 80
MAX_LEN = 96
BLOCKS = 32
TOKENS = 4096


def place_ends(entries, stream_key, least, high):
    extent = entries.shape
    spot = [jax.random.randint(jax.random.fold_in(stream_key, axis), (), 0, extent[axis]) for axis in range(len(extent))]
    entries = entries.at[tuple(spot)].set(least)
    longest = extent.index(max(extent))
    spot[longest] = (spot[longest] + 1) % extent[longest]
    return entries.at[tuple(spot)].set(high)


def level_of(own_key, extent, pieces, smallest, top_value):
    factor_of, own = 1.0, jax.random.fold_in(own_key, 6)
    for position, shards_of in pieces:
        steps = jnp.exp(jax.random.uniform(jax.random.fold_in(own, position), (shards_of,), jnp.float32, smallest / len(pieces), top_value / len(pieces)))
        factor_of = factor_of * jnp.repeat(steps, extent[position] // shards_of).reshape([-1 if axis == position else 1 for axis in range(len(extent))])
    return factor_of


def profile(amount, total, most, slope):
    loads = [(1 << 20) // math.isqrt(rank ** slope) + 1 for rank in range(2, amount + 1)]
    rest, counts = total - most - (amount - 1), [1] * (amount - 1)
    while rest > 0:
        candidates = [i for i in range(amount - 1) if counts[i] < most]
        whole, remaining = sum([loads[i] for i in candidates]), rest
        for i in candidates:
            extra = min(most - counts[i], max(1, remaining * loads[i] // whole), rest)
            counts[i] = counts[i] + extra
            rest = rest - extra
    return np.array([most] + counts)


def ragged_sizes(key, count, total, limit, lean):
    if count == 2:
        one = jax.random.randint(key, (), max(1, total - limit), min(limit, total - 1) + 1)
        return jnp.stack([one, total - one])
    sizes = jnp.asarray(profile(count, total, limit, lean), jnp.int32)
    pairs = (count - 1) // 2
    giver, receiver = sizes[1:1 + 2 * pairs:2], sizes[2:2 + 2 * pairs:2]
    room = jnp.minimum(giver - 1, limit - receiver)
    shifted = jax.random.randint(jax.random.fold_in(key, 1), (pairs,), 0, 1 << 20) % (room + 1)
    sizes = sizes.at[1:1 + 2 * pairs:2].set(giver - shifted).at[2:2 + 2 * pairs:2].set(receiver + shifted)
    return sizes[jax.random.permutation(jax.random.fold_in(key, 2), count)]


def deal_out(key, own, number, rows, count, top, most, slope):
    sequence = jax.random.permutation(key, count)
    packed, ordinary = portions_of(count, rows * top, most, slope, True), portions_of(count, rows * top, most, slope, False)
    places = jnp.arange(count)

    def named(sizes, turn):
        used = int((sizes > 0).sum())
        fixed = max(1, used // 4)
        moved = fixed + (places - fixed + turn * (used - fixed)) % max(1, count - fixed)
        return jnp.zeros((count,), jnp.int32).at[sequence[jnp.where(places < fixed, places, moved)]].set(jnp.asarray(sizes, jnp.int32))

    sizes = jnp.where(number % 4 == 0, named(packed, number // 4), named(ordinary, number - number // 4 - 1))
    mixed = jax.random.permutation(jax.random.fold_in(own, 3), count)
    giver, taker = mixed[0:count // 2 * 2:2], mixed[1:count // 2 * 2:2]
    slack = jnp.minimum(sizes[giver] - 1, most - sizes[taker]) // 2
    slack = jnp.where((giver == sequence[0]) | (taker == sequence[0]) | (sizes[taker] == 0), 0, jnp.maximum(slack, 0))
    moved = jax.random.randint(jax.random.fold_in(own, 4), (count // 2,), 0, 1 << 20) % (slack + 1)
    sizes = sizes.at[giver].add(-moved).at[taker].add(moved)
    labels = jnp.searchsorted(jnp.cumsum(sizes), jnp.arange(rows * top), side="right").astype(jnp.int32)
    listing = labels.reshape(top, rows).T
    listing = listing[jax.random.permutation(jax.random.fold_in(own, 1), rows)]
    turn = jax.random.randint(jax.random.fold_in(own, 2), (rows, 1), 0, top)
    return jnp.take_along_axis(listing, (jnp.arange(top)[None, :] + turn) % top, axis=1)


def portions_of(number_of, total, bound, lean, full):
    weights = [(1 << 20) // math.isqrt(grade ** lean) + 1 for grade in range(1, number_of + 1)]
    largest = bound if full else min(bound, max(-(-total // number_of), total * weights[0] // sum(weights)))
    least = 1 if total - largest >= number_of - 1 else 0
    holding, rest = [largest] + [least] * (number_of - 1), total - largest - least * (number_of - 1)
    while rest > 0:
        movable = [i for i in range(1, number_of) if holding[i] < largest] or [i for i in range(1, number_of) if holding[i] < bound]
        pool, remaining = sum([weights[i] for i in movable]), rest
        for i in movable:
            addition = min(bound - holding[i], max(1, remaining * weights[i] // pool), rest)
            holding[i] = holding[i] + addition
            rest = rest - addition
    return np.array(holding)


def normal_values(stream_key, shape, scale, limit, cuts=(), kind=jnp.bfloat16):
    level = level_of(stream_key, shape, cuts, -0.22, 0.18) if cuts else 1.0
    values = jax.random.normal(stream_key, shape, jnp.float32) * scale * level
    return jnp.minimum(jnp.maximum(values, -limit), limit).astype(kind)


def setup_inputs(seed: int = 0) -> dict:
    key_list = jax.random.split(jax.random.key(seed), 13)
    tokens = normal_values(key_list[0], (TOKENS, D), 1.0, 6.0, ((0, 32),))
    cotangent = normal_values(key_list[1], (TOKENS, D), 1.0, 6.0, ((0, 32),))
    lengths = jax.vmap(lambda own: ragged_sizes(own, SEQ_DEV, TOK_DEV, MAX_LEN, 2))(jax.random.split(key_list[2], BLOCKS)).reshape((BLOCKS, SEQ_DEV)).astype(jnp.int32)
    routes_keys = jax.random.split(jax.random.fold_in(key_list[3], 1), TOKENS // TOK_DEV)
    routes_turns = jax.random.permutation(jax.random.fold_in(key_list[3], 3), TOKENS // TOK_DEV)
    routes = jax.vmap(lambda own, number: deal_out(jax.random.fold_in(key_list[3], 2), own, number, TOK_DEV, E, 1, CAP, 1))(routes_keys, routes_turns).reshape((TOKENS, 1))
    bucket_ids = place_ends(jax.random.randint(key_list[4], (2 * TOK_DEV - 1,), 0, BUCKETS), jax.random.fold_in(key_list[4], 1), 0, BUCKETS - 1).astype(jnp.int32)
    attn_in = normal_values(key_list[5], (3, D, D), D ** -0.5, 0.21875, ((1, 16),))
    attn_out = normal_values(key_list[6], (D, D), (D // 16) ** -0.5, 0.875, ((0, 16),))
    gains = jnp.clip(1.0 + 0.15 * jax.random.normal(key_list[7], (2, D), jnp.float32), 0.25, 1.75).astype(jnp.bfloat16)
    router = normal_values(key_list[8], (D, E), (4 * D) ** -0.5, 0.109375, ((0, 16),))
    rel_table = normal_values(key_list[9], (BUCKETS, H), 1.0, 4.0, ((0, 16),))
    expert_in = normal_values(key_list[10], (E, D, FF), D ** -0.5, 0.21875, ((1, 16),))
    expert_out = normal_values(key_list[11], (E, FF, D), (FF // 4) ** -0.5, 0.21875, ((1, 16),))
    return {"tokens": tokens, "cotangent": cotangent, "lengths": lengths, "routes": routes, "bucket_ids": bucket_ids, "attn_in": attn_in, "attn_out": attn_out, "gains": gains, "router": router, "rel_table": rel_table, "expert_in": expert_in, "expert_out": expert_out}


@jax.custom_vjp
def low(v):
    return lax.optimization_barrier(v.astype(jnp.bfloat16)).astype(jnp.float32)

@jax.custom_vjp
def low_back(v):
    return v

def low_keep(v):
    return (low(v), None)

def low_pass(kept, grad):
    return (grad,)

def back_keep(v):
    return (v, None)

def back_low(kept, grad):
    return (low(grad),)
low.defvjp(low_keep, low_pass)
low_back.defvjp(back_keep, back_low)

def rms_norm(values, gain):
    return values * lax.rsqrt(lax.optimization_barrier(jnp.mean(values * values, axis=-1, keepdims=True)) + 1e-06) * gain

def block_layer(params, tokens, lengths, routes, bucket_ids):
    attn_in, attn_out, gains, router, rel_table, expert_in, expert_out = params
    highest = lax.Precision.HIGHEST
    rows = tokens.shape[0]
    normed = low(rms_norm(tokens, gains[0]))
    projected = low(low_back(jnp.einsum('td,kde->kte', normed, attn_in, precision=highest)))
    query = projected[0].reshape(rows, H, HD)
    keys = projected[1].reshape(rows, H, HD)
    values = projected[2].reshape(rows, H, HD)
    raw = low_back(jnp.einsum('qhc,khc->hqk', query, keys, precision=highest) * 0.125)
    places = jnp.arange(rows, dtype=jnp.int32)
    offsets = places[None, :] - places[:, None] + (rows - 1)
    buckets = jnp.take(bucket_ids, offsets, axis=0)
    bias = jnp.transpose(jnp.take(rel_table, buckets, axis=0), (2, 0, 1))
    ends = jnp.cumsum(lengths)
    segment = lax.optimization_barrier(jnp.sum((places[:, None] >= ends[None, :]).astype(jnp.int32), axis=1))
    allowed = segment[:, None] == segment[None, :]
    scores = jnp.where(allowed[None], raw + bias, -1e+30)
    peak = lax.optimization_barrier(jnp.max(scores, axis=-1, keepdims=True))
    expo = jnp.exp(scores - peak)
    probs = low(expo / lax.optimization_barrier(jnp.sum(expo, axis=-1, keepdims=True)))
    context = low(low_back(jnp.einsum('hqk,khc->qhc', probs, values, precision=highest))).reshape(rows, D)
    hidden = tokens + low_back(jnp.dot(context, attn_out, precision=highest))
    normed_ffn = low(rms_norm(hidden, gains[1]))
    logits = jnp.dot(normed_ffn, router, precision=highest)
    gate_probs = jax.nn.softmax(logits, axis=-1)
    chosen = routes[:, 0]
    picked = chosen[:, None] == jnp.arange(E, dtype=jnp.int32)[None, :]
    gate = lax.optimization_barrier(jnp.sum(jnp.where(picked, gate_probs, 0.0), axis=1))
    ranks = jnp.cumsum(picked.astype(jnp.int32), axis=0) - 1
    slot = chosen * CAP + lax.optimization_barrier(jnp.sum(jnp.where(picked, ranks, 0), axis=1))
    dispatch = (jnp.arange(E * CAP, dtype=jnp.int32)[:, None] == slot[None, :]).astype(jnp.float32)
    buffers = jnp.dot(dispatch, normed_ffn, precision=highest).reshape(E, CAP, D)
    before = low_back(jnp.einsum('ecd,edf->ecf', buffers, expert_in, precision=highest))
    active = low(jax.nn.gelu(before, approximate=True))
    returned = low_back(jnp.einsum('ecf,efd->ecd', active, expert_out, precision=highest)).reshape(E * CAP, D)
    gathered = jnp.take(returned, slot, axis=0)
    return hidden + gate[:, None] * gathered

def reference(tokens, cotangent, lengths, routes, bucket_ids, attn_in, attn_out, gains, router, rel_table, expert_in, expert_out):
    params = (attn_in.astype(jnp.float32), attn_out.astype(jnp.float32), gains.astype(jnp.float32), router.astype(jnp.float32), rel_table.astype(jnp.float32), expert_in.astype(jnp.float32), expert_out.astype(jnp.float32))
    token_blocks = tokens.astype(jnp.float32).reshape(BLOCKS, TOK_DEV, D)
    route_blocks = routes.reshape(BLOCKS, TOK_DEV, 1)

    def forward(weights, inputs):

        def single(items):
            return block_layer(weights, items[0], items[1], items[2], bucket_ids)
        return lax.map(jax.checkpoint(single), (inputs, lengths, route_blocks))
    result, pullback = jax.vjp(forward, params, token_blocks)
    param_grads, token_grads = pullback(cotangent.astype(jnp.float32).reshape(BLOCKS, TOK_DEV, D))
    return (result.reshape(TOKENS, D).astype(jnp.bfloat16), token_grads.reshape(TOKENS, D), param_grads[0], param_grads[1], param_grads[2], param_grads[3], param_grads[4], param_grads[5], param_grads[6])
```

```python
import functools

import jax
import jax.numpy as jnp
from jax import lax
from jax.experimental import pallas as pl
from jax.experimental.pallas import tpu as pltpu
from jax.sharding import PartitionSpec as P

EPSILON = 1e-06
SMALL = 16
LOW = jnp.bfloat16
WIDE = jnp.float32
NT = (((1,), (1,)), ((), ()))
TN = (((0,), (0,)), ((), ()))
MESH = pl.DeviceIdType.MESH
VMEM = pl.BlockSpec(memory_space=pltpu.VMEM)
SMEM = pl.BlockSpec(memory_space=pltpu.SMEM)
DMA = pltpu.SemaphoreType.DMA


def grid_of(size):
    chips = size // 2
    outer = 4 if chips % 4 == 0 else 1
    return outer, chips // outer


class Place:
    def __init__(self, size):
        self.size = size
        self.outer, self.inner = grid_of(size)
        self.chips = size // 2
        me = lax.axis_index("shard")
        self.core = lax.rem(me, 2)
        self.chip = lax.div(me, 2)
        self.z = lax.div(self.chip, self.inner)
        self.y = lax.rem(self.chip, self.inner)

    def at(self, dz, dy):
        far = lax.rem(self.z + dz + self.outer, self.outer)
        near = lax.rem(self.y + dy + self.inner, self.inner)
        return far * self.inner + near

    def device(self, chip):
        return {"shard": chip * 2 + self.core}

    def partner(self):
        return {"shard": self.chip * 2 + 1 - self.core}

    def step(self, d, e):
        if d == 0:
            return e
        if e == 0:
            return self.inner + d - 1
        return self.inner + self.outer - 1 + (d - 1) * (self.inner - 1) + e - 1

    def pairs(self):
        order = [(0, e) for e in range(self.inner)]
        order += [(d, 0) for d in range(1, self.outer)]
        order += [(d, e) for d in range(1, self.outer) for e in range(1, self.inner)]
        return order

    def pair(self, i):
        inner, outer = self.inner, self.outer
        j = i - (inner + outer - 1)
        side = max(inner - 1, 1)
        d = jnp.where(i < inner, 0, jnp.where(j < 0, i - inner + 1, 1 + lax.div(j, side)))
        e = jnp.where(i < inner, i, jnp.where(j < 0, 0, 1 + lax.rem(j, side)))
        return d, e

    def greet(self, chips, reps):
        barrier = pltpu.get_barrier_semaphore()
        count = 0

        def signal(target):
            pl.semaphore_signal(barrier, inc=1, device_id=target, device_id_type=MESH)

        for dz, dy in self.pairs()[1:]:
            if chips or dz == 0 or dy == 0:
                signal(self.device(self.at(dz, dy)))
                count += 1
        signal(self.partner())
        count += 1
        for f in range(1, reps):
            signal({"rep": lax.rem(lax.axis_index("rep") + f, reps)})
            count += 1
        pl.semaphore_wait(barrier, count)


def remote(src, dst, send_sem, recv_sem, target):
    return pltpu.make_async_remote_copy(
        src_ref=src,
        dst_ref=dst,
        send_sem=send_sem,
        recv_sem=recv_sem,
        device_id=target,
        device_id_type=MESH,
    )


def dot(a, b, dims=None):
    if dims is None:
        return jnp.dot(a, b, preferred_element_type=WIDE)
    return lax.dot_general(a, b, dims, preferred_element_type=WIDE)


def joined(ref, first, rows, pad):
    chips, _, _, width = ref.shape
    if rows == pad:
        return ref[:, :, first : first + rows, :].reshape(chips * 2 * rows, width)
    parts = [ref[j // 2, j % 2, first : first + rows, :].astype(WIDE) for j in range(chips * 2)]
    return jnp.concatenate(parts, axis=0).astype(LOW)


def split(ref, first, rows, pad, values):
    chips, _, _, width = ref.shape
    if rows == pad:
        ref[:, :, first : first + rows, :] = values.reshape(chips, 2, rows, width).astype(LOW)
        return
    for j in range(chips * 2):
        ref[j // 2, j % 2, first : first + rows, :] = values[j * rows : (j + 1) * rows].astype(LOW)


def rms_scale(values):
    return lax.rsqrt(jnp.mean(values * values, axis=1, keepdims=True) + EPSILON)


def gate_of(logits, route):
    first, second = logits[:, 2:3], logits[:, 3:4]
    top = jnp.maximum(first, second)
    first, second = jnp.exp(first - top), jnp.exp(second - top)
    total = first + second
    first, second = first / total, second / total
    return first, second, jnp.where(route > 0.5, second, first)


def gather_start(place, own, slots, send_sem, recv_sem):
    for d, e in place.pairs()[1:]:
        if d == 0 or e == 0:
            i = place.step(d, e)
            target = place.device(place.at(d, e))
            remote(own, slots.at[place.chip], send_sem.at[i], recv_sem.at[i], target).start()


def gather_arrive(place, i, own, slots, send_sem, recv_sem):
    d, e = place.pair(i)
    source = place.at(-d, -e)
    remote(own, slots.at[source], send_sem.at[i], recv_sem.at[i], place.device(source)).wait_recv()

    @pl.when(jnp.logical_and(d > 0, e == 0))
    def _():
        for side in range(1, place.inner):
            j = place.inner + place.outer - 1 + (d - 1) * (place.inner - 1) + side - 1
            target = place.device(place.at(0, side))
            remote(
                slots.at[source], slots.at[source], send_sem.at[j], recv_sem.at[j], target
            ).start()

    return source


def front_kernel(
    size,
    heads,
    tok_ref,
    in_ref,
    out_ref,
    small_ref,
    strip_ref,
    half_ref,
    bucket_ref,
    length_ref,
    whole_ref,
    w1_ref,
    w2_ref,
    normed_ref,
    proj_ref,
    probs_ref,
    context_ref,
    hidden_ref,
    ffn_ref,
    sum_ref,
    route_ref,
    g_send,
    g_recv,
    c_send,
    c_recv,
    s_send,
    s_recv,
    d_send,
    d_recv,
    h_send,
    h_recv,
    own_sem,
):
    place = Place(size)
    chips = place.chips
    core, chip = place.core, place.chip
    length, width = tok_ref.shape
    rows = out_ref.shape[0]
    pad = w1_ref.shape[2]
    head_size = width // heads
    mine = whole_ref.at[chip, core]
    for k in range(3):
        whole_ref[chip, core, k * pad : k * pad + rows, :] = in_ref[k]
    whole_ref[chip, core, 3 * pad : 3 * pad + rows, :] = out_ref[...]
    whole_ref[chip, core, 4 * pad : 4 * pad + SMALL, :] = small_ref[...]
    place.greet(True, 1)
    partner = place.partner()
    slots = whole_ref.at[:, core]
    gather_start(place, mine, slots, g_send, g_recv)

    def dup(i, source):
        return remote(
            whole_ref.at[source, core],
            whole_ref.at[source, core],
            c_send.at[i],
            c_recv.at[i],
            partner,
        )

    dup(0, chip).start()
    local = [
        pltpu.make_async_copy(strip_ref.at[chip], w1_ref.at[chip, core], own_sem.at[0]),
        pltpu.make_async_copy(half_ref, w2_ref.at[:, core], own_sem.at[1]),
    ]
    for copy in local:
        copy.start()
    halves = remote(half_ref, w2_ref.at[:, core], h_send, h_recv, partner)
    halves.start()

    def arrive(i, carry):
        source = gather_arrive(place, i, mine, slots, g_send, g_recv)
        dup(i, source).start()
        return carry

    lax.fori_loop(1, place.inner + place.outer - 1, arrive, 0)
    strips = []
    for i, (d, e) in enumerate(place.pairs()):
        if i > 0:
            target = place.at(d, e)
            copy = remote(
                strip_ref.at[target],
                w1_ref.at[chip, core],
                s_send.at[i],
                s_recv.at[i],
                place.device(target),
            )
            copy.start()
            strips.append(copy)
    lax.fori_loop(place.inner + place.outer - 1, chips, arrive, 0)

    def other(i, carry):
        d, e = place.pair(i)
        source = place.at(-d, -e)
        remote(
            whole_ref.at[source, core],
            whole_ref.at[source, 1 - core],
            c_send.at[i],
            c_recv.at[i],
            partner,
        ).wait_recv()
        return carry

    lax.fori_loop(0, chips, other, 0)

    total = jnp.zeros((SMALL, width), WIDE)
    for j in range(size):
        total = total + whole_ref[j // 2, j % 2, 4 * pad : 4 * pad + SMALL, :].astype(WIDE)
    sum_ref[...] = total
    lines = [
        whole_ref[k, core, 4 * pad : 4 * pad + SMALL, length : 2 * length].astype(WIDE)[4:5]
        for k in range(chips)
    ]
    lines.append(jnp.zeros((length - chips, length), WIDE))
    route_ref[...] = jnp.transpose(jnp.concatenate(lines, axis=0))

    inputs = tok_ref[...].astype(WIDE)
    normed = (inputs * rms_scale(inputs) * total[0:1]).astype(LOW)
    normed_ref[...] = normed
    for k in range(3):
        proj_ref[k] = dot(normed, joined(whole_ref, k * pad, rows, pad)).astype(LOW)
    spots = lax.broadcasted_iota(jnp.int32, (length, 2 * length), 0)
    onehot = jnp.where(bucket_ref[...] == spots, 1.0, 0.0).astype(LOW)
    table = total[:, :length].astype(LOW)
    bias = dot(table, onehot)
    down = lax.broadcasted_iota(jnp.int32, (length, length), 0)
    across = lax.broadcasted_iota(jnp.int32, (length, length), 1)
    part_q = jnp.zeros((length, length), jnp.int32)
    part_k = jnp.zeros((length, length), jnp.int32)
    end = jnp.int32(0)
    for s in range(length_ref.shape[1]):
        end = end + length_ref[0, s]
        part_q = part_q + jnp.where(down >= end, 1, 0)
        part_k = part_k + jnp.where(across >= end, 1, 0)
    allowed = part_q == part_k
    parts = []
    for h in range(heads):
        at = slice(h * head_size, (h + 1) * head_size)
        raw = dot(proj_ref[0, :, at], proj_ref[1, :, at], NT)
        spread = jnp.broadcast_to(bias[4 + h : 5 + h, :], (length, 2 * length))
        skewed = pltpu.roll(spread, length + 1, 1, stride=1, stride_axis=0)
        scores = jnp.where(allowed, raw * 0.125 + skewed[:, :length], -1e30)
        expo = jnp.exp(scores - jnp.max(scores, axis=1, keepdims=True))
        probs = expo / jnp.sum(expo, axis=1, keepdims=True)
        probs_ref[h] = probs
        parts.append(dot(probs.astype(LOW), proj_ref[2, :, at]))
    context = jnp.concatenate(parts, axis=1).astype(LOW)
    context_ref[...] = context
    hidden = inputs + dot(context, joined(whole_ref, 3 * pad, rows, pad))
    hidden_ref[...] = hidden
    ffn_ref[...] = (hidden * rms_scale(hidden) * total[1:2]).astype(LOW)

    def pass_on(i, carry):
        d, e = place.pair(i)
        source = place.at(-d, -e)
        block = w1_ref.at[source, core]
        remote(block, block, s_send.at[i], s_recv.at[i], partner).wait_recv()
        remote(block, block, d_send.at[i], d_recv.at[i], partner).start()
        return carry

    local[0].wait()
    remote(w1_ref.at[chip, core], w1_ref.at[chip, core], d_send.at[0], d_recv.at[0], partner).start()
    lax.fori_loop(1, chips, pass_on, 0)

    def last(i, carry):
        d, e = place.pair(i)
        source = place.at(-d, -e)
        block = w1_ref.at[source, 1 - core]
        sent = w1_ref.at[source, core]
        remote(sent, block, d_send.at[i], d_recv.at[i], partner).wait()
        remote(
            whole_ref.at[source, core], whole_ref.at[source, core], c_send.at[i], c_recv.at[i], partner
        ).wait_send()
        return carry

    lax.fori_loop(0, chips, last, 0)

    def sent(i, carry):
        remote(mine, mine, g_send.at[i], g_recv.at[i], partner).wait_send()
        remote(
            strip_ref.at[0], w1_ref.at[chip, core], s_send.at[i], s_recv.at[i], partner
        ).wait_send()
        return carry

    lax.fori_loop(1, chips, sent, 0)
    local[1].wait()
    halves.wait()


def front(size, tokens, attn_in, attn_out, small, strips, halves, buckets, lengths, heads):
    chips = size // 2
    length, width = tokens.shape
    rows = attn_out.shape[0]
    pad = strips.shape[1]
    cols = strips.shape[2]
    depth = 4 * pad + SMALL
    sems = [DMA((chips,))] * 8
    return pl.pallas_call(
        functools.partial(front_kernel, size, heads),
        out_shape=(
            jax.ShapeDtypeStruct((chips, 2, depth, width), LOW),
            jax.ShapeDtypeStruct((chips, 2, pad, cols), LOW),
            jax.ShapeDtypeStruct((2, 2) + halves.shape[1:], LOW),
            jax.ShapeDtypeStruct((length, width), LOW),
            jax.ShapeDtypeStruct((3, length, width), LOW),
            jax.ShapeDtypeStruct((heads, length, length), WIDE),
            jax.ShapeDtypeStruct((length, width), LOW),
            jax.ShapeDtypeStruct((length, width), WIDE),
            jax.ShapeDtypeStruct((length, width), LOW),
            jax.ShapeDtypeStruct((SMALL, width), WIDE),
            jax.ShapeDtypeStruct((length, length), WIDE),
        ),
        in_specs=[VMEM] * 7 + [SMEM],
        out_specs=[VMEM] * 11,
        scratch_shapes=[*sems, DMA, DMA, DMA((2,))],
        compiler_params=pltpu.CompilerParams(
            collective_id=0, has_side_effects=True, vmem_limit_bytes=50 << 20
        ),
    )(tokens, attn_in, attn_out, small, strips, halves, buckets, lengths)


def expert_kernel(
    size,
    reps,
    rows,
    x_ref,
    u_ref,
    w1_ref,
    w2_ref,
    sum_ref,
    route_ref,
    ret_ref,
    back_ref,
    g1_ref,
    g2_ref,
    xs,
    us,
    act,
    slope,
    scaled,
    before_grad,
    part,
    y_buf,
    z_out,
    z_in,
    g1_own,
    g1_got,
    g2_own,
    g2_got,
    g2_all,
    x_send,
    x_recv,
    u_send,
    u_recv,
    y_send,
    y_recv,
    z_send,
    z_recv,
    p_send,
    p_recv,
    r_send,
    r_recv,
    own_sem,
):
    place = Place(size)
    chips, outer, inner = place.chips, place.outer, place.inner
    core, chip = place.core, place.chip
    rep = lax.axis_index("rep")
    length, width = x_ref.shape
    cols = w1_ref.shape[1]
    strip = cols // 2
    pad = g1_own.shape[2]
    place.greet(False, reps)
    partner = place.partner()
    gather_start(place, x_ref, xs, x_send, x_recv)
    own = [
        pltpu.make_async_copy(x_ref, xs.at[chip], own_sem.at[0]),
        pltpu.make_async_copy(u_ref, us.at[chip], own_sem.at[1]),
    ]
    for copy in own:
        copy.start()
    for copy in own:
        copy.wait()
    lane = lax.broadcasted_iota(jnp.int32, (length, length), 1)
    side = lax.broadcasted_iota(jnp.int32, (length, cols), 1) >= strip
    router = sum_ref[...].astype(LOW)

    def route_of(k):
        return jnp.sum(jnp.where(lane == k, route_ref[...], 0.0), axis=1, keepdims=True)

    def y_copy(q, i, d, e):
        k = place.at(-d, -e)
        return remote(
            part.at[q, k],
            y_buf.at[q, i],
            y_send.at[q, i],
            y_recv.at[q, i],
            place.device(place.at(0, -e)),
        )

    def z_copy(q, d):
        return remote(
            z_out.at[q, d - 1],
            z_in.at[q, d - 1],
            z_send.at[q, d - 1],
            z_recv.at[q, d - 1],
            place.device(place.at(-d, 0)),
        )

    def forward(i, carry):
        @pl.when(i > 0)
        def _():
            gather_arrive(place, i, x_ref, xs, x_send, x_recv)

        d, e = place.pair(i)
        k = place.at(-d, -e)
        before = dot(xs[k], w1_ref[...])
        keep = jnp.logical_xor(side, route_of(k) < 0.5)
        square = before * before
        bent = jnp.tanh(0.7978845608 * before * (1.0 + 0.044715 * square))
        half = 0.5 * (1.0 + bent)
        rise = half + 0.5 * before * (1.0 - bent * bent) * 0.7978845608 * (
            1.0 + 0.134145 * square
        )
        active = jnp.where(keep, before * half, 0.0).astype(LOW)
        act[k] = active
        slope[k] = jnp.where(keep, rise, 0.0)
        part[0, k] = dot(active, w2_ref[...]).astype(LOW)

        @pl.when(e > 0)
        def _():
            y_copy(0, i, d, e).start()

        return carry

    lax.fori_loop(0, inner + 1, forward, 0)
    gather_start(place, u_ref, us, u_send, u_recv)
    lax.fori_loop(inner + 1, chips, forward, 0)

    def collect(q, d):
        def add(k, carry):
            at = pl.ds(pl.multiple_of(k * 16, 16), 16)
            value = part[q, place.at(-d, 0), at].astype(WIDE)
            for e in range(1, inner):
                value = value + y_buf[q, place.step(d, e), at].astype(WIDE)
            if d == 0:
                target = ret_ref if q == 0 else back_ref
                target[at] = value
            else:
                z_out[q, d - 1, at] = value.astype(LOW)
            return carry

        for e in range(1, inner):
            y_copy(q, place.step(d, e), d, e).wait_recv()
        lax.fori_loop(0, length // 16, add, 0, unroll=True)
        if d > 0:
            z_copy(q, d).start()

    def backward(i, carry):
        @pl.when(i > 0)
        def _():
            gather_arrive(place, i, u_ref, us, u_send, u_recv)

        d, e = place.pair(i)
        k = place.at(-d, -e)
        gate = gate_of(dot(xs[k], router, NT), route_of(k))[2]
        low = (gate * us[k].astype(WIDE)).astype(LOW)
        scaled[k] = low
        grad = (dot(low, w2_ref[...], NT) * slope[k]).astype(LOW)
        before_grad[k] = grad
        part[1, k] = dot(grad, w1_ref[...], NT).astype(LOW)

        @pl.when(e > 0)
        def _():
            y_copy(1, i, d, e).start()

        return carry

    lax.fori_loop(0, inner + outer - 1, backward, 0)
    for d in range(1, outer):
        collect(0, d)
    lax.fori_loop(inner + outer - 1, chips, backward, 0)
    collect(0, 0)

    def flat(ref):
        return ref[...].reshape(chips * length, ref.shape[2])

    g2 = dot(flat(act), flat(scaled), TN)
    g2_own[...] = g2.astype(LOW).reshape(g2_own.shape)
    g2_swap = remote(g2_own.at[:, 1 - core], g2_got, p_send.at[0], p_recv.at[0], partner)
    g2_swap.start()
    for d in range(1, outer):
        collect(1, d)
    g2_swap.wait()
    g2_all[rep] = (g2_own[:, core].astype(WIDE) + g2_got[...].astype(WIDE)).astype(LOW)
    swaps = []
    for f in range(1, reps):
        swaps.append(
            remote(
                g2_all.at[rep],
                g2_all.at[rep],
                r_send.at[f - 1],
                r_recv.at[f - 1],
                {"rep": lax.rem(rep + f, reps)},
            )
        )
        swaps[-1].start()
    g1 = dot(flat(xs), flat(before_grad), TN)
    split(g1_own, 0, rows, pad, g1)
    g1_swap = remote(g1_own.at[:, 1 - core], g1_got, p_send.at[1], p_recv.at[1], partner)
    g1_swap.start()
    collect(1, 0)

    def finish(q, target):
        for d in range(1, outer):
            z_copy(q, d).wait()

        def add(k, carry):
            at = pl.ds(pl.multiple_of(k * 16, 16), 16)
            value = target[at]
            for d in range(1, outer):
                value = value + z_in[q, d - 1, at].astype(WIDE)
            target[at] = value
            return carry

        lax.fori_loop(0, length // 16, add, 0, unroll=True)

    finish(0, ret_ref)
    g1_swap.wait()
    g1_ref[...] = (g1_own[:, core].astype(WIDE) + g1_got[...].astype(WIDE)).astype(LOW)
    for copy in swaps:
        copy.wait()
    value = g2_all[0].astype(WIDE)
    for r in range(1, reps):
        value = value + g2_all[r].astype(WIDE)
    g2_ref[...] = value
    finish(1, back_ref)

    def sent(i, carry):
        remote(x_ref, xs.at[0], x_send.at[i], x_recv.at[i], partner).wait_send()
        remote(u_ref, us.at[0], u_send.at[i], u_recv.at[i], partner).wait_send()
        d, e = place.pair(i)

        @pl.when(e > 0)
        def _():
            y_copy(0, i, d, e).wait_send()
            y_copy(1, i, d, e).wait_send()

        return carry

    lax.fori_loop(1, chips, sent, 0)


def expert(size, reps, rows, pad, x, u, w1, w2, small, routes):
    chips = size // 2
    outer = grid_of(size)[0]
    steps = max(outer - 1, 1)
    length, width = x.shape
    cols = w1.shape[1]
    half = cols // 4
    block = (chips, length, width)
    wide = (chips, length, cols)
    return pl.pallas_call(
        functools.partial(expert_kernel, size, reps, rows),
        out_shape=(
            jax.ShapeDtypeStruct((length, width), WIDE),
            jax.ShapeDtypeStruct((length, width), WIDE),
            jax.ShapeDtypeStruct((chips, pad, cols), LOW),
            jax.ShapeDtypeStruct((2, half, width), WIDE),
        ),
        in_specs=[VMEM] * 6,
        out_specs=[VMEM] * 4,
        scratch_shapes=[
            pltpu.VMEM(block, LOW),
            pltpu.VMEM(block, LOW),
            pltpu.VMEM(wide, LOW),
            pltpu.VMEM(wide, WIDE),
            pltpu.VMEM(block, LOW),
            pltpu.VMEM(wide, LOW),
            pltpu.VMEM((2,) + block, LOW),
            pltpu.VMEM((2,) + block, LOW),
            pltpu.VMEM((2, steps, length, width), LOW),
            pltpu.VMEM((2, steps, length, width), LOW),
            pltpu.VMEM((chips, 2, pad, cols), LOW),
            pltpu.VMEM((chips, pad, cols), LOW),
            pltpu.VMEM((2, 2, half, width), LOW),
            pltpu.VMEM((2, half, width), LOW),
            pltpu.VMEM((reps, 2, half, width), LOW),
            DMA((chips,)),
            DMA((chips,)),
            DMA((chips,)),
            DMA((chips,)),
            DMA((2, chips)),
            DMA((2, chips)),
            DMA((2, steps)),
            DMA((2, steps)),
            DMA((2,)),
            DMA((2,)),
            DMA((max(reps - 1, 1),)),
            DMA((max(reps - 1, 1),)),
            DMA((2,)),
        ],
        compiler_params=pltpu.CompilerParams(
            collective_id=1, has_side_effects=True, vmem_limit_bytes=56 << 20
        ),
    )(x, u, w1, w2, small, routes)


def back_kernel(
    size,
    reps,
    heads,
    rows,
    tok_ref,
    u_ref,
    hidden_ref,
    ffn_ref,
    normed_ref,
    proj_ref,
    probs_ref,
    context_ref,
    whole_ref,
    sum_ref,
    route_ref,
    turned_ref,
    ret_ref,
    norm_ref,
    g1_ref,
    layer_ref,
    input_ref,
    mine_ref,
    g1_out_ref,
    grads,
    got,
    kept,
    y_buf,
    z_out,
    z_in,
    total,
    rep_all,
    strips,
    s_send,
    s_recv,
    t_send,
    t_recv,
    p_send,
    p_recv,
    y_send,
    y_recv,
    z_send,
    z_recv,
    r_send,
    r_recv,
    own_sem,
):
    place = Place(size)
    chips, outer, inner = place.chips, place.outer, place.inner
    core, chip = place.core, place.chip
    rep = lax.axis_index("rep")
    length, width = tok_ref.shape
    head_size = width // heads
    depth = mine_ref.shape[0]
    pad = (depth - SMALL) // 4
    place.greet(True, reps)
    partner = place.partner()
    moves = []
    own = pltpu.make_async_copy(g1_ref.at[chip], strips.at[rep, chip], own_sem)
    own.start()
    for i, (d, e) in enumerate(place.pairs()):
        if i > 0:
            target = place.at(d, e)
            moves.append(
                remote(
                    g1_ref.at[target],
                    strips.at[rep, chip],
                    s_send.at[i],
                    s_recv.at[i],
                    place.device(target),
                )
            )
            moves[-1].start()

    router = sum_ref[2:4, :]
    upstream = u_ref[...].astype(WIDE)
    hidden = hidden_ref[...]
    returned = ret_ref[...]
    route = route_ref[...].astype(WIDE)
    logits = dot(ffn_ref[...], sum_ref[...].astype(LOW), NT)
    first, second, gate = gate_of(logits, route)
    layer_ref[...] = (hidden + gate * returned).astype(LOW)
    gate_grad = jnp.sum(upstream * returned, axis=1, keepdims=True)
    scaled = gate * gate_grad
    first_grad = first * (jnp.where(route > 0.5, 0.0, gate_grad) - scaled)
    second_grad = second * (jnp.where(route > 0.5, gate_grad, 0.0) - scaled)
    ffn = ffn_ref[...].astype(WIDE)
    router_grad = jnp.concatenate(
        [
            jnp.sum(ffn * first_grad, axis=0, keepdims=True),
            jnp.sum(ffn * second_grad, axis=0, keepdims=True),
        ],
        axis=0,
    )
    norm_grad = norm_ref[...] + first_grad * router[0:1] + second_grad * router[1:2]
    scale = rms_scale(hidden)
    gain_ffn_grad = jnp.sum(norm_grad * hidden * scale, axis=0, keepdims=True)
    bent = norm_grad * sum_ref[1:2, :]
    hidden_grad = (
        upstream
        + scale * bent
        - hidden * (scale * scale * scale) * jnp.mean(bent * hidden, axis=1, keepdims=True)
    )
    attn_grad = hidden_grad.astype(LOW)
    split(grads, 3 * pad, rows, pad, dot(context_ref[...], attn_grad, TN))
    context_grad = dot(attn_grad, joined(whole_ref, 3 * pad, rows, pad), NT).astype(LOW)

    row = lax.broadcasted_iota(jnp.int32, (length, length), 0)
    col = lax.broadcasted_iota(jnp.int32, (length, length), 1)
    mirror = jnp.where(row + col == length - 1, 1.0, 0.0).astype(LOW)
    blank = jnp.zeros((length, length), WIDE)
    parts = [[], [], []]
    diagonals = []
    for h in range(heads):
        at = slice(h * head_size, (h + 1) * head_size)
        grad = context_grad[:, at]
        probs = probs_ref[h]
        prob_grad = dot(grad, proj_ref[2, :, at], NT)
        summed = jnp.sum(probs * prob_grad, axis=1, keepdims=True)
        low = (probs * (prob_grad - summed)).astype(LOW)
        flipped = dot(low, mirror)
        skewed = pltpu.roll(
            jnp.concatenate([flipped, blank], axis=1), 0, 1, stride=1, stride_axis=0
        )
        diagonals.append(jnp.sum(skewed, axis=0, keepdims=True))
        parts[0].append(dot(low, proj_ref[1, :, at]) * 0.125)
        parts[1].append(dot(low, proj_ref[0, :, at], TN) * 0.125)
        parts[2].append(dot(probs.astype(LOW), grad, TN))
    diagonal = jnp.concatenate(diagonals, axis=0)
    spots = lax.broadcasted_iota(jnp.int32, (length, 2 * length), 0)
    onehot = jnp.where(turned_ref[...] == spots, 1.0, 0.0).astype(LOW)
    high = diagonal.astype(LOW)
    rest = (diagonal - high.astype(WIDE)).astype(LOW)
    table_grad = dot(high, onehot, NT) + dot(rest, onehot, NT)
    normed = normed_ref[...]
    normed_grad = jnp.zeros((length, width), WIDE)
    for k in range(3):
        projected = jnp.concatenate(parts[k], axis=1).astype(LOW)
        split(grads, k * pad, rows, pad, dot(normed, projected, TN))
        normed_grad = normed_grad + dot(projected, joined(whole_ref, k * pad, rows, pad), NT)
    inputs = tok_ref[...].astype(WIDE)
    scale = rms_scale(inputs)
    gain_attn_grad = jnp.sum(normed_grad * inputs * scale, axis=0, keepdims=True)
    small = jnp.concatenate(
        [
            gain_attn_grad,
            gain_ffn_grad,
            router_grad,
            jnp.concatenate(
                [table_grad, jnp.zeros((heads, width - length), WIDE)], axis=1
            ),
        ],
        axis=0,
    ).astype(LOW)
    for j in range(size):
        grads[j // 2, j % 2, 4 * pad : 4 * pad + SMALL, :] = small

    def swap(i, d, e):
        k = place.at(-d, -e)
        return remote(
            grads.at[k, 1 - core], got.at[k], p_send.at[i], p_recv.at[i], partner
        )

    order = place.pairs()
    order = [p for p in order if p[1] > 0] + [p for p in order[1:] if p[1] == 0] + [(0, 0)]
    for d, e in order:
        swap(place.step(d, e), d, e).start()
    bent = normed_grad * sum_ref[0:1, :]
    input_ref[...] = (
        hidden_grad
        + scale * bent
        - inputs * (scale * scale * scale) * jnp.mean(bent * inputs, axis=1, keepdims=True)
    )

    own.wait()
    for copy in moves:
        copy.wait_recv()
    turns = []
    for f in range(1, reps):
        turns.append(
            remote(
                strips.at[rep],
                strips.at[rep],
                t_send.at[f - 1],
                t_recv.at[f - 1],
                {"rep": lax.rem(rep + f, reps)},
            )
        )
        turns[-1].start()

    def y_copy(d, e):
        i = place.step(d, e)
        k = place.at(-d, -e)
        return remote(
            kept.at[k],
            y_buf.at[i],
            y_send.at[i],
            y_recv.at[i],
            place.device(place.at(0, -e)),
        )

    def z_copy(d):
        return remote(
            z_out.at[d - 1],
            z_in.at[d - 1],
            z_send.at[d - 1],
            z_recv.at[d - 1],
            place.device(place.at(-d, 0)),
        )

    for d, e in order:
        i = place.step(d, e)
        k = place.at(-d, -e)
        swap(i, d, e).wait_recv()

        def add(n, carry):
            at = pl.ds(pl.multiple_of(n * 16, 16), 16)
            value = grads[k, core, at].astype(WIDE) + got[k, at].astype(WIDE)
            if e == 0:
                for s in range(1, inner):
                    value = value + y_buf[place.step(d, s), at].astype(WIDE)
            if e > 0:
                kept[k, at] = value.astype(LOW)
            elif d > 0:
                z_out[d - 1, at] = value.astype(LOW)
            else:
                total[at] = value
            return carry

        if e == 0:
            for s in range(1, inner):
                y_copy(d, s).wait_recv()
        lax.fori_loop(0, depth // 16, add, 0, unroll=True)
        if e > 0:
            y_copy(d, e).start()
        elif d > 0:
            z_copy(d).start()
    for d in range(1, outer):
        z_copy(d).wait()

    def finish(n, carry):
        at = pl.ds(pl.multiple_of(n * 16, 16), 16)
        value = total[at]
        for d in range(1, outer):
            value = value + z_in[d - 1, at].astype(WIDE)
        rep_all[rep, at] = value.astype(LOW)
        return carry

    lax.fori_loop(0, depth // 16, finish, 0, unroll=True)
    swaps = []
    for f in range(1, reps):
        swaps.append(
            remote(
                rep_all.at[rep],
                rep_all.at[rep],
                r_send.at[f - 1],
                r_recv.at[f - 1],
                {"rep": lax.rem(rep + f, reps)},
            )
        )
        swaps[-1].start()
    for copy in turns:
        copy.wait()
    strip = g1_ref.shape[2] // 2
    for k in range(chips):
        value = strips[0, k].astype(WIDE)
        for r in range(1, reps):
            value = value + strips[r, k].astype(WIDE)
        for e in range(2):
            g1_out_ref[e, :, k * strip : (k + 1) * strip] = value[:, e * strip : (e + 1) * strip]
    for copy in swaps:
        copy.wait()
    value = rep_all[0].astype(WIDE)
    for r in range(1, reps):
        value = value + rep_all[r].astype(WIDE)
    mine_ref[...] = value
    for copy in moves:
        copy.wait_send()
    for d, e in order:
        swap(place.step(d, e), d, e).wait_send()
        if e > 0:
            y_copy(d, e).wait_send()


def back(size, reps, heads, rows, *operands):
    chips = size // 2
    outer = grid_of(size)[0]
    steps = max(outer - 1, 1)
    length, width = operands[0].shape
    strips = operands[-1]
    pad, cols = strips.shape[1:]
    depth = 4 * pad + SMALL
    block = (chips, depth, width)
    return pl.pallas_call(
        functools.partial(back_kernel, size, reps, heads, rows),
        out_shape=(
            jax.ShapeDtypeStruct((length, width), LOW),
            jax.ShapeDtypeStruct((length, width), WIDE),
            jax.ShapeDtypeStruct((depth, width), WIDE),
            jax.ShapeDtypeStruct((2, pad, chips * cols // 2), WIDE),
        ),
        in_specs=[VMEM] * len(operands),
        out_specs=[VMEM] * 4,
        scratch_shapes=[
            pltpu.VMEM((chips, 2, depth, width), LOW),
            pltpu.VMEM(block, LOW),
            pltpu.VMEM(block, LOW),
            pltpu.VMEM(block, LOW),
            pltpu.VMEM((steps, depth, width), LOW),
            pltpu.VMEM((steps, depth, width), LOW),
            pltpu.VMEM((depth, width), WIDE),
            pltpu.VMEM((reps, depth, width), LOW),
            pltpu.VMEM((reps, chips, pad, cols), LOW),
            DMA((chips,)),
            DMA((chips,)),
            DMA((max(reps - 1, 1),)),
            DMA((max(reps - 1, 1),)),
            DMA((chips,)),
            DMA((chips,)),
            DMA((chips,)),
            DMA((chips,)),
            DMA((steps,)),
            DMA((steps,)),
            DMA((max(reps - 1, 1),)),
            DMA((max(reps - 1, 1),)),
            DMA,
        ],
        compiler_params=pltpu.CompilerParams(
            collective_id=2, has_side_effects=True, vmem_limit_bytes=56 << 20
        ),
    )(*operands)


def shards(
    size,
    reps,
    tokens,
    cotangent,
    lengths,
    routes,
    bucket_ids,
    attn_in,
    attn_out,
    gains,
    router,
    rel_table,
    expert_in,
    expert_out,
):
    length, width = tokens.shape
    heads = rel_table.shape[1]
    table_rows = rel_table.shape[0]
    chips = size // 2
    rows = attn_out.shape[0]
    pad = rows + -rows % 16
    hidden_units = expert_in.shape[2]
    strip = hidden_units // chips
    half = expert_out.shape[1]
    me = lax.axis_index("shard")

    small = jnp.zeros((SMALL, width), LOW)
    small = lax.dynamic_update_slice(
        small, jnp.concatenate([gains, router.T], axis=0), (0, me * rows)
    )
    table_block = lax.dynamic_update_slice(
        jnp.zeros((heads, length), LOW), rel_table.T, (0, me * table_rows)
    )
    upper = small[:4]
    lower = jnp.concatenate(
        [
            table_block,
            jnp.broadcast_to(routes.reshape(1, length).astype(LOW), (heads, length)),
            jnp.zeros((heads, width - 2 * length), LOW),
        ],
        axis=1,
    )
    small = jnp.concatenate([upper, lower], axis=0)
    buckets = jnp.pad(bucket_ids, (0, 1), constant_values=-1).reshape(1, 2 * length)
    turned = jnp.pad(bucket_ids[::-1], (0, 1), constant_values=-1).reshape(1, 2 * length)
    strips = jnp.transpose(expert_in.reshape(2, rows, chips, strip), (2, 1, 0, 3))
    strips = strips.reshape(chips, rows, 2 * strip)
    strips = jnp.pad(strips, ((0, 0), (0, pad - rows), (0, 0)))
    whole, w1, w2, normed, projected, probs, context, hidden, ffn, totals, columns = front(
        size,
        tokens,
        attn_in,
        attn_out,
        small,
        strips,
        expert_out,
        buckets,
        lengths,
        heads,
    )
    w1 = w1[:, :, :rows].reshape(width, 2 * strip)
    w2 = w2.reshape(2 * strip, width)
    returned, norm_grad, strip_grad, expert_out_grad = expert(
        size, reps, rows, pad, ffn, cotangent, w1, w2, totals, columns
    )
    layer_out, input_grad, mine, expert_in_grad = back(
        size,
        reps,
        heads,
        rows,
        tokens,
        cotangent,
        hidden,
        ffn,
        normed,
        projected,
        probs,
        context,
        whole,
        totals,
        routes,
        turned,
        returned,
        norm_grad,
        strip_grad,
    )
    in_shard = mine[: 3 * pad].reshape(3, pad, width)[:, :rows]
    out_shard = mine[3 * pad : 3 * pad + rows]
    sums = mine[4 * pad :]
    picked = lax.dynamic_slice(sums, (0, me * rows), (4, rows))
    table_shard = lax.dynamic_slice(sums, (4, me * table_rows), (heads, table_rows)).T
    return (
        layer_out,
        input_grad,
        in_shard,
        out_shard,
        picked[:2],
        picked[2:].T,
        table_shard,
        expert_in_grad[:, :rows],
        expert_out_grad,
    )


def solution(mesh):
    placed = (
        P(("rep", "shard"), None),
        P(("rep", "shard"), None),
        P(("rep", "shard"), None),
        P(("rep", "shard"), None),
        P(),
        P(None, "shard", None),
        P("shard", None),
        P(None, "shard"),
        P("shard", None),
        P("shard", None),
        P(None, "shard", None),
        P(None, "shard", None),
    )
    return jax.shard_map(
        functools.partial(shards, mesh.shape["shard"], mesh.shape["rep"]),
        mesh=mesh,
        in_specs=placed,
        out_specs=(
            P(("rep", "shard"), None),
            P(("rep", "shard"), None),
            P(None, "shard", None),
            P("shard", None),
            P(None, "shard"),
            P("shard", None),
            P("shard", None),
            P(None, "shard", None),
            P(None, "shard", None),
        ),
        check_vma=False,
    )
```

```python
import functools

import jax
import jax.numpy as jnp
from jax import lax
from jax.experimental import pallas as pl
from jax.experimental.pallas import tpu as pltpu
from jax.sharding import PartitionSpec as P

EPSILON = 1e-06
SMALL = 16
LOW = jnp.bfloat16
WIDE = jnp.float32
NT = (((1,), (1,)), ((), ()))
TN = (((0,), (0,)), ((), ()))
MESH = pl.DeviceIdType.MESH
VMEM = pl.BlockSpec(memory_space=pltpu.VMEM)
SMEM = pl.BlockSpec(memory_space=pltpu.SMEM)
DMA = pltpu.SemaphoreType.DMA


def grid_of(size):
    chips = size // 2
    outer = 4 if chips % 4 == 0 else 1
    return outer, chips // outer


class Place:
    def __init__(self, size):
        self.size = size
        self.outer, self.inner = grid_of(size)
        self.chips = size // 2
        me = lax.axis_index("shard")
        self.core = lax.rem(me, 2)
        self.chip = lax.div(me, 2)
        self.z = lax.div(self.chip, self.inner)
        self.y = lax.rem(self.chip, self.inner)

    def at(self, dz, dy):
        far = lax.rem(self.z + dz + self.outer, self.outer)
        near = lax.rem(self.y + dy + self.inner, self.inner)
        return far * self.inner + near

    def device(self, chip):
        return {"shard": chip * 2 + self.core}

    def partner(self):
        return {"shard": self.chip * 2 + 1 - self.core}

    def pairs(self):
        return [(d, e) for d in range(self.outer) for e in range(self.inner)]

    def line(self, j):
        z, top = self.z, self.outer - 1
        short = jnp.minimum(z, top - z)
        t = lax.div(j + 1, 2)
        near = jnp.where(lax.rem(j, 2) == 1, z - t, z + t)
        far = jnp.where(z <= top - z, z + j - short, z - j + short)
        return jnp.where(j <= 2 * short, near, far)

    def source(self, far, e):
        return far * self.inner + lax.rem(self.y - e + self.inner, self.inner)

    def pair(self, i):
        q, r = lax.div(i + self.inner - 1, self.inner) - 1, lax.rem(i + self.inner - 1, self.inner)
        last = q == self.outer - 1
        e = jnp.where(last, r + 1, r)
        j = jnp.where(last, q, jnp.where(r == 0, q + 1, q))
        return jnp.where(i == 0, 0, j), jnp.where(i == 0, 0, e)

    def greet(self, chips, reps):
        barrier = pltpu.get_barrier_semaphore()
        count = 0

        def signal(target):
            pl.semaphore_signal(barrier, inc=1, device_id=target, device_id_type=MESH)

        for dz, dy in self.pairs()[1:]:
            if chips or dz == 0:
                signal(self.device(self.at(dz, dy)))
                count += 1
        signal(self.partner())
        count += 1
        if not chips:
            below = jnp.where(self.z > 0, 1, 0)
            above = jnp.where(self.z < self.outer - 1, 1, 0)

            @pl.when(self.z > 0)
            def _():
                signal(self.device(self.chip - self.inner))

            @pl.when(self.z < self.outer - 1)
            def _():
                signal(self.device(self.chip + self.inner))

            count = count + below + above
        for f in range(1, reps):
            signal({"rep": lax.rem(lax.axis_index("rep") + f, reps)})
            count += 1
        pl.semaphore_wait(barrier, count)


def remote(src, dst, send_sem, recv_sem, target):
    return pltpu.make_async_remote_copy(
        src_ref=src,
        dst_ref=dst,
        send_sem=send_sem,
        recv_sem=recv_sem,
        device_id=target,
        device_id_type=MESH,
    )


def dot(a, b, dims=None):
    if dims is None:
        return jnp.dot(a, b, preferred_element_type=WIDE)
    return lax.dot_general(a, b, dims, preferred_element_type=WIDE)


def joined(ref, first, rows, pad):
    chips, _, _, width = ref.shape
    if rows == pad:
        return ref[:, :, first : first + rows, :].reshape(chips * 2 * rows, width)
    parts = [ref[j // 2, j % 2, first : first + rows, :].astype(WIDE) for j in range(chips * 2)]
    return jnp.concatenate(parts, axis=0).astype(LOW)


def split(ref, first, rows, pad, values):
    chips, _, _, width = ref.shape
    if rows == pad:
        ref[:, :, first : first + rows, :] = values.reshape(chips, 2, rows, width).astype(LOW)
        return
    for j in range(chips * 2):
        ref[j // 2, j % 2, first : first + rows, :] = values[j * rows : (j + 1) * rows].astype(LOW)


def rms_scale(values):
    return lax.rsqrt(jnp.mean(values * values, axis=1, keepdims=True) + EPSILON)


def gate_of(logits, route):
    first, second = logits[:, 2:3], logits[:, 3:4]
    top = jnp.maximum(first, second)
    first, second = jnp.exp(first - top), jnp.exp(second - top)
    total = first + second
    first, second = first / total, second / total
    return first, second, jnp.where(route > 0.5, second, first)


class Gather:
    def __init__(self, place, own, slots, up_send, down_send, z_recv, y_send, y_recv):
        self.place, self.own, self.slots = place, own, slots
        self.up_send, self.down_send, self.z_recv = up_send, down_send, z_recv
        self.y_send, self.y_recv = y_send, y_recv

    @staticmethod
    def sems(size):
        outer, inner = grid_of(size)
        side = max(inner - 1, 1)
        return [DMA((outer,))] * 3 + [DMA((outer, side))] * 2

    def up(self, src, far):
        place = self.place
        slot = self.slots.at[place.source(far, 0)]
        target = place.device(place.chip + place.inner)
        return remote(src, slot, self.up_send.at[far], self.z_recv.at[far], target)

    def down(self, src, far):
        place = self.place
        slot = self.slots.at[place.source(far, 0)]
        target = place.device(place.chip - place.inner)
        return remote(src, slot, self.down_send.at[far], self.z_recv.at[far], target)

    def across(self, src, far, e):
        place = self.place
        slot = self.slots.at[place.source(far, 0)]
        target = place.device(place.at(0, e))
        return remote(
            src, slot, self.y_send.at[far, e - 1], self.y_recv.at[far, e - 1], target
        )

    def spread(self, src, far, own):
        place = self.place

        @pl.when(place.z < place.outer - 1 if own else jnp.logical_and(far < place.z, place.z < place.outer - 1))
        def _():
            self.up(src, far).start()

        @pl.when(place.z > 0 if own else jnp.logical_and(far > place.z, place.z > 0))
        def _():
            self.down(src, far).start()

        for e in range(1, place.inner):
            self.across(src, far, e).start()

    def start(self):
        self.spread(self.own, self.place.z, True)

    def arrive_z(self, j):
        far = self.place.line(j)
        source = self.place.source(far, 0)
        slot = self.slots.at[source]
        remote(
            self.own, slot, self.up_send.at[far], self.z_recv.at[far], self.place.partner()
        ).wait_recv()
        self.spread(slot, far, False)
        return source

    def arrive_y(self, j, e):
        far = self.place.line(j)
        source = self.place.source(far, e)
        remote(
            self.own,
            self.slots.at[source],
            self.y_send.at[far, e - 1],
            self.y_recv.at[far, e - 1],
            self.place.partner(),
        ).wait_recv()
        return source

    def arrive(self, j, e):
        @pl.when(jnp.logical_and(j > 0, e == 0))
        def _():
            self.arrive_z(j)

        @pl.when(e > 0)
        def _():
            self.arrive_y(j, e)

        return self.place.source(self.place.line(j), e)

    def finish(self):
        place = self.place

        def sent(far, carry):
            @pl.when(jnp.logical_and(far <= place.z, place.z < place.outer - 1))
            def _():
                self.up(self.own, far).wait_send()

            @pl.when(jnp.logical_and(far >= place.z, place.z > 0))
            def _():
                self.down(self.own, far).wait_send()

            for e in range(1, place.inner):
                self.across(self.own, far, e).wait_send()
            return carry

        lax.fori_loop(0, place.outer, sent, 0)


class Scatter:
    def __init__(self, place, part, y_buf, z_out, z_in, acc, y_send, y_recv, z_send, z_recv):
        self.place, self.part, self.acc = place, part, acc
        self.y_buf, self.z_out, self.z_in = y_buf, z_out, z_in
        self.y_send, self.y_recv, self.z_send, self.z_recv = y_send, y_recv, z_send, z_recv

    @staticmethod
    def buffers(size, block):
        outer, inner = grid_of(size)
        side = max(inner - 1, 1)
        return [
            pltpu.VMEM((outer, side) + block, LOW),
            pltpu.VMEM((outer,) + block, LOW),
            pltpu.VMEM((2, outer) + block, LOW),
            pltpu.VMEM(block, WIDE),
            DMA((outer, side)),
            DMA((outer, side)),
            DMA((outer,)),
            DMA((2, outer)),
        ]

    def across(self, far, e):
        place = self.place
        return remote(
            self.part.at[place.source(far, e)],
            self.y_buf.at[far, e - 1],
            self.y_send.at[far, e - 1],
            self.y_recv.at[far, e - 1],
            place.device(place.at(0, -e)),
        )

    def along(self, far, way):
        place = self.place
        target = place.chip + (place.inner if way == 0 else -place.inner)
        return remote(
            self.z_out.at[far],
            self.z_in.at[way, far],
            self.z_send.at[far],
            self.z_recv.at[way, far],
            place.device(target),
        )

    def collect(self, j, last, first_term, give):
        place, acc = self.place, self.acc
        far = place.line(j)
        count = acc.shape[0] // 16
        for e in range(1, place.inner):
            self.across(far, e).wait_recv()

        def rows(n):
            return pl.ds(pl.multiple_of(n * 16, 16), 16)

        def begin(n, carry):
            value = first_term(place.source(far, 0), rows(n))
            for e in range(1, place.inner):
                value = value + self.y_buf[far, e - 1, rows(n)].astype(WIDE)
            acc[rows(n)] = value
            return carry

        lax.fori_loop(0, count, begin, 0, unroll=True)
        for way in range(2):
            more = place.z > 0 if way == 0 else place.z < place.outer - 1
            if not last:
                more = jnp.logical_and(more, far > place.z if way == 0 else far < place.z)

            @pl.when(more)
            def _(way=way):
                self.along(far, way).wait_recv()

                def add(n, carry):
                    acc[rows(n)] += self.z_in[way, far, rows(n)].astype(WIDE)
                    return carry

                lax.fori_loop(0, count, add, 0, unroll=True)

        if last:
            give()
            return
        self.z_out[far] = acc[...].astype(LOW)

        @pl.when(far > place.z)
        def _():
            self.along(far, 0).start()

        @pl.when(far < place.z)
        def _():
            self.along(far, 1).start()

    def finish(self):
        place = self.place

        def sent(far, carry):
            for e in range(1, place.inner):
                self.across(far, e).wait_send()

            @pl.when(far != place.z)
            def _():
                self.along(far, 0).wait_send()

            return carry

        lax.fori_loop(0, place.outer, sent, 0)


def front_kernel(
    size,
    heads,
    tok_ref,
    in_ref,
    out_ref,
    small_ref,
    strip_ref,
    half_ref,
    bucket_ref,
    length_ref,
    whole_ref,
    w1_ref,
    w2_ref,
    normed_ref,
    proj_ref,
    probs_ref,
    context_ref,
    hidden_ref,
    ffn_ref,
    sum_ref,
    route_ref,
    g_up,
    g_down,
    g_z,
    g_send,
    g_recv,
    c_send,
    c_recv,
    s_send,
    s_recv,
    d_send,
    d_recv,
    h_send,
    h_recv,
    own_sem,
):
    place = Place(size)
    chips = place.chips
    core, chip = place.core, place.chip
    length, width = tok_ref.shape
    rows = out_ref.shape[0]
    pad = w1_ref.shape[2]
    head_size = width // heads
    mine = whole_ref.at[chip, core]
    for k in range(3):
        whole_ref[chip, core, k * pad : k * pad + rows, :] = in_ref[k]
    whole_ref[chip, core, 3 * pad : 3 * pad + rows, :] = out_ref[...]
    whole_ref[chip, core, 4 * pad : 4 * pad + SMALL, :] = small_ref[...]
    place.greet(True, 1)
    partner = place.partner()
    gather = Gather(place, mine, whole_ref.at[:, core], g_up, g_down, g_z, g_send, g_recv)
    gather.start()

    def dup(source):
        return remote(
            whole_ref.at[source, core],
            whole_ref.at[source, core],
            c_send.at[source],
            c_recv.at[source],
            partner,
        )

    dup(chip).start()
    local = [
        pltpu.make_async_copy(strip_ref.at[chip], w1_ref.at[chip, core], own_sem.at[0]),
        pltpu.make_async_copy(half_ref, w2_ref.at[:, core], own_sem.at[1]),
    ]
    for copy in local:
        copy.start()
    halves = remote(half_ref, w2_ref.at[:, core], h_send, h_recv, partner)
    halves.start()

    def arrive(i, carry):
        j, e = place.pair(i)
        dup(gather.arrive(j, e)).start()
        return carry

    late = chips - 2 * (place.inner - 1)
    lax.fori_loop(1, late, arrive, 0)
    strips = []
    for i, (d, e) in enumerate(place.pairs()):
        if i > 0:
            target = place.at(d, e)
            copy = remote(
                strip_ref.at[target],
                w1_ref.at[chip, core],
                s_send.at[i],
                s_recv.at[i],
                place.device(target),
            )
            copy.start()
            strips.append(copy)
    lax.fori_loop(late, chips, arrive, 0)

    def other(source, carry):
        remote(
            whole_ref.at[source, core],
            whole_ref.at[source, 1 - core],
            c_send.at[source],
            c_recv.at[source],
            partner,
        ).wait_recv()
        return carry

    lax.fori_loop(0, chips, other, 0)

    total = jnp.zeros((SMALL, width), WIDE)
    for j in range(size):
        total = total + whole_ref[j // 2, j % 2, 4 * pad : 4 * pad + SMALL, :].astype(WIDE)
    sum_ref[...] = total
    lines = [
        whole_ref[k, core, 4 * pad : 4 * pad + SMALL, length : 2 * length].astype(WIDE)[4:5]
        for k in range(chips)
    ]
    lines.append(jnp.zeros((length - chips, length), WIDE))
    route_ref[...] = jnp.transpose(jnp.concatenate(lines, axis=0))

    inputs = tok_ref[...].astype(WIDE)
    normed = (inputs * rms_scale(inputs) * total[0:1]).astype(LOW)
    normed_ref[...] = normed
    for k in range(3):
        proj_ref[k] = dot(normed, joined(whole_ref, k * pad, rows, pad)).astype(LOW)
    spots = lax.broadcasted_iota(jnp.int32, (length, 2 * length), 0)
    onehot = jnp.where(bucket_ref[...] == spots, 1.0, 0.0).astype(LOW)
    table = total[:, :length].astype(LOW)
    bias = dot(table, onehot)
    down = lax.broadcasted_iota(jnp.int32, (length, length), 0)
    across = lax.broadcasted_iota(jnp.int32, (length, length), 1)
    part_q = jnp.zeros((length, length), jnp.int32)
    part_k = jnp.zeros((length, length), jnp.int32)
    end = jnp.int32(0)
    for s in range(length_ref.shape[1]):
        end = end + length_ref[0, s]
        part_q = part_q + jnp.where(down >= end, 1, 0)
        part_k = part_k + jnp.where(across >= end, 1, 0)
    allowed = part_q == part_k
    parts = []
    for h in range(heads):
        at = slice(h * head_size, (h + 1) * head_size)
        raw = dot(proj_ref[0, :, at], proj_ref[1, :, at], NT)
        spread = jnp.broadcast_to(bias[4 + h : 5 + h, :], (length, 2 * length))
        skewed = pltpu.roll(spread, length + 1, 1, stride=1, stride_axis=0)
        scores = jnp.where(allowed, raw * 0.125 + skewed[:, :length], -1e30)
        expo = jnp.exp(scores - jnp.max(scores, axis=1, keepdims=True))
        probs = expo / jnp.sum(expo, axis=1, keepdims=True)
        probs_ref[h] = probs
        parts.append(dot(probs.astype(LOW), proj_ref[2, :, at]))
    context = jnp.concatenate(parts, axis=1).astype(LOW)
    context_ref[...] = context
    hidden = inputs + dot(context, joined(whole_ref, 3 * pad, rows, pad))
    hidden_ref[...] = hidden
    ffn_ref[...] = (hidden * rms_scale(hidden) * total[1:2]).astype(LOW)

    def moved(i):
        return place.at(-lax.div(i, place.inner), -lax.rem(i, place.inner))

    def pass_on(i, carry):
        block = w1_ref.at[moved(i), core]
        remote(block, block, s_send.at[i], s_recv.at[i], partner).wait_recv()
        remote(block, block, d_send.at[i], d_recv.at[i], partner).start()
        return carry

    local[0].wait()
    remote(w1_ref.at[chip, core], w1_ref.at[chip, core], d_send.at[0], d_recv.at[0], partner).start()
    lax.fori_loop(1, chips, pass_on, 0)

    def last(i, carry):
        source = moved(i)
        block = w1_ref.at[source, 1 - core]
        sent = w1_ref.at[source, core]
        remote(sent, block, d_send.at[i], d_recv.at[i], partner).wait()
        dup(source).wait_send()
        return carry

    lax.fori_loop(0, chips, last, 0)

    def sent(i, carry):
        remote(
            strip_ref.at[0], w1_ref.at[chip, core], s_send.at[i], s_recv.at[i], partner
        ).wait_send()
        return carry

    lax.fori_loop(1, chips, sent, 0)
    gather.finish()
    local[1].wait()
    halves.wait()


def front(size, tokens, attn_in, attn_out, small, strips, halves, buckets, lengths, heads):
    chips = size // 2
    length, width = tokens.shape
    rows = attn_out.shape[0]
    pad = strips.shape[1]
    cols = strips.shape[2]
    depth = 4 * pad + SMALL
    sems = [*Gather.sems(size), *[DMA((chips,))] * 6]
    return pl.pallas_call(
        functools.partial(front_kernel, size, heads),
        out_shape=(
            jax.ShapeDtypeStruct((chips, 2, depth, width), LOW),
            jax.ShapeDtypeStruct((chips, 2, pad, cols), LOW),
            jax.ShapeDtypeStruct((2, 2) + halves.shape[1:], LOW),
            jax.ShapeDtypeStruct((length, width), LOW),
            jax.ShapeDtypeStruct((3, length, width), LOW),
            jax.ShapeDtypeStruct((heads, length, length), WIDE),
            jax.ShapeDtypeStruct((length, width), LOW),
            jax.ShapeDtypeStruct((length, width), WIDE),
            jax.ShapeDtypeStruct((length, width), LOW),
            jax.ShapeDtypeStruct((SMALL, width), WIDE),
            jax.ShapeDtypeStruct((length, length), WIDE),
        ),
        in_specs=[VMEM] * 7 + [SMEM],
        out_specs=[VMEM] * 11,
        scratch_shapes=[*sems, DMA, DMA, DMA((2,))],
        compiler_params=pltpu.CompilerParams(
            collective_id=0, has_side_effects=True, vmem_limit_bytes=50 << 20
        ),
    )(tokens, attn_in, attn_out, small, strips, halves, buckets, lengths)


def expert_kernel(
    size,
    reps,
    rows,
    x_ref,
    u_ref,
    w1_ref,
    w2_ref,
    sum_ref,
    route_ref,
    ret_ref,
    back_ref,
    g1_ref,
    g2_ref,
    xs,
    us,
    act,
    slope,
    scaled,
    before_grad,
    ret_part,
    back_part,
    g1_own,
    g1_got,
    g2_own,
    g2_got,
    g2_all,
    p_send,
    p_recv,
    r_send,
    r_recv,
    own_sem,
    *rest,
):
    place = Place(size)
    chips, outer, inner = place.chips, place.outer, place.inner
    core, chip = place.core, place.chip
    rep = lax.axis_index("rep")
    length, width = x_ref.shape
    cols = w1_ref.shape[1]
    strip = cols // 2
    pad = g1_own.shape[2]
    place.greet(False, reps)
    partner = place.partner()
    x_gather = Gather(place, x_ref, xs, *rest[:5])
    u_gather = Gather(place, u_ref, us, *rest[5:10])
    ret_scatter = Scatter(place, ret_part, *rest[10:18])
    back_scatter = Scatter(place, back_part, *rest[18:26])
    x_gather.start()
    own = [
        pltpu.make_async_copy(x_ref, xs.at[chip], own_sem.at[0]),
        pltpu.make_async_copy(u_ref, us.at[chip], own_sem.at[1]),
    ]
    for copy in own:
        copy.start()
    for copy in own:
        copy.wait()
    lane = lax.broadcasted_iota(jnp.int32, (length, length), 1)
    side = lax.broadcasted_iota(jnp.int32, (length, cols), 1) >= strip
    router = sum_ref[...].astype(LOW)

    def route_of(k):
        return jnp.sum(jnp.where(lane == k, route_ref[...], 0.0), axis=1, keepdims=True)

    def forward(i, carry):
        j, e = place.pair(i)
        k = x_gather.arrive(j, e)
        before = dot(xs[k], w1_ref[...])
        keep = jnp.logical_xor(side, route_of(k) < 0.5)
        square = before * before
        bent = jnp.tanh(0.7978845608 * before * (1.0 + 0.044715 * square))
        half = 0.5 * (1.0 + bent)
        rise = half + 0.5 * before * (1.0 - bent * bent) * 0.7978845608 * (
            1.0 + 0.134145 * square
        )
        active = jnp.where(keep, before * half, 0.0).astype(LOW)
        act[k] = active
        slope[k] = jnp.where(keep, rise, 0.0)
        ret_part[k] = dot(active, w2_ref[...]).astype(LOW)
        return carry

    late = chips - 2 * (inner - 1)
    lax.fori_loop(0, late, forward, 0)
    u_gather.start()
    lax.fori_loop(late, chips, forward, 0)

    def ret_term(k, at):
        return ret_part[k, at].astype(WIDE)

    def back_term(k, at):
        return back_part[k, at].astype(WIDE)

    def ret_give():
        ret_ref[...] = ret_scatter.acc[...]

    def back_give():
        back_ref[...] = back_scatter.acc[...]

    for j in range(1, outer):
        u_gather.arrive_z(j)
        for e in range(1, inner):
            ret_scatter.across(place.line(outer - j), e).start()
    for e in range(1, inner):
        ret_scatter.across(place.line(0), e).start()

    def backward(j, e):
        k = place.source(place.line(j), e)
        gate = gate_of(dot(xs[k], router, NT), route_of(k))[2]
        low = (gate * us[k].astype(WIDE)).astype(LOW)
        scaled[k] = low
        grad = (dot(low, w2_ref[...], NT) * slope[k]).astype(LOW)
        before_grad[k] = grad
        back_part[k] = dot(grad, w1_ref[...], NT).astype(LOW)

    def back_step(n, carry):
        j = outer - 1 - n
        for e in range(1, inner):
            u_gather.arrive_y(j, e)
            backward(j, e)
            back_scatter.across(place.line(j), e).start()

        @pl.when(j > 0)
        def _():
            ret_scatter.collect(j, False, ret_term, None)

        backward(j, 0)
        return carry

    lax.fori_loop(0, outer, back_step, 0)

    def flat(ref):
        return ref[...].reshape(chips * length, ref.shape[2])

    g2 = dot(flat(act), flat(scaled), TN)
    g2_own[...] = g2.astype(LOW).reshape(g2_own.shape)
    g2_swap = remote(g2_own.at[:, 1 - core], g2_got, p_send.at[0], p_recv.at[0], partner)
    g2_swap.start()
    for j in range(outer - 1, 1, -1):
        back_scatter.collect(j, False, back_term, None)
    g2_swap.wait()
    g2_all[rep] = (g2_own[:, core].astype(WIDE) + g2_got[...].astype(WIDE)).astype(LOW)
    swaps = []
    for f in range(1, reps):
        swaps.append(
            remote(
                g2_all.at[rep],
                g2_all.at[rep],
                r_send.at[f - 1],
                r_recv.at[f - 1],
                {"rep": lax.rem(rep + f, reps)},
            )
        )
        swaps[-1].start()
    g1 = dot(flat(xs), flat(before_grad), TN)
    split(g1_own, 0, rows, pad, g1)
    g1_swap = remote(g1_own.at[:, 1 - core], g1_got, p_send.at[1], p_recv.at[1], partner)
    g1_swap.start()
    if outer > 1:
        back_scatter.collect(1, False, back_term, None)
    ret_scatter.collect(0, True, ret_term, ret_give)
    g1_swap.wait()
    g1_ref[...] = (g1_own[:, core].astype(WIDE) + g1_got[...].astype(WIDE)).astype(LOW)
    for copy in swaps:
        copy.wait()
    value = g2_all[0].astype(WIDE)
    for r in range(1, reps):
        value = value + g2_all[r].astype(WIDE)
    g2_ref[...] = value
    back_scatter.collect(0, True, back_term, back_give)
    x_gather.finish()
    u_gather.finish()
    ret_scatter.finish()
    back_scatter.finish()


def expert(size, reps, rows, pad, x, u, w1, w2, small, routes):
    chips = size // 2
    length, width = x.shape
    cols = w1.shape[1]
    half = cols // 4
    block = (chips, length, width)
    wide = (chips, length, cols)
    return pl.pallas_call(
        functools.partial(expert_kernel, size, reps, rows),
        out_shape=(
            jax.ShapeDtypeStruct((length, width), WIDE),
            jax.ShapeDtypeStruct((length, width), WIDE),
            jax.ShapeDtypeStruct((chips, pad, cols), LOW),
            jax.ShapeDtypeStruct((2, half, width), WIDE),
        ),
        in_specs=[VMEM] * 6,
        out_specs=[VMEM] * 4,
        scratch_shapes=[
            pltpu.VMEM(block, LOW),
            pltpu.VMEM(block, LOW),
            pltpu.VMEM(wide, LOW),
            pltpu.VMEM(wide, WIDE),
            pltpu.VMEM(block, LOW),
            pltpu.VMEM(wide, LOW),
            pltpu.VMEM(block, LOW),
            pltpu.VMEM(block, LOW),
            pltpu.VMEM((chips, 2, pad, cols), LOW),
            pltpu.VMEM((chips, pad, cols), LOW),
            pltpu.VMEM((2, 2, half, width), LOW),
            pltpu.VMEM((2, half, width), LOW),
            pltpu.VMEM((reps, 2, half, width), LOW),
            DMA((2,)),
            DMA((2,)),
            DMA((max(reps - 1, 1),)),
            DMA((max(reps - 1, 1),)),
            DMA((2,)),
            *Gather.sems(size),
            *Gather.sems(size),
            *Scatter.buffers(size, (length, width)),
            *Scatter.buffers(size, (length, width)),
        ],
        compiler_params=pltpu.CompilerParams(
            collective_id=1, has_side_effects=True, vmem_limit_bytes=56 << 20
        ),
    )(x, u, w1, w2, small, routes)


def back_kernel(
    size,
    reps,
    heads,
    rows,
    tok_ref,
    u_ref,
    hidden_ref,
    ffn_ref,
    normed_ref,
    proj_ref,
    probs_ref,
    context_ref,
    whole_ref,
    sum_ref,
    route_ref,
    turned_ref,
    ret_ref,
    norm_ref,
    g1_ref,
    layer_ref,
    input_ref,
    mine_ref,
    g1_out_ref,
    grads,
    got,
    kept,
    rep_all,
    strips,
    s_send,
    s_recv,
    t_send,
    t_recv,
    p_send,
    p_recv,
    r_send,
    r_recv,
    own_sem,
    *rest,
):
    place = Place(size)
    chips, outer, inner = place.chips, place.outer, place.inner
    core, chip = place.core, place.chip
    rep = lax.axis_index("rep")
    length, width = tok_ref.shape
    head_size = width // heads
    depth = mine_ref.shape[0]
    pad = (depth - SMALL) // 4
    place.greet(True, reps)
    partner = place.partner()
    moves = []
    own = pltpu.make_async_copy(g1_ref.at[chip], strips.at[rep, chip], own_sem)
    own.start()
    for i, (d, e) in enumerate(place.pairs()):
        if i > 0:
            target = place.at(d, e)
            moves.append(
                remote(
                    g1_ref.at[target],
                    strips.at[rep, chip],
                    s_send.at[i],
                    s_recv.at[i],
                    place.device(target),
                )
            )
            moves[-1].start()

    router = sum_ref[2:4, :]
    upstream = u_ref[...].astype(WIDE)
    hidden = hidden_ref[...]
    returned = ret_ref[...]
    route = route_ref[...].astype(WIDE)
    logits = dot(ffn_ref[...], sum_ref[...].astype(LOW), NT)
    first, second, gate = gate_of(logits, route)
    layer_ref[...] = (hidden + gate * returned).astype(LOW)
    gate_grad = jnp.sum(upstream * returned, axis=1, keepdims=True)
    scaled = gate * gate_grad
    first_grad = first * (jnp.where(route > 0.5, 0.0, gate_grad) - scaled)
    second_grad = second * (jnp.where(route > 0.5, gate_grad, 0.0) - scaled)
    ffn = ffn_ref[...].astype(WIDE)
    router_grad = jnp.concatenate(
        [
            jnp.sum(ffn * first_grad, axis=0, keepdims=True),
            jnp.sum(ffn * second_grad, axis=0, keepdims=True),
        ],
        axis=0,
    )
    norm_grad = norm_ref[...] + first_grad * router[0:1] + second_grad * router[1:2]
    scale = rms_scale(hidden)
    gain_ffn_grad = jnp.sum(norm_grad * hidden * scale, axis=0, keepdims=True)
    bent = norm_grad * sum_ref[1:2, :]
    hidden_grad = (
        upstream
        + scale * bent
        - hidden * (scale * scale * scale) * jnp.mean(bent * hidden, axis=1, keepdims=True)
    )
    attn_grad = hidden_grad.astype(LOW)
    split(grads, 3 * pad, rows, pad, dot(context_ref[...], attn_grad, TN))
    context_grad = dot(attn_grad, joined(whole_ref, 3 * pad, rows, pad), NT).astype(LOW)

    row = lax.broadcasted_iota(jnp.int32, (length, length), 0)
    col = lax.broadcasted_iota(jnp.int32, (length, length), 1)
    mirror = jnp.where(row + col == length - 1, 1.0, 0.0).astype(LOW)
    blank = jnp.zeros((length, length), WIDE)
    parts = [[], [], []]
    diagonals = []
    for h in range(heads):
        at = slice(h * head_size, (h + 1) * head_size)
        grad = context_grad[:, at]
        probs = probs_ref[h]
        prob_grad = dot(grad, proj_ref[2, :, at], NT)
        summed = jnp.sum(probs * prob_grad, axis=1, keepdims=True)
        low = (probs * (prob_grad - summed)).astype(LOW)
        flipped = dot(low, mirror)
        skewed = pltpu.roll(
            jnp.concatenate([flipped, blank], axis=1), 0, 1, stride=1, stride_axis=0
        )
        diagonals.append(jnp.sum(skewed, axis=0, keepdims=True))
        parts[0].append(dot(low, proj_ref[1, :, at]) * 0.125)
        parts[1].append(dot(low, proj_ref[0, :, at], TN) * 0.125)
        parts[2].append(dot(probs.astype(LOW), grad, TN))
    diagonal = jnp.concatenate(diagonals, axis=0)
    spots = lax.broadcasted_iota(jnp.int32, (length, 2 * length), 0)
    onehot = jnp.where(turned_ref[...] == spots, 1.0, 0.0).astype(LOW)
    high = diagonal.astype(LOW)
    below = (diagonal - high.astype(WIDE)).astype(LOW)
    table_grad = dot(high, onehot, NT) + dot(below, onehot, NT)
    normed = normed_ref[...]
    normed_grad = jnp.zeros((length, width), WIDE)
    for k in range(3):
        projected = jnp.concatenate(parts[k], axis=1).astype(LOW)
        split(grads, k * pad, rows, pad, dot(normed, projected, TN))
        normed_grad = normed_grad + dot(projected, joined(whole_ref, k * pad, rows, pad), NT)
    inputs = tok_ref[...].astype(WIDE)
    scale = rms_scale(inputs)
    gain_attn_grad = jnp.sum(normed_grad * inputs * scale, axis=0, keepdims=True)
    small = jnp.concatenate(
        [
            gain_attn_grad,
            gain_ffn_grad,
            router_grad,
            jnp.concatenate(
                [table_grad, jnp.zeros((heads, width - length), WIDE)], axis=1
            ),
        ],
        axis=0,
    ).astype(LOW)
    for j in range(size):
        grads[j // 2, j % 2, 4 * pad : 4 * pad + SMALL, :] = small

    scatter = Scatter(place, kept, *rest)

    def swap(k):
        return remote(
            grads.at[k, 1 - core], got.at[k], p_send.at[k], p_recv.at[k], partner
        )

    order = [(j, e) for j in range(outer - 1, -1, -1) for e in range(1, inner)]
    order += [(j, 0) for j in range(outer - 1, -1, -1)]
    for j, e in order:
        swap(place.source(place.line(j), e)).start()
    bent = normed_grad * sum_ref[0:1, :]
    input_ref[...] = (
        hidden_grad
        + scale * bent
        - inputs * (scale * scale * scale) * jnp.mean(bent * inputs, axis=1, keepdims=True)
    )

    own.wait()
    for copy in moves:
        copy.wait_recv()
    turns = []
    for f in range(1, reps):
        turns.append(
            remote(
                strips.at[rep],
                strips.at[rep],
                t_send.at[f - 1],
                t_recv.at[f - 1],
                {"rep": lax.rem(rep + f, reps)},
            )
        )
        turns[-1].start()

    def cross(n, carry):
        j = outer - 1 - n
        far = place.line(j)
        for e in range(1, inner):
            k = place.source(far, e)
            swap(k).wait_recv()
            kept[k] = (grads[k, core].astype(WIDE) + got[k].astype(WIDE)).astype(LOW)
            scatter.across(far, e).start()
        return carry

    lax.fori_loop(0, outer, cross, 0)

    def term(k, at):
        return grads[k, core, at].astype(WIDE) + got[k, at].astype(WIDE)

    def pass_on(n, carry):
        j = outer - 1 - n
        swap(place.source(place.line(j), 0)).wait_recv()
        scatter.collect(j, False, term, None)
        return carry

    lax.fori_loop(0, outer - 1, pass_on, 0)
    swap(chip).wait_recv()

    def give():
        rep_all[rep] = scatter.acc[...].astype(LOW)

    scatter.collect(0, True, term, give)
    swaps = []
    for f in range(1, reps):
        swaps.append(
            remote(
                rep_all.at[rep],
                rep_all.at[rep],
                r_send.at[f - 1],
                r_recv.at[f - 1],
                {"rep": lax.rem(rep + f, reps)},
            )
        )
        swaps[-1].start()
    for copy in turns:
        copy.wait()
    strip = g1_ref.shape[2] // 2
    for k in range(chips):
        value = strips[0, k].astype(WIDE)
        for r in range(1, reps):
            value = value + strips[r, k].astype(WIDE)
        for e in range(2):
            g1_out_ref[e, :, k * strip : (k + 1) * strip] = value[:, e * strip : (e + 1) * strip]
    for copy in swaps:
        copy.wait()
    value = rep_all[0].astype(WIDE)
    for r in range(1, reps):
        value = value + rep_all[r].astype(WIDE)
    mine_ref[...] = value
    for copy in moves:
        copy.wait_send()
    for k in range(chips):
        swap(k).wait_send()
    scatter.finish()


def back(size, reps, heads, rows, *operands):
    chips = size // 2
    length, width = operands[0].shape
    strips = operands[-1]
    pad, cols = strips.shape[1:]
    depth = 4 * pad + SMALL
    block = (chips, depth, width)
    return pl.pallas_call(
        functools.partial(back_kernel, size, reps, heads, rows),
        out_shape=(
            jax.ShapeDtypeStruct((length, width), LOW),
            jax.ShapeDtypeStruct((length, width), WIDE),
            jax.ShapeDtypeStruct((depth, width), WIDE),
            jax.ShapeDtypeStruct((2, pad, chips * cols // 2), WIDE),
        ),
        in_specs=[VMEM] * len(operands),
        out_specs=[VMEM] * 4,
        scratch_shapes=[
            pltpu.VMEM((chips, 2, depth, width), LOW),
            pltpu.VMEM(block, LOW),
            pltpu.VMEM(block, LOW),
            pltpu.VMEM((reps, depth, width), LOW),
            pltpu.VMEM((reps, chips, pad, cols), LOW),
            DMA((chips,)),
            DMA((chips,)),
            DMA((max(reps - 1, 1),)),
            DMA((max(reps - 1, 1),)),
            DMA((chips,)),
            DMA((chips,)),
            DMA((max(reps - 1, 1),)),
            DMA((max(reps - 1, 1),)),
            DMA,
            *Scatter.buffers(size, (depth, width)),
        ],
        compiler_params=pltpu.CompilerParams(
            collective_id=2, has_side_effects=True, vmem_limit_bytes=56 << 20
        ),
    )(*operands)


def shards(
    size,
    reps,
    tokens,
    cotangent,
    lengths,
    routes,
    bucket_ids,
    attn_in,
    attn_out,
    gains,
    router,
    rel_table,
    expert_in,
    expert_out,
):
    length, width = tokens.shape
    heads = rel_table.shape[1]
    table_rows = rel_table.shape[0]
    chips = size // 2
    rows = attn_out.shape[0]
    pad = rows + -rows % 16
    hidden_units = expert_in.shape[2]
    strip = hidden_units // chips
    half = expert_out.shape[1]
    me = lax.axis_index("shard")

    small = jnp.zeros((SMALL, width), LOW)
    small = lax.dynamic_update_slice(
        small, jnp.concatenate([gains, router.T], axis=0), (0, me * rows)
    )
    table_block = lax.dynamic_update_slice(
        jnp.zeros((heads, length), LOW), rel_table.T, (0, me * table_rows)
    )
    upper = small[:4]
    lower = jnp.concatenate(
        [
            table_block,
            jnp.broadcast_to(routes.reshape(1, length).astype(LOW), (heads, length)),
            jnp.zeros((heads, width - 2 * length), LOW),
        ],
        axis=1,
    )
    small = jnp.concatenate([upper, lower], axis=0)
    buckets = jnp.pad(bucket_ids, (0, 1), constant_values=-1).reshape(1, 2 * length)
    turned = jnp.pad(bucket_ids[::-1], (0, 1), constant_values=-1).reshape(1, 2 * length)
    strips = jnp.transpose(expert_in.reshape(2, rows, chips, strip), (2, 1, 0, 3))
    strips = strips.reshape(chips, rows, 2 * strip)
    strips = jnp.pad(strips, ((0, 0), (0, pad - rows), (0, 0)))
    whole, w1, w2, normed, projected, probs, context, hidden, ffn, totals, columns = front(
        size,
        tokens,
        attn_in,
        attn_out,
        small,
        strips,
        expert_out,
        buckets,
        lengths,
        heads,
    )
    w1 = w1[:, :, :rows].reshape(width, 2 * strip)
    w2 = w2.reshape(2 * strip, width)
    returned, norm_grad, strip_grad, expert_out_grad = expert(
        size, reps, rows, pad, ffn, cotangent, w1, w2, totals, columns
    )
    layer_out, input_grad, mine, expert_in_grad = back(
        size,
        reps,
        heads,
        rows,
        tokens,
        cotangent,
        hidden,
        ffn,
        normed,
        projected,
        probs,
        context,
        whole,
        totals,
        routes,
        turned,
        returned,
        norm_grad,
        strip_grad,
    )
    in_shard = mine[: 3 * pad].reshape(3, pad, width)[:, :rows]
    out_shard = mine[3 * pad : 3 * pad + rows]
    sums = mine[4 * pad :]
    picked = lax.dynamic_slice(sums, (0, me * rows), (4, rows))
    table_shard = lax.dynamic_slice(sums, (4, me * table_rows), (heads, table_rows)).T
    return (
        layer_out,
        input_grad,
        in_shard,
        out_shard,
        picked[:2],
        picked[2:].T,
        table_shard,
        expert_in_grad[:, :rows],
        expert_out_grad,
    )


def solution(mesh):
    placed = (
        P(("rep", "shard"), None),
        P(("rep", "shard"), None),
        P(("rep", "shard"), None),
        P(("rep", "shard"), None),
        P(),
        P(None, "shard", None),
        P("shard", None),
        P(None, "shard"),
        P("shard", None),
        P("shard", None),
        P(None, "shard", None),
        P(None, "shard", None),
    )
    return jax.shard_map(
        functools.partial(shards, mesh.shape["shard"], mesh.shape["rep"]),
        mesh=mesh,
        in_specs=placed,
        out_specs=(
            P(("rep", "shard"), None),
            P(("rep", "shard"), None),
            P(None, "shard", None),
            P("shard", None),
            P(None, "shard"),
            P("shard", None),
            P("shard", None),
            P(None, "shard", None),
            P(None, "shard", None),
        ),
        check_vma=False,
    )
```

```python
import functools

import jax
import jax.numpy as jnp
from jax import lax
from jax.experimental import pallas as pl
from jax.experimental.pallas import tpu as pltpu
from jax.sharding import PartitionSpec as P

EPSILON = 1e-06
SMALL = 16
LOW = jnp.bfloat16
WIDE = jnp.float32
NT = (((1,), (1,)), ((), ()))
TN = (((0,), (0,)), ((), ()))
MESH = pl.DeviceIdType.MESH
VMEM = pl.BlockSpec(memory_space=pltpu.VMEM)
SMEM = pl.BlockSpec(memory_space=pltpu.SMEM)
DMA = pltpu.SemaphoreType.DMA


def grid_of(size):
    chips = size // 2
    outer = 4 if chips % 4 == 0 else 1
    return outer, chips // outer


class Place:
    def __init__(self, size):
        self.size = size
        self.outer, self.inner = grid_of(size)
        self.chips = size // 2
        me = lax.axis_index("shard")
        self.index = me
        self.core = lax.rem(me, 2)
        self.chip = lax.div(me, 2)
        self.z = lax.div(self.chip, self.inner)
        self.y = lax.rem(self.chip, self.inner)

    def at(self, dz, dy):
        far = lax.rem(self.z + dz + self.outer, self.outer)
        near = lax.rem(self.y + dy + self.inner, self.inner)
        return far * self.inner + near

    def device(self, chip):
        return {"shard": chip * 2 + self.core}

    def partner(self):
        return {"shard": self.chip * 2 + 1 - self.core}

    def pairs(self):
        return [(d, e) for d in range(self.outer) for e in range(self.inner)]

    def line(self, j):
        z, top = self.z, self.outer - 1
        short = jnp.minimum(z, top - z)
        t = lax.div(j + 1, 2)
        near = jnp.where(lax.rem(j, 2) == 1, z - t, z + t)
        far = jnp.where(z <= top - z, z + j - short, z - j + short)
        return jnp.where(j <= 2 * short, near, far)

    def source(self, far, e):
        return far * self.inner + lax.rem(self.y - e + self.inner, self.inner)

    def pair(self, i):
        q, r = lax.div(i + self.inner - 1, self.inner) - 1, lax.rem(i + self.inner - 1, self.inner)
        last = q == self.outer - 1
        e = jnp.where(last, r + 1, r)
        j = jnp.where(last, q, jnp.where(r == 0, q + 1, q))
        return jnp.where(i == 0, 0, j), jnp.where(i == 0, 0, e)

    def greet(self, chips, reps):
        barrier = pltpu.get_barrier_semaphore()
        count = 0

        def signal(target):
            pl.semaphore_signal(barrier, inc=1, device_id=target, device_id_type=MESH)

        for dz, dy in self.pairs()[1:]:
            if chips or dz == 0:
                signal(self.device(self.at(dz, dy)))
                count += 1
        signal(self.partner())
        count += 1
        if not chips:
            below = jnp.where(self.z > 0, 1, 0)
            above = jnp.where(self.z < self.outer - 1, 1, 0)

            @pl.when(self.z > 0)
            def _():
                signal(self.device(self.chip - self.inner))

            @pl.when(self.z < self.outer - 1)
            def _():
                signal(self.device(self.chip + self.inner))

            count = count + below + above
        for f in range(1, reps):
            signal({"rep": lax.rem(lax.axis_index("rep") + f, reps)})
            count += 1
        pl.semaphore_wait(barrier, count)


def remote(src, dst, send_sem, recv_sem, target):
    return pltpu.make_async_remote_copy(
        src_ref=src,
        dst_ref=dst,
        send_sem=send_sem,
        recv_sem=recv_sem,
        device_id=target,
        device_id_type=MESH,
    )


def dot(a, b, dims=None):
    if dims is None:
        return jnp.dot(a, b, preferred_element_type=WIDE)
    return lax.dot_general(a, b, dims, preferred_element_type=WIDE)


def joined(ref, first, rows, pad):
    chips, _, _, width = ref.shape
    if rows == pad:
        return ref[:, :, first : first + rows, :].reshape(chips * 2 * rows, width)
    parts = [ref[j // 2, j % 2, first : first + rows, :].astype(WIDE) for j in range(chips * 2)]
    return jnp.concatenate(parts, axis=0).astype(LOW)


def split(ref, first, rows, pad, values):
    chips, _, _, width = ref.shape
    if rows == pad:
        ref[:, :, first : first + rows, :] = values.reshape(chips, 2, rows, width).astype(LOW)
        return
    for j in range(chips * 2):
        ref[j // 2, j % 2, first : first + rows, :] = values[j * rows : (j + 1) * rows].astype(LOW)


def rms_scale(values):
    return lax.rsqrt(jnp.mean(values * values, axis=1, keepdims=True) + EPSILON)


def gate_of(logits, route):
    first, second = logits[:, 2:3], logits[:, 3:4]
    top = jnp.maximum(first, second)
    first, second = jnp.exp(first - top), jnp.exp(second - top)
    total = first + second
    first, second = first / total, second / total
    return first, second, jnp.where(route > 0.5, second, first)


class Gather:
    def __init__(self, place, own, slots, up_send, down_send, z_recv, y_send, y_recv):
        self.place, self.own, self.slots = place, own, slots
        self.up_send, self.down_send, self.z_recv = up_send, down_send, z_recv
        self.y_send, self.y_recv = y_send, y_recv

    @staticmethod
    def sems(size):
        outer, inner = grid_of(size)
        side = max(inner - 1, 1)
        return [DMA((outer,))] * 3 + [DMA((outer, side))] * 2

    def up(self, src, far):
        place = self.place
        slot = self.slots.at[place.source(far, 0)]
        target = place.device(place.chip + place.inner)
        return remote(src, slot, self.up_send.at[far], self.z_recv.at[far], target)

    def down(self, src, far):
        place = self.place
        slot = self.slots.at[place.source(far, 0)]
        target = place.device(place.chip - place.inner)
        return remote(src, slot, self.down_send.at[far], self.z_recv.at[far], target)

    def across(self, src, far, e):
        place = self.place
        slot = self.slots.at[place.source(far, 0)]
        target = place.device(place.at(0, e))
        return remote(
            src, slot, self.y_send.at[far, e - 1], self.y_recv.at[far, e - 1], target
        )

    def spread(self, src, far, own):
        place = self.place

        @pl.when(place.z < place.outer - 1 if own else jnp.logical_and(far < place.z, place.z < place.outer - 1))
        def _():
            self.up(src, far).start()

        @pl.when(place.z > 0 if own else jnp.logical_and(far > place.z, place.z > 0))
        def _():
            self.down(src, far).start()

        for e in range(1, place.inner):
            self.across(src, far, e).start()

    def start(self):
        self.spread(self.own, self.place.z, True)

    def arrive_z(self, j):
        far = self.place.line(j)
        source = self.place.source(far, 0)
        slot = self.slots.at[source]
        remote(
            self.own, slot, self.up_send.at[far], self.z_recv.at[far], self.place.partner()
        ).wait_recv()
        self.spread(slot, far, False)
        return source

    def arrive_y(self, j, e):
        far = self.place.line(j)
        source = self.place.source(far, e)
        remote(
            self.own,
            self.slots.at[source],
            self.y_send.at[far, e - 1],
            self.y_recv.at[far, e - 1],
            self.place.partner(),
        ).wait_recv()
        return source

    def arrive(self, j, e):
        @pl.when(jnp.logical_and(j > 0, e == 0))
        def _():
            self.arrive_z(j)

        @pl.when(e > 0)
        def _():
            self.arrive_y(j, e)

        return self.place.source(self.place.line(j), e)

    def finish(self):
        place = self.place

        def sent(far, carry):
            @pl.when(jnp.logical_and(far <= place.z, place.z < place.outer - 1))
            def _():
                self.up(self.own, far).wait_send()

            @pl.when(jnp.logical_and(far >= place.z, place.z > 0))
            def _():
                self.down(self.own, far).wait_send()

            for e in range(1, place.inner):
                self.across(self.own, far, e).wait_send()
            return carry

        lax.fori_loop(0, place.outer, sent, 0)


class Scatter:
    def __init__(self, place, part, y_buf, z_out, z_in, acc, y_send, y_recv, z_send, z_recv):
        self.place, self.part, self.acc = place, part, acc
        self.y_buf, self.z_out, self.z_in = y_buf, z_out, z_in
        self.y_send, self.y_recv, self.z_send, self.z_recv = y_send, y_recv, z_send, z_recv

    @staticmethod
    def buffers(size, block):
        outer, inner = grid_of(size)
        side = max(inner - 1, 1)
        return [
            pltpu.VMEM((outer, side) + block, LOW),
            pltpu.VMEM((max(outer - 1, 1),) + block, LOW),
            pltpu.VMEM((outer + 1,) + block, LOW),
            pltpu.VMEM(block, WIDE),
            DMA((outer, side)),
            DMA((outer, side)),
            DMA((outer,)),
            DMA((2, outer)),
        ]

    def across(self, far, e):
        place = self.place
        return remote(
            self.part.at[place.source(far, e)],
            self.y_buf.at[far, e - 1],
            self.y_send.at[far, e - 1],
            self.y_recv.at[far, e - 1],
            place.device(place.at(0, -e)),
        )

    def slot(self, far, way, z):
        return far if way == 0 else jnp.where(far == z, self.place.outer, far)

    def leave(self, far):
        return jnp.where(far < self.place.z, far, jnp.maximum(far - 1, 0))

    def along(self, far, way, z=None):
        place = self.place
        target = place.chip + (place.inner if way == 0 else -place.inner)
        if z is None:
            z = place.z + (1 if way == 0 else -1)
        return remote(
            self.z_out.at[self.leave(far)],
            self.z_in.at[self.slot(far, way, z)],
            self.z_send.at[far],
            self.z_recv.at[way, far],
            place.device(target),
        )

    def collect(self, j, last, first_term, give):
        place, acc = self.place, self.acc
        far = place.line(j)
        count = acc.shape[0] // 16
        for e in range(1, place.inner):
            self.across(far, e).wait_recv()

        def rows(n):
            return pl.ds(pl.multiple_of(n * 16, 16), 16)

        def begin(n, carry):
            value = first_term(place.source(far, 0), rows(n))
            for e in range(1, place.inner):
                value = value + self.y_buf[far, e - 1, rows(n)].astype(WIDE)
            acc[rows(n)] = value
            return carry

        lax.fori_loop(0, count, begin, 0, unroll=True)
        for way in range(2):
            more = place.z > 0 if way == 0 else place.z < place.outer - 1
            if not last:
                more = jnp.logical_and(more, far > place.z if way == 0 else far < place.z)

            @pl.when(more)
            def _(way=way):
                self.along(far, way, place.z).wait_recv()

                def add(n, carry):
                    acc[rows(n)] += self.z_in[self.slot(far, way, place.z), rows(n)].astype(WIDE)
                    return carry

                lax.fori_loop(0, count, add, 0, unroll=True)

        if last:
            give()
            return
        self.z_out[self.leave(far)] = acc[...].astype(LOW)

        @pl.when(far > place.z)
        def _():
            self.along(far, 0).start()

        @pl.when(far < place.z)
        def _():
            self.along(far, 1).start()

    def finish(self):
        place = self.place

        def sent(far, carry):
            for e in range(1, place.inner):
                self.across(far, e).wait_send()

            @pl.when(far != place.z)
            def _():
                self.along(far, 0).wait_send()

            return carry

        lax.fori_loop(0, place.outer, sent, 0)


def shared_rows(depth, reps):
    return depth * 5 // 256 * 16 if reps == 2 else 0


def spot_of(section, pad):
    return section * pad + (SMALL if section > 1 else 0)


def placing(count, width, first):
    row = lax.broadcasted_iota(jnp.int32, (count, width), 0)
    col = lax.broadcasted_iota(jnp.int32, (count, width), 1)
    return jnp.where(col == row + first, 1.0, 0.0).astype(LOW)


def front_part(
    place,
    reps,
    heads,
    more,
    tok_ref,
    in_ref,
    out_ref,
    gain_ref,
    router_ref,
    table_ref,
    here_ref,
    strip_ref,
    half_ref,
    bucket_ref,
    length_ref,
    whole_ref,
    w1_ref,
    w2_ref,
    normed_ref,
    proj_ref,
    probs_ref,
    context_ref,
    hidden_ref,
    ffn_ref,
    sum_ref,
    route_ref,
    g_up,
    g_down,
    g_z,
    g_send,
    g_recv,
    c_send,
    c_recv,
    e_send,
    e_recv,
    x_send,
    x_recv,
    s_send,
    s_recv,
    d_send,
    d_recv,
    h_send,
    h_recv,
    own_sem,
):
    size, chips = place.size, place.chips
    core, chip = place.core, place.chip
    length, width = tok_ref.shape
    rows = out_ref.shape[0]
    pad = w1_ref.shape[3]
    strip = w1_ref.shape[4]
    head_size = width // heads
    depth = whole_ref.shape[2]
    shared = shared_rows(depth, reps)
    rep = lax.axis_index("rep") if shared else 0
    window = pl.ds(pl.multiple_of(shared * rep, 16), depth - shared)
    for k in range(3):
        whole_ref[chip, core, spot_of(k, pad) : spot_of(k, pad) + rows, :] = in_ref[k]
    whole_ref[chip, core, spot_of(3, pad) : spot_of(3, pad) + rows, :] = out_ref[...]
    spot = placing(rows, width, place.index * rows)
    table_rows = table_ref.shape[0]
    here = jnp.broadcast_to(here_ref[...].astype(WIDE), (length, length))
    lower = jnp.concatenate(
        [
            dot(table_ref[...], placing(table_rows, length, place.index * table_rows), TN),
            jnp.transpose(here)[:heads],
            jnp.zeros((heads, width - 2 * length), WIDE),
        ],
        axis=1,
    )
    small = jnp.concatenate(
        [dot(gain_ref[...], spot), dot(router_ref[...], spot, TN), lower], axis=0
    )
    whole_ref[chip, core, 2 * pad : 2 * pad + SMALL, :] = small.astype(LOW)
    place.greet(True, reps)
    partner = place.partner()
    slots = whole_ref.at[:, core, window]
    gather = Gather(place, slots.at[chip], slots, g_up, g_down, g_z, g_send, g_recv)
    gather.start()

    def dup(source):
        block = whole_ref.at[source, core, window]
        return remote(block, block, c_send.at[source], c_recv.at[source], partner)

    def end(who):
        return pl.ds(pl.multiple_of((depth - shared) * who, 16), shared)

    def dup_end(source):
        block = whole_ref.at[source, core, end(1 - rep)]
        return remote(block, block, e_send.at[source], e_recv.at[source], partner)

    def give(source, who):
        block = whole_ref.at[source, core, end(who)]
        target = {"rep": 1 - rep}
        return remote(block, block, x_send.at[source], x_recv.at[source], target)

    def strip_of(k):
        if strip % 128 == 0 and rows == pad:
            return strip_ref.at[:, :, pl.ds(pl.multiple_of(k * strip, 128), strip)]
        return strip_ref.at[k]

    dup(chip).start()
    if shared:
        dup_end(chip).start()
    local = [
        pltpu.make_async_copy(strip_of(chip), w1_ref.at[:, chip, core], own_sem.at[0]),
        pltpu.make_async_copy(half_ref, w2_ref.at[:, core], own_sem.at[1]),
    ]
    for copy in local:
        copy.start()
    halves = remote(half_ref, w2_ref.at[:, core], h_send, h_recv, partner)
    halves.start()

    def arrive(i, carry):
        j, e = place.pair(i)
        source = gather.arrive(j, e)
        if shared:
            give(source, rep).start()
        dup(source).start()
        if shared:

            @pl.when(i > 2)
            def _():
                take(i - 2)

        return carry

    def take(i):
        j, e = place.pair(i)
        source = place.source(place.line(j), e)
        give(source, 1 - rep).wait_recv()
        dup_end(source).start()

    late = chips - 2 * (place.inner - 1)
    lax.fori_loop(1, late, arrive, 0)
    strips = []
    for i, (d, e) in enumerate(place.pairs()):
        if i > 0:
            target = place.at(d, e)
            copy = remote(
                strip_of(target),
                w1_ref.at[:, chip, core],
                s_send.at[i],
                s_recv.at[i],
                place.device(target),
            )
            copy.start()
            strips.append(copy)
    lax.fori_loop(late, chips, arrive, 0)
    if shared:
        for i in range(chips - 2, chips):
            take(i)

    def other(source, carry):
        block = whole_ref.at[source, 1 - core, window]
        remote(block, block, c_send.at[source], c_recv.at[source], partner).wait_recv()
        if shared:
            block = whole_ref.at[source, 1 - core, end(1 - rep)]
            remote(block, block, e_send.at[source], e_recv.at[source], partner).wait_recv()
        return carry

    more(0)
    lax.fori_loop(0, chips, other, 0)

    total = jnp.zeros((SMALL, width), WIDE)
    for j in range(size):
        total = total + whole_ref[j // 2, j % 2, 2 * pad : 2 * pad + SMALL, :].astype(WIDE)
    sum_ref[...] = total
    lines = [
        whole_ref[k, core, 2 * pad : 2 * pad + SMALL, length : 2 * length].astype(WIDE)[4:5]
        for k in range(chips)
    ]
    lines.append(jnp.zeros((length - chips, length), WIDE))
    route_ref[...] = jnp.transpose(jnp.concatenate(lines, axis=0))

    inputs = tok_ref[...].astype(WIDE)
    normed = (inputs * rms_scale(inputs) * total[0:1]).astype(LOW)
    normed_ref[...] = normed
    for k in range(3):
        proj_ref[k] = dot(normed, joined(whole_ref, spot_of(k, pad), rows, pad)).astype(LOW)
    spots = lax.broadcasted_iota(jnp.int32, (length, 2 * length), 0)
    onehot = jnp.where(bucket_ref[...] == spots, 1.0, 0.0).astype(LOW)
    table = total[:, :length].astype(LOW)
    bias = dot(table, onehot)
    down = lax.broadcasted_iota(jnp.int32, (length, length), 0)
    across = lax.broadcasted_iota(jnp.int32, (length, length), 1)
    part_q = jnp.zeros((length, length), jnp.int32)
    part_k = jnp.zeros((length, length), jnp.int32)
    bound = jnp.int32(0)
    for s in range(length_ref.shape[1]):
        bound = bound + length_ref[0, s]
        part_q = part_q + jnp.where(down >= bound, 1, 0)
        part_k = part_k + jnp.where(across >= bound, 1, 0)
    allowed = part_q == part_k
    parts = []
    for h in range(heads):
        at = slice(h * head_size, (h + 1) * head_size)
        raw = dot(proj_ref[0, :, at], proj_ref[1, :, at], NT)
        spread = jnp.broadcast_to(bias[4 + h : 5 + h, :], (length, 2 * length))
        skewed = pltpu.roll(spread, length + 1, 1, stride=1, stride_axis=0)
        scores = jnp.where(allowed, raw * 0.125 + skewed[:, :length], -1e30)
        expo = jnp.exp(scores - jnp.max(scores, axis=1, keepdims=True))
        probs = expo / jnp.sum(expo, axis=1, keepdims=True)
        probs_ref[h] = probs
        parts.append(dot(probs.astype(LOW), proj_ref[2, :, at]))
    context = jnp.concatenate(parts, axis=1).astype(LOW)
    context_ref[...] = context
    more(1)
    hidden = inputs + dot(context, joined(whole_ref, spot_of(3, pad), rows, pad))
    hidden_ref[...] = hidden
    ffn_ref[...] = (hidden * rms_scale(hidden) * total[1:2]).astype(LOW)

    def moved(i):
        return place.at(-lax.div(i, place.inner), -lax.rem(i, place.inner))

    def pass_on(i, carry):
        block = w1_ref.at[:, moved(i), core]
        remote(block, block, s_send.at[i], s_recv.at[i], partner).wait_recv()
        remote(block, block, d_send.at[i], d_recv.at[i], partner).start()
        return carry

    def strips_on():
        local[0].wait()
        block = w1_ref.at[:, chip, core]
        remote(block, block, d_send.at[0], d_recv.at[0], partner).start()
        lax.fori_loop(1, chips, pass_on, 0)

    def last(i, carry):
        source = moved(i)
        block = w1_ref.at[:, source, 1 - core]
        sent = w1_ref.at[:, source, core]
        remote(sent, block, d_send.at[i], d_recv.at[i], partner).wait()
        dup(source).wait_send()
        if shared:
            dup_end(source).wait_send()
        return carry

    def strips_here():
        lax.fori_loop(0, chips, last, 0)
        local[1].wait()
        halves.wait()

    def sent(i, carry):
        block = w1_ref.at[:, chip, core]
        remote(block, block, s_send.at[i], s_recv.at[i], partner).wait_send()
        if shared:
            give(moved(i), rep).wait_send()
        return carry

    def finish():
        lax.fori_loop(1, chips, sent, 0)
        gather.finish()

    return strips_on, strips_here, finish


def expert_part(
    place,
    reps,
    rows,
    strips_on,
    strips_here,
    u_gather,
    x_ref,
    u_ref,
    w1_ref,
    w2_ref,
    sum_ref,
    route_ref,
    ret_ref,
    back_ref,
    g1_ref,
    g2_ref,
    xs,
    us,
    act,
    slope,
    before_grad,
    ret_part,
    back_part,
    g1_own,
    g2_own,
    g2_all,
    p_send,
    p_recv,
    r_send,
    r_recv,
    own_sem,
    *rest,
):
    chips, outer, inner = place.chips, place.outer, place.inner
    core, chip = place.core, place.chip
    rep = lax.axis_index("rep")
    length, width = x_ref.shape
    strip = w1_ref.shape[4]
    cols = 2 * strip
    pad = g1_own.shape[2]
    partner = place.partner()
    x_gather = Gather(place, x_ref, xs, *rest[:5])
    ret_scatter = Scatter(place, ret_part, *rest[5:13])
    back_scatter = Scatter(place, back_part, *rest[13:16], rest[8], *rest[16:20])
    x_gather.start()
    strips_on()
    own = [
        pltpu.make_async_copy(x_ref, xs.at[chip], own_sem.at[0]),
        pltpu.make_async_copy(u_ref, us.at[chip], own_sem.at[1]),
    ]
    for copy in own:
        copy.start()
    for copy in own:
        copy.wait()
    strips_here()

    def w1_of(e):
        if rows == pad:
            return w1_ref[e].reshape(width, strip)
        parts = [w1_ref[e, j // 2, j % 2, :rows].astype(WIDE) for j in range(chips * 2)]
        return jnp.concatenate(parts, axis=0).astype(LOW)

    def w2_of():
        return w2_ref[...].reshape(cols, width)

    lane = lax.broadcasted_iota(jnp.int32, (length, length), 1)
    side = lax.broadcasted_iota(jnp.int32, (length, cols), 1) >= strip
    router = sum_ref[...].astype(LOW)

    def route_of(k):
        return jnp.sum(jnp.where(lane == k, route_ref[...], 0.0), axis=1, keepdims=True)

    def forward(i, carry):
        j, e = place.pair(i)
        k = x_gather.arrive(j, e)
        before = jnp.concatenate([dot(xs[k], w1_of(0)), dot(xs[k], w1_of(1))], axis=1)
        keep = jnp.logical_xor(side, route_of(k) < 0.5)
        square = before * before
        bent = jnp.tanh(0.7978845608 * before * (1.0 + 0.044715 * square))
        half = 0.5 * (1.0 + bent)
        rise = half + 0.5 * before * (1.0 - bent * bent) * 0.7978845608 * (
            1.0 + 0.134145 * square
        )
        active = jnp.where(keep, before * half, 0.0).astype(LOW)
        act[k] = active
        slope[k] = jnp.where(keep, rise, 0.0)
        ret_part[k] = dot(active, w2_of()).astype(LOW)
        return carry

    late = chips - 2 * (inner - 1)
    lax.fori_loop(0, late // 2, forward, 0)
    for j in range(2, outer - 1):
        u_gather.arrive_z(j)
    lax.fori_loop(late // 2, late, forward, 0)
    if outer > 2:
        u_gather.arrive_z(outer - 1)
    lax.fori_loop(late, chips, forward, 0)

    def ret_term(k, at):
        return ret_part[k, at].astype(WIDE)

    def back_term(k, at):
        return back_part[k, at].astype(WIDE)

    def ret_give():
        ret_ref[...] = ret_scatter.acc[...]

    def back_give():
        back_ref[...] = back_scatter.acc[...]

    for j in range(outer - 1, -1, -1):
        for e in range(1, inner):
            ret_scatter.across(place.line(j), e).start()

    def backward(j, e):
        k = place.source(place.line(j), e)
        gate = gate_of(dot(xs[k], router, NT), route_of(k))[2]
        low = (gate * us[k].astype(WIDE)).astype(LOW)
        us[k] = low
        grad = (dot(low, w2_of(), NT) * slope[k]).astype(LOW)
        before_grad[k] = grad
        back_part[k] = (
            dot(grad[:, :strip], w1_of(0), NT) + dot(grad[:, strip:], w1_of(1), NT)
        ).astype(LOW)

    def u_here(n, carry):
        for e in range(1, inner):
            u_gather.arrive_y(n, e)
        return carry

    lax.fori_loop(0, outer, u_here, 0)
    u_gather.finish()

    def back_step(n, carry):
        j = outer - 1 - n
        for e in range(1, inner):
            backward(j, e)
            back_scatter.across(place.line(j), e).start()

        @pl.when(j > 0)
        def _():
            ret_scatter.collect(j, False, ret_term, None)

        backward(j, 0)
        return carry

    lax.fori_loop(0, outer, back_step, 0)

    def flat(ref):
        return ref[...].reshape(chips * length, ref.shape[2])

    g2 = dot(flat(act), flat(us), TN)
    g2_own[...] = g2.astype(LOW).reshape(g2_own.shape)
    g2_swap = remote(g2_own.at[:, 1 - core], g2_all.at[rep], p_send.at[0], p_recv.at[0], partner)
    g2_swap.start()
    for j in range(outer - 1, 1, -1):
        back_scatter.collect(j, False, back_term, None)
    g2_swap.wait()
    g2_all[rep] = (g2_own[:, core].astype(WIDE) + g2_all[rep].astype(WIDE)).astype(LOW)
    swaps = []
    for f in range(1, reps):
        swaps.append(
            remote(
                g2_all.at[rep],
                g2_all.at[rep],
                r_send.at[f - 1],
                r_recv.at[f - 1],
                {"rep": lax.rem(rep + f, reps)},
            )
        )
        swaps[-1].start()
    g1 = dot(flat(xs), flat(before_grad), TN)
    split(g1_own, 0, rows, pad, g1)
    g1_swap = remote(g1_own.at[:, 1 - core], g1_ref, p_send.at[1], p_recv.at[1], partner)
    g1_swap.start()
    if outer > 1:
        back_scatter.collect(1, False, back_term, None)
    ret_scatter.collect(0, True, ret_term, ret_give)
    g1_swap.wait()
    g1_ref[...] = (g1_own[:, core].astype(WIDE) + g1_ref[...].astype(WIDE)).astype(LOW)
    for copy in swaps:
        copy.wait()
    value = g2_all[0].astype(WIDE)
    for r in range(1, reps):
        value = value + g2_all[r].astype(WIDE)
    g2_ref[...] = value
    back_scatter.collect(0, True, back_term, back_give)

    def finish():
        x_gather.finish()
        ret_scatter.finish()
        back_scatter.finish()

    return finish


def back_part_of(
    place,
    reps,
    heads,
    rows,
    tok_ref,
    u_ref,
    hidden_ref,
    ffn_ref,
    normed_ref,
    proj_ref,
    probs_ref,
    context_ref,
    whole_ref,
    sum_ref,
    route_ref,
    turned_ref,
    ret_ref,
    norm_ref,
    g1_ref,
    layer_ref,
    input_ref,
    in_out_ref,
    out_out_ref,
    small_out_ref,
    g1_out_ref,
    got,
    x_got,
    rep_all,
    strips,
    s_send,
    s_recv,
    t_send,
    t_recv,
    p_send,
    p_recv,
    r_send,
    r_recv,
    x_send,
    x_recv,
    own_sem,
    *rest,
):
    size = place.size
    chips, outer, inner = place.chips, place.outer, place.inner
    core, chip = place.core, place.chip
    rep = lax.axis_index("rep")
    length, width = tok_ref.shape
    head_size = width // heads
    depth = got.shape[1]
    pad = (depth - SMALL) // 4
    shared = 0
    lead = pl.multiple_of(shared * rep, 16) if shared else 0
    window = pl.ds(lead, depth - shared)
    partner = place.partner()
    grads = whole_ref
    moves = []
    own = pltpu.make_async_copy(g1_ref.at[chip], strips.at[rep, chip], own_sem)
    own.start()
    for i, (d, e) in enumerate(place.pairs()):
        if i > 0:
            target = place.at(d, e)
            moves.append(
                remote(
                    g1_ref.at[target],
                    strips.at[rep, chip],
                    s_send.at[i],
                    s_recv.at[i],
                    place.device(target),
                )
            )
            moves[-1].start()

    router = sum_ref[2:4, :]
    upstream = u_ref[...].astype(WIDE)
    hidden = hidden_ref[...]
    returned = ret_ref[...]
    route = route_ref[...].astype(WIDE)
    logits = dot(ffn_ref[...], sum_ref[...].astype(LOW), NT)
    first, second, gate = gate_of(logits, route)
    layer_ref[...] = (hidden + gate * returned).astype(LOW)
    gate_grad = jnp.sum(upstream * returned, axis=1, keepdims=True)
    scaled = gate * gate_grad
    first_grad = first * (jnp.where(route > 0.5, 0.0, gate_grad) - scaled)
    second_grad = second * (jnp.where(route > 0.5, gate_grad, 0.0) - scaled)
    ffn = ffn_ref[...].astype(WIDE)
    router_grad = jnp.concatenate(
        [
            jnp.sum(ffn * first_grad, axis=0, keepdims=True),
            jnp.sum(ffn * second_grad, axis=0, keepdims=True),
        ],
        axis=0,
    )
    norm_grad = norm_ref[...] + first_grad * router[0:1] + second_grad * router[1:2]
    scale = rms_scale(hidden)
    gain_ffn_grad = jnp.sum(norm_grad * hidden * scale, axis=0, keepdims=True)
    bent = norm_grad * sum_ref[1:2, :]
    hidden_grad = (
        upstream
        + scale * bent
        - hidden * (scale * scale * scale) * jnp.mean(bent * hidden, axis=1, keepdims=True)
    )
    attn_grad = hidden_grad.astype(LOW)
    context_grad = dot(attn_grad, joined(whole_ref, spot_of(3, pad), rows, pad), NT).astype(LOW)
    split(grads, spot_of(3, pad), rows, pad, dot(context_ref[...], attn_grad, TN))

    row = lax.broadcasted_iota(jnp.int32, (length, length), 0)
    col = lax.broadcasted_iota(jnp.int32, (length, length), 1)
    mirror = jnp.where(row + col == length - 1, 1.0, 0.0).astype(LOW)
    blank = jnp.zeros((length, length), WIDE)
    parts = [[], [], []]
    diagonals = []
    for h in range(heads):
        at = slice(h * head_size, (h + 1) * head_size)
        grad = context_grad[:, at]
        probs = probs_ref[h]
        prob_grad = dot(grad, proj_ref[2, :, at], NT)
        summed = jnp.sum(probs * prob_grad, axis=1, keepdims=True)
        low = (probs * (prob_grad - summed)).astype(LOW)
        flipped = dot(low, mirror)
        skewed = pltpu.roll(
            jnp.concatenate([flipped, blank], axis=1), 0, 1, stride=1, stride_axis=0
        )
        diagonals.append(jnp.sum(skewed, axis=0, keepdims=True))
        parts[0].append(dot(low, proj_ref[1, :, at]) * 0.125)
        parts[1].append(dot(low, proj_ref[0, :, at], TN) * 0.125)
        parts[2].append(dot(probs.astype(LOW), grad, TN))
    diagonal = jnp.concatenate(diagonals, axis=0)
    spots = lax.broadcasted_iota(jnp.int32, (length, 2 * length), 0)
    onehot = jnp.where(turned_ref[...] == spots, 1.0, 0.0).astype(LOW)
    high = diagonal.astype(LOW)
    below = (diagonal - high.astype(WIDE)).astype(LOW)
    table_grad = dot(high, onehot, NT) + dot(below, onehot, NT)
    normed = normed_ref[...]
    normed_grad = jnp.zeros((length, width), WIDE)
    for k in range(3):
        projected = jnp.concatenate(parts[k], axis=1).astype(LOW)
        normed_grad = normed_grad + dot(projected, joined(whole_ref, spot_of(k, pad), rows, pad), NT)
        split(grads, spot_of(k, pad), rows, pad, dot(normed, projected, TN))
    inputs = tok_ref[...].astype(WIDE)
    scale = rms_scale(inputs)
    gain_attn_grad = jnp.sum(normed_grad * inputs * scale, axis=0, keepdims=True)
    small = jnp.concatenate(
        [
            gain_attn_grad,
            gain_ffn_grad,
            router_grad,
            jnp.concatenate(
                [table_grad, jnp.zeros((heads, width - length), WIDE)], axis=1
            ),
        ],
        axis=0,
    ).astype(LOW)
    for j in range(size):
        grads[j // 2, j % 2, 2 * pad : 2 * pad + SMALL, :] = small

    kept = got
    scatter = Scatter(place, kept.at[:, window], *rest)

    def swap(k):
        return remote(
            grads.at[k, 1 - core], got.at[k], p_send.at[k], p_recv.at[k], partner
        )

    order = [(j, e) for j in range(outer - 1, -1, -1) for e in range(1, inner)]
    order += [(j, 0) for j in range(outer - 1, -1, -1)]
    for j, e in order:
        swap(place.source(place.line(j), e)).start()
    bent = normed_grad * sum_ref[0:1, :]
    input_ref[...] = (
        hidden_grad
        + scale * bent
        - inputs * (scale * scale * scale) * jnp.mean(bent * inputs, axis=1, keepdims=True)
    )

    def item(n):
        side = max(inner - 1, 1)
        j = n - outer * (inner - 1)
        e = jnp.where(j < 0, 1 + lax.rem(n, side), 0)
        j = outer - 1 - jnp.where(j < 0, lax.div(n, side), j)
        return place.line(j), e

    def end(who):
        return pl.ds(pl.multiple_of((depth - shared) * who, 16), shared)

    def give(k):
        return remote(
            kept.at[k, end(1 - rep)], x_got.at[k], x_send.at[k], x_recv.at[k], {"rep": 1 - rep}
        )

    def cross(n, carry):
        @pl.when(n < chips)
        def _():
            far, e = item(n)
            k = place.source(far, e)
            swap(k).wait_recv()
            kept[k] = (grads[k, core].astype(WIDE) + got[k].astype(WIDE)).astype(LOW)
            if shared:
                give(k).start()

        @pl.when(n > 1)
        def _():
            far, e = item(n - 2)
            k = place.source(far, e)
            if shared:
                give(k).wait_recv()
                kept[k, end(rep)] = (
                    kept[k, end(rep)].astype(WIDE) + x_got[k].astype(WIDE)
                ).astype(LOW)

            @pl.when(e > 0)
            def _():
                scatter.across(far, e).start()

        return carry

    lax.fori_loop(0, chips + 2, cross, 0)
    own.wait()
    for copy in moves:
        copy.wait_recv()
    turns = []
    for f in range(1, reps):
        turns.append(
            remote(
                strips.at[rep],
                strips.at[rep],
                t_send.at[f - 1],
                t_recv.at[f - 1],
                {"rep": lax.rem(rep + f, reps)},
            )
        )
        turns[-1].start()

    def term(k, at):
        at = pl.ds(pl.multiple_of(lead + at.start, 16), 16)
        return kept[k, at].astype(WIDE)

    def pass_on(n, carry):
        scatter.collect(outer - 1 - n, False, term, None)
        return carry

    lax.fori_loop(0, outer - 1, pass_on, 0)

    def give_sum():
        rep_all[rep] = scatter.acc[...].astype(LOW)

    scatter.collect(0, True, term, give_sum)
    swaps = []
    for f in range(1, reps):
        swaps.append(
            remote(
                rep_all.at[rep],
                rep_all.at[rep],
                r_send.at[f - 1],
                r_recv.at[f - 1],
                {"rep": lax.rem(rep + f, reps)},
            )
        )
        swaps[-1].start()
    for copy in turns:
        copy.wait()
    strip = g1_ref.shape[2] // 2
    for k in range(chips):
        value = strips[0, k].astype(WIDE)
        for r in range(1, reps):
            value = value + strips[r, k].astype(WIDE)
        for e in range(2):
            g1_out_ref[e, :, k * strip : (k + 1) * strip] = value[
                :rows, e * strip : (e + 1) * strip
            ]
    for copy in swaps:
        copy.wait()
    if shared:
        both = depth - 2 * shared
        value = jnp.concatenate(
            [
                rep_all[0, :shared].astype(WIDE),
                rep_all[0, shared:].astype(WIDE) + rep_all[1, :both].astype(WIDE),
                rep_all[1, both:].astype(WIDE),
            ],
            axis=0,
        )
    else:
        value = rep_all[0].astype(WIDE)
        for r in range(1, reps):
            value = value + rep_all[r].astype(WIDE)
    for k in range(3):
        in_out_ref[k] = value[spot_of(k, pad) : spot_of(k, pad) + rows]
    out_out_ref[...] = value[spot_of(3, pad) : spot_of(3, pad) + rows]
    small_out_ref[...] = value[2 * pad : 2 * pad + SMALL]
    for copy in moves:
        copy.wait_send()
    for k in range(chips):
        swap(k).wait_send()
        if shared:
            give(k).wait_send()
    scatter.finish()


def layer_kernel(size, reps, heads, counts, *refs):
    groups = []
    for count in counts:
        groups.append(refs[:count])
        refs = refs[count:]
    inputs, outputs, loads, load_sem, front, front_sems, expert, u_sems, back = groups
    tokens, cotangent, attn_in, attn_out, gains, router, table, routes = inputs[:8]
    strips, halves, buckets, turned, lengths = inputs[8:]
    layer_out, input_grad, in_out, out_out, small_out, g1_out, g2_out = outputs
    whole, w1, w2, normed, proj, probs, context, hidden, ffn, totals, columns = front
    x_local, u_local, returned, norm_grad, g1 = loads
    place = Place(size)
    rows = attn_out.shape[0]
    u_gather = Gather(place, u_local, expert[1], *u_sems)
    get = [
        pltpu.make_async_copy(cotangent, u_local, load_sem[0].at[0]),
        pltpu.make_async_copy(tokens, x_local, load_sem[0].at[1]),
    ]
    for copy in get:
        copy.start()

    def more(stage):
        if stage == 0:
            for copy in get:
                copy.wait()
            u_gather.start()
        elif place.outer > 1:
            u_gather.arrive_z(1)

    strips_on, strips_here, front_finish = front_part(
        place,
        reps,
        heads,
        more,
        x_local,
        attn_in,
        attn_out,
        gains,
        router,
        table,
        routes,
        strips,
        halves,
        buckets,
        lengths,
        *front,
        *front_sems,
    )
    expert_finish = expert_part(
        place,
        reps,
        rows,
        strips_on,
        strips_here,
        u_gather,
        ffn,
        u_local,
        w1,
        w2,
        totals,
        columns,
        returned,
        norm_grad,
        g1,
        g2_out,
        *expert,
    )
    front_finish()
    back_part_of(
        place,
        reps,
        heads,
        rows,
        x_local,
        u_local,
        hidden,
        ffn,
        normed,
        proj,
        probs,
        context,
        whole,
        totals,
        routes,
        turned,
        returned,
        norm_grad,
        g1,
        layer_out,
        input_grad,
        in_out,
        out_out,
        small_out,
        g1_out,
        *back,
    )
    expert_finish()


def layer(size, reps, heads, pad, strip, *operands):
    chips = size // 2
    length, width = operands[0].shape
    rows = operands[3].shape[0]
    half = operands[9].shape[1]
    cols = 2 * strip
    depth = 4 * pad + SMALL
    block = (chips, length, width)
    wide = (chips, length, cols)
    row = (length, width)
    weights = (chips, depth, width)
    others = max(reps - 1, 1)
    outputs = (
        jax.ShapeDtypeStruct(row, LOW),
        jax.ShapeDtypeStruct(row, WIDE),
        jax.ShapeDtypeStruct((3, rows, width), WIDE),
        jax.ShapeDtypeStruct((rows, width), WIDE),
        jax.ShapeDtypeStruct((SMALL, width), WIDE),
        jax.ShapeDtypeStruct((2, rows, chips * strip), WIDE),
        jax.ShapeDtypeStruct((2, half, width), WIDE),
    )
    loads = [
        pltpu.VMEM(row, LOW),
        pltpu.VMEM(row, LOW),
        pltpu.VMEM(row, WIDE),
        pltpu.VMEM(row, WIDE),
        pltpu.VMEM((chips, pad, cols), LOW),
    ]
    front = [
        pltpu.VMEM((chips, 2, depth, width), LOW),
        pltpu.VMEM((2, chips, 2, pad, strip), LOW),
        pltpu.VMEM((2, 2, half, width), LOW),
        pltpu.VMEM(row, LOW),
        pltpu.VMEM((3,) + row, LOW),
        pltpu.VMEM((heads, length, length), WIDE),
        pltpu.VMEM(row, LOW),
        pltpu.VMEM(row, WIDE),
        pltpu.VMEM(row, LOW),
        pltpu.VMEM((SMALL, width), WIDE),
        pltpu.VMEM((length, length), WIDE),
    ]
    front_sems = [*Gather.sems(size), *[DMA((chips,))] * 10, DMA, DMA, DMA((2,))]
    expert = [
        pltpu.VMEM(block, LOW),
        pltpu.VMEM(block, LOW),
        pltpu.VMEM(wide, LOW),
        pltpu.VMEM(wide, WIDE),
        pltpu.VMEM(wide, LOW),
        pltpu.VMEM(block, LOW),
        pltpu.VMEM(block, LOW),
        pltpu.VMEM((chips, 2, pad, cols), LOW),
        pltpu.VMEM((2, 2, half, width), LOW),
        pltpu.VMEM((reps, 2, half, width), LOW),
        DMA((2,)),
        DMA((2,)),
        DMA((others,)),
        DMA((others,)),
        DMA((2,)),
        *Gather.sems(size),
        *Scatter.buffers(size, row),
        *[item for n, item in enumerate(Scatter.buffers(size, row)) if n != 3],
    ]
    back = [
        pltpu.VMEM(weights, LOW),
        pltpu.VMEM((1, 16, width), LOW),
        pltpu.VMEM((reps, depth, width), LOW),
        pltpu.VMEM((reps, chips, pad, cols), LOW),
        DMA((chips,)),
        DMA((chips,)),
        DMA((others,)),
        DMA((others,)),
        DMA((chips,)),
        DMA((chips,)),
        DMA((others,)),
        DMA((others,)),
        DMA((chips,)),
        DMA((chips,)),
        DMA,
        *Scatter.buffers(size, (depth, width)),
    ]
    load_sem = [DMA((2,))]
    scratch = [loads, load_sem, front, front_sems, expert, Gather.sems(size), back]
    counts = [len(operands), len(outputs), *[len(group) for group in scratch]]
    far = pl.BlockSpec(memory_space=pl.ANY)
    return pl.pallas_call(
        functools.partial(layer_kernel, size, reps, heads, counts),
        out_shape=outputs,
        in_specs=[far, far, *[VMEM] * 6, far, far, VMEM, VMEM, SMEM],
        out_specs=[VMEM] * len(outputs),
        scratch_shapes=[item for group in scratch for item in group],
        compiler_params=pltpu.CompilerParams(
            collective_id=0, has_side_effects=True, vmem_limit_bytes=60 << 20
        ),
    )(*operands)


def shards(
    size,
    reps,
    tokens,
    cotangent,
    lengths,
    routes,
    bucket_ids,
    attn_in,
    attn_out,
    gains,
    router,
    rel_table,
    expert_in,
    expert_out,
):
    length, width = tokens.shape
    heads = rel_table.shape[1]
    table_rows = rel_table.shape[0]
    chips = size // 2
    rows = attn_out.shape[0]
    pad = rows + -rows % 16
    hidden_units = expert_in.shape[2]
    strip = hidden_units // chips
    half = expert_out.shape[1]
    me = lax.axis_index("shard")

    buckets = jnp.pad(bucket_ids, (0, 1), constant_values=-1).reshape(1, 2 * length)
    turned = jnp.pad(bucket_ids[::-1], (0, 1), constant_values=-1).reshape(1, 2 * length)
    strips = expert_in
    if strip % 128 or pad != rows:
        strips = jnp.transpose(expert_in.reshape(2, rows, chips, strip), (2, 0, 1, 3))
        strips = jnp.pad(strips, ((0, 0), (0, 0), (0, pad - rows), (0, 0)))
    layer_out, input_grad, in_shard, out_shard, sums, expert_in_grad, expert_out_grad = layer(
        size,
        reps,
        heads,
        pad,
        strip,
        tokens,
        cotangent,
        attn_in,
        attn_out,
        gains,
        router,
        rel_table,
        routes,
        strips,
        expert_out,
        buckets,
        turned,
        lengths,
    )
    picked = lax.dynamic_slice(sums, (0, me * rows), (4, rows))
    table_shard = lax.dynamic_slice(sums, (4, me * table_rows), (heads, table_rows)).T
    return (
        layer_out,
        input_grad,
        in_shard,
        out_shard,
        picked[:2],
        picked[2:].T,
        table_shard,
        expert_in_grad,
        expert_out_grad,
    )


def solution(mesh):
    placed = (
        P(("rep", "shard"), None),
        P(("rep", "shard"), None),
        P(("rep", "shard"), None),
        P(("rep", "shard"), None),
        P(),
        P(None, "shard", None),
        P("shard", None),
        P(None, "shard"),
        P("shard", None),
        P("shard", None),
        P(None, "shard", None),
        P(None, "shard", None),
    )
    return jax.shard_map(
        functools.partial(shards, mesh.shape["shard"], mesh.shape["rep"]),
        mesh=mesh,
        in_specs=placed,
        out_specs=(
            P(("rep", "shard"), None),
            P(("rep", "shard"), None),
            P(None, "shard", None),
            P("shard", None),
            P(None, "shard"),
            P("shard", None),
            P("shard", None),
            P(None, "shard", None),
            P(None, "shard", None),
        ),
        check_vma=False,
    )
```

```python
import functools

import jax
import jax.numpy as jnp
from jax import lax
from jax.experimental import pallas as pl
from jax.experimental.pallas import tpu as pltpu
from jax.sharding import PartitionSpec as P

EPSILON = 1e-06
SMALL = 16
LOW = jnp.bfloat16
WIDE = jnp.float32
NT = (((1,), (1,)), ((), ()))
TN = (((0,), (0,)), ((), ()))
MESH = pl.DeviceIdType.MESH
VMEM = pl.BlockSpec(memory_space=pltpu.VMEM)
SMEM = pl.BlockSpec(memory_space=pltpu.SMEM)
DMA = pltpu.SemaphoreType.DMA


def grid_of(size):
    chips = size // 2
    outer = 4 if chips % 4 == 0 else 1
    return outer, chips // outer


class Place:
    def __init__(self, size):
        self.size = size
        self.outer, self.inner = grid_of(size)
        self.chips = size // 2
        me = lax.axis_index("shard")
        self.index = me
        self.core = lax.rem(me, 2)
        self.chip = lax.div(me, 2)
        self.z = lax.div(self.chip, self.inner)
        self.y = lax.rem(self.chip, self.inner)

    def at(self, dz, dy):
        far = lax.rem(self.z + dz + self.outer, self.outer)
        near = lax.rem(self.y + dy + self.inner, self.inner)
        return far * self.inner + near

    def device(self, chip):
        return {"shard": chip * 2 + self.core}

    def partner(self):
        return {"shard": self.chip * 2 + 1 - self.core}

    def pairs(self):
        return [(d, e) for d in range(self.outer) for e in range(self.inner)]

    def line(self, j):
        z, top = self.z, self.outer - 1
        short = jnp.minimum(z, top - z)
        t = lax.div(j + 1, 2)
        near = jnp.where(lax.rem(j, 2) == 1, z - t, z + t)
        far = jnp.where(z <= top - z, z + j - short, z - j + short)
        return jnp.where(j <= 2 * short, near, far)

    def source(self, far, e):
        return far * self.inner + lax.rem(self.y - e + self.inner, self.inner)

    def pair(self, i):
        q, r = lax.div(i + self.inner - 1, self.inner) - 1, lax.rem(i + self.inner - 1, self.inner)
        last = q == self.outer - 1
        e = jnp.where(last, r + 1, r)
        j = jnp.where(last, q, jnp.where(r == 0, q + 1, q))
        return jnp.where(i == 0, 0, j), jnp.where(i == 0, 0, e)

    def greet(self, chips, reps):
        barrier = pltpu.get_barrier_semaphore()
        count = 0

        def signal(target):
            pl.semaphore_signal(barrier, inc=1, device_id=target, device_id_type=MESH)

        for dz, dy in self.pairs()[1:]:
            if chips or dz == 0:
                signal(self.device(self.at(dz, dy)))
                count += 1
        signal(self.partner())
        count += 1
        if not chips:
            below = jnp.where(self.z > 0, 1, 0)
            above = jnp.where(self.z < self.outer - 1, 1, 0)

            @pl.when(self.z > 0)
            def _():
                signal(self.device(self.chip - self.inner))

            @pl.when(self.z < self.outer - 1)
            def _():
                signal(self.device(self.chip + self.inner))

            count = count + below + above
        for f in range(1, reps):
            signal({"rep": lax.rem(lax.axis_index("rep") + f, reps)})
            count += 1
        pl.semaphore_wait(barrier, count)


def remote(src, dst, send_sem, recv_sem, target):
    return pltpu.make_async_remote_copy(
        src_ref=src,
        dst_ref=dst,
        send_sem=send_sem,
        recv_sem=recv_sem,
        device_id=target,
        device_id_type=MESH,
    )


def dot(a, b, dims=None):
    if dims is None:
        return jnp.dot(a, b, preferred_element_type=WIDE)
    return lax.dot_general(a, b, dims, preferred_element_type=WIDE)


def joined(ref, first, rows, pad):
    chips, _, _, width = ref.shape
    if rows == pad:
        return ref[:, :, first : first + rows, :].reshape(chips * 2 * rows, width)
    parts = [ref[j // 2, j % 2, first : first + rows, :].astype(WIDE) for j in range(chips * 2)]
    return jnp.concatenate(parts, axis=0).astype(LOW)


def split(ref, first, rows, pad, values):
    chips, _, _, width = ref.shape
    if rows == pad:
        ref[:, :, first : first + rows, :] = values.reshape(chips, 2, rows, width).astype(LOW)
        return
    for j in range(chips * 2):
        ref[j // 2, j % 2, first : first + rows, :] = values[j * rows : (j + 1) * rows].astype(LOW)


def rms_scale(values):
    return lax.rsqrt(jnp.mean(values * values, axis=1, keepdims=True) + EPSILON)


def gate_of(logits, route):
    first, second = logits[:, 2:3], logits[:, 3:4]
    top = jnp.maximum(first, second)
    first, second = jnp.exp(first - top), jnp.exp(second - top)
    total = first + second
    first, second = first / total, second / total
    return first, second, jnp.where(route > 0.5, second, first)


class Gather:
    def __init__(self, place, own, slots, up_send, down_send, z_recv, y_send, y_recv):
        self.place, self.own, self.slots = place, own, slots
        self.up_send, self.down_send, self.z_recv = up_send, down_send, z_recv
        self.y_send, self.y_recv = y_send, y_recv

    @staticmethod
    def sems(size):
        outer, inner = grid_of(size)
        side = max(inner - 1, 1)
        return [DMA((outer,))] * 3 + [DMA((outer, side))] * 2

    def up(self, src, far):
        place = self.place
        slot = self.slots.at[place.source(far, 0)]
        target = place.device(place.chip + place.inner)
        return remote(src, slot, self.up_send.at[far], self.z_recv.at[far], target)

    def down(self, src, far):
        place = self.place
        slot = self.slots.at[place.source(far, 0)]
        target = place.device(place.chip - place.inner)
        return remote(src, slot, self.down_send.at[far], self.z_recv.at[far], target)

    def across(self, src, far, e):
        place = self.place
        slot = self.slots.at[place.source(far, 0)]
        target = place.device(place.at(0, e))
        return remote(
            src, slot, self.y_send.at[far, e - 1], self.y_recv.at[far, e - 1], target
        )

    def spread(self, src, far, own):
        place = self.place

        @pl.when(place.z < place.outer - 1 if own else jnp.logical_and(far < place.z, place.z < place.outer - 1))
        def _():
            self.up(src, far).start()

        @pl.when(place.z > 0 if own else jnp.logical_and(far > place.z, place.z > 0))
        def _():
            self.down(src, far).start()

        for e in range(1, place.inner):
            self.across(src, far, e).start()

    def start(self):
        self.spread(self.own, self.place.z, True)

    def arrive_z(self, j):
        far = self.place.line(j)
        source = self.place.source(far, 0)
        slot = self.slots.at[source]
        remote(
            self.own, slot, self.up_send.at[far], self.z_recv.at[far], self.place.partner()
        ).wait_recv()
        self.spread(slot, far, False)
        return source

    def arrive_y(self, j, e):
        far = self.place.line(j)
        source = self.place.source(far, e)
        remote(
            self.own,
            self.slots.at[source],
            self.y_send.at[far, e - 1],
            self.y_recv.at[far, e - 1],
            self.place.partner(),
        ).wait_recv()
        return source

    def arrive(self, j, e):
        @pl.when(jnp.logical_and(j > 0, e == 0))
        def _():
            self.arrive_z(j)

        @pl.when(e > 0)
        def _():
            self.arrive_y(j, e)

        return self.place.source(self.place.line(j), e)

    def finish(self):
        place = self.place

        def sent(far, carry):
            @pl.when(jnp.logical_and(far <= place.z, place.z < place.outer - 1))
            def _():
                self.up(self.own, far).wait_send()

            @pl.when(jnp.logical_and(far >= place.z, place.z > 0))
            def _():
                self.down(self.own, far).wait_send()

            for e in range(1, place.inner):
                self.across(self.own, far, e).wait_send()
            return carry

        lax.fori_loop(0, place.outer, sent, 0)


class Scatter:
    def __init__(self, place, part, y_buf, z_out, z_in, acc, y_send, y_recv, z_send, z_recv):
        self.place, self.part, self.acc = place, part, acc
        self.y_buf, self.z_out, self.z_in = y_buf, z_out, z_in
        self.y_send, self.y_recv, self.z_send, self.z_recv = y_send, y_recv, z_send, z_recv

    @staticmethod
    def buffers(size, block):
        outer, inner = grid_of(size)
        side = max(inner - 1, 1)
        return [
            pltpu.VMEM((outer, side) + block, LOW),
            pltpu.VMEM((max(outer - 1, 1),) + block, LOW),
            pltpu.VMEM((outer + 1,) + block, LOW),
            pltpu.VMEM(block, WIDE),
            DMA((outer, side)),
            DMA((outer, side)),
            DMA((outer,)),
            DMA((2, outer)),
        ]

    def across(self, far, e):
        place = self.place
        return remote(
            self.part.at[place.source(far, e)],
            self.y_buf.at[far, e - 1],
            self.y_send.at[far, e - 1],
            self.y_recv.at[far, e - 1],
            place.device(place.at(0, -e)),
        )

    def slot(self, far, way, z):
        return far if way == 0 else jnp.where(far == z, self.place.outer, far)

    def leave(self, far):
        return jnp.where(far < self.place.z, far, jnp.maximum(far - 1, 0))

    def along(self, far, way, z=None):
        place = self.place
        target = place.chip + (place.inner if way == 0 else -place.inner)
        if z is None:
            z = place.z + (1 if way == 0 else -1)
        return remote(
            self.z_out.at[self.leave(far)],
            self.z_in.at[self.slot(far, way, z)],
            self.z_send.at[far],
            self.z_recv.at[way, far],
            place.device(target),
        )

    def collect(self, j, last, first_term, give):
        place, acc = self.place, self.acc
        far = place.line(j)
        count = acc.shape[0] // 16
        for e in range(1, place.inner):
            self.across(far, e).wait_recv()

        def rows(n):
            return pl.ds(pl.multiple_of(n * 16, 16), 16)

        def begin(n, carry):
            value = first_term(place.source(far, 0), rows(n))
            for e in range(1, place.inner):
                value = value + self.y_buf[far, e - 1, rows(n)].astype(WIDE)
            acc[rows(n)] = value
            return carry

        lax.fori_loop(0, count, begin, 0, unroll=True)
        for way in range(2):
            more = place.z > 0 if way == 0 else place.z < place.outer - 1
            if not last:
                more = jnp.logical_and(more, far > place.z if way == 0 else far < place.z)

            @pl.when(more)
            def _(way=way):
                self.along(far, way, place.z).wait_recv()

                def add(n, carry):
                    acc[rows(n)] += self.z_in[self.slot(far, way, place.z), rows(n)].astype(WIDE)
                    return carry

                lax.fori_loop(0, count, add, 0, unroll=True)

        if last:
            give()
            return
        self.z_out[self.leave(far)] = acc[...].astype(LOW)

        @pl.when(far > place.z)
        def _():
            self.along(far, 0).start()

        @pl.when(far < place.z)
        def _():
            self.along(far, 1).start()

    def finish(self):
        place = self.place

        def sent(far, carry):
            for e in range(1, place.inner):
                self.across(far, e).wait_send()

            @pl.when(far != place.z)
            def _():
                self.along(far, 0).wait_send()

            return carry

        lax.fori_loop(0, place.outer, sent, 0)


def shared_rows(depth, reps):
    return depth * 5 // 256 * 16 if reps == 2 else 0


def spot_of(section, pad):
    return section * pad + (SMALL if section > 1 else 0)


def padded(ref):
    return jnp.concatenate([ref[...], jnp.full((1, 1), -1, jnp.int32)], axis=1)


def column(line):
    count = line.shape[1]
    return jnp.transpose(jnp.broadcast_to(line, (count, count)))[:, :1]


def placing(count, width, first):
    row = lax.broadcasted_iota(jnp.int32, (count, width), 0)
    col = lax.broadcasted_iota(jnp.int32, (count, width), 1)
    return jnp.where(col == row + first, 1.0, 0.0).astype(LOW)


def front_part(
    place,
    reps,
    heads,
    more,
    tok_ref,
    in_ref,
    out_ref,
    gain_ref,
    router_ref,
    table_ref,
    here_ref,
    strip_ref,
    half_ref,
    bucket_ref,
    length_ref,
    whole_ref,
    w1_ref,
    w2_ref,
    normed_ref,
    proj_ref,
    probs_ref,
    context_ref,
    hidden_ref,
    ffn_ref,
    sum_ref,
    route_ref,
    g_up,
    g_down,
    g_z,
    g_send,
    g_recv,
    c_send,
    c_recv,
    e_send,
    e_recv,
    x_send,
    x_recv,
    s_send,
    s_recv,
    f_send,
    f_recv,
    n_send,
    n_recv,
    d_send,
    d_recv,
    h_send,
    h_recv,
    own_sem,
):
    size, chips = place.size, place.chips
    core, chip = place.core, place.chip
    length, width = tok_ref.shape
    rows = out_ref.shape[0]
    pad = w1_ref.shape[3]
    strip = w1_ref.shape[4]
    head_size = width // heads
    depth = whole_ref.shape[2]
    shared = shared_rows(depth, reps)
    rep = lax.axis_index("rep") if shared else 0
    window = pl.ds(pl.multiple_of(shared * rep, 16), depth - shared)
    for k in range(3):
        whole_ref[chip, core, spot_of(k, pad) : spot_of(k, pad) + rows, :] = in_ref[k]
    whole_ref[chip, core, spot_of(3, pad) : spot_of(3, pad) + rows, :] = out_ref[...]
    spot = placing(rows, width, place.index * rows)
    table_rows = table_ref.shape[0]
    here = jnp.broadcast_to(here_ref[...].astype(WIDE), (heads, length))
    lower = jnp.concatenate(
        [
            dot(table_ref[...], placing(table_rows, length, place.index * table_rows), TN),
            here,
            jnp.zeros((heads, width - 2 * length), WIDE),
        ],
        axis=1,
    )
    small = jnp.concatenate(
        [dot(gain_ref[...], spot), dot(router_ref[...], spot), lower], axis=0
    )
    whole_ref[chip, core, 2 * pad : 2 * pad + SMALL, :] = small.astype(LOW)
    place.greet(True, reps)
    partner = place.partner()
    slots = whole_ref.at[:, core, window]
    gather = Gather(place, slots.at[chip], slots, g_up, g_down, g_z, g_send, g_recv)
    gather.start()

    def dup(source):
        block = whole_ref.at[source, core, window]
        return remote(block, block, c_send.at[source], c_recv.at[source], partner)

    def end(who):
        return pl.ds(pl.multiple_of((depth - shared) * who, 16), shared)

    def dup_end(source):
        block = whole_ref.at[source, core, end(1 - rep)]
        return remote(block, block, e_send.at[source], e_recv.at[source], partner)

    def give(source, who):
        block = whole_ref.at[source, core, end(who)]
        target = {"rep": 1 - rep}
        return remote(block, block, x_send.at[source], x_recv.at[source], target)

    swapped = shared and strip % 128 == 0 and rows == pad

    def strip_of(k, which):
        if strip % 128 == 0 and rows == pad:
            return strip_ref.at[which, :, pl.ds(pl.multiple_of(k * strip, 128), strip)]
        return strip_ref.at[k]

    mine = rep if swapped else slice(None)
    theirs = 1 - rep

    dup(chip).start()
    if shared:
        dup_end(chip).start()
    local = [
        pltpu.make_async_copy(strip_of(chip, slice(None)), w1_ref.at[:, chip, core], own_sem.at[0]),
        pltpu.make_async_copy(half_ref, w2_ref.at[:, core], own_sem.at[1]),
    ]
    for copy in local:
        copy.start()
    halves = remote(half_ref, w2_ref.at[:, core], h_send, h_recv, partner)
    halves.start()

    def arrive(i, carry):
        j, e = place.pair(i)
        source = gather.arrive(j, e)
        if shared:
            give(source, rep).start()
        dup(source).start()
        if shared:

            @pl.when(i > 2)
            def _():
                take(i - 2)

        return carry

    def take(i):
        j, e = place.pair(i)
        source = place.source(place.line(j), e)
        give(source, 1 - rep).wait_recv()
        dup_end(source).start()

    late = chips - 2 * (place.inner - 1)
    lax.fori_loop(1, late, arrive, 0)
    strips = []
    for i, (d, e) in enumerate(place.pairs()):
        if i > 0:
            target = place.at(d, e)
            copy = remote(
                strip_of(target, mine),
                w1_ref.at[mine, chip, core],
                s_send.at[i],
                s_recv.at[i],
                place.device(target),
            )
            copy.start()
            strips.append(copy)
    lax.fori_loop(late, chips, arrive, 0)
    if shared:
        for i in range(chips - 2, chips):
            take(i)

    def other(source, carry):
        block = whole_ref.at[source, 1 - core, window]
        remote(block, block, c_send.at[source], c_recv.at[source], partner).wait_recv()
        if shared:
            block = whole_ref.at[source, 1 - core, end(1 - rep)]
            remote(block, block, e_send.at[source], e_recv.at[source], partner).wait_recv()
        return carry

    more(0)
    lax.fori_loop(0, chips, other, 0)

    total = jnp.zeros((SMALL, width), WIDE)
    for j in range(size):
        total = total + whole_ref[j // 2, j % 2, 2 * pad : 2 * pad + SMALL, :].astype(WIDE)
    sum_ref[...] = total
    lines = [
        whole_ref[k, core, 2 * pad : 2 * pad + SMALL, length : 2 * length].astype(WIDE)[4:5]
        for k in range(chips)
    ]
    lines.append(jnp.zeros((length - chips, length), WIDE))
    route_ref[...] = jnp.transpose(jnp.concatenate(lines, axis=0))

    inputs = tok_ref[...].astype(WIDE)
    normed = (inputs * rms_scale(inputs) * total[0:1]).astype(LOW)
    normed_ref[...] = normed
    for k in range(3):
        proj_ref[k] = dot(normed, joined(whole_ref, spot_of(k, pad), rows, pad)).astype(LOW)
    spots = lax.broadcasted_iota(jnp.int32, (length, 2 * length), 0)
    onehot = jnp.where(padded(bucket_ref) == spots, 1.0, 0.0).astype(LOW)
    table = total[:, :length].astype(LOW)
    bias = dot(table, onehot)
    down = lax.broadcasted_iota(jnp.int32, (length, length), 0)
    across = lax.broadcasted_iota(jnp.int32, (length, length), 1)
    part_q = jnp.zeros((length, length), jnp.int32)
    part_k = jnp.zeros((length, length), jnp.int32)
    bound = jnp.int32(0)
    for s in range(length_ref.shape[1]):
        bound = bound + length_ref[0, s]
        part_q = part_q + jnp.where(down >= bound, 1, 0)
        part_k = part_k + jnp.where(across >= bound, 1, 0)
    allowed = part_q == part_k
    def moved(i):
        return place.at(-lax.div(i, place.inner), -lax.rem(i, place.inner))

    def along_x(i, which):
        block = w1_ref.at[which, moved(i), core]
        return remote(block, block, f_send.at[i], f_recv.at[i], {"rep": theirs})

    def to_partner(block, i, send, recv):
        return remote(block, block, send.at[i], recv.at[i], partner)

    def pass_on(i, carry):
        block = w1_ref.at[mine, moved(i), core]
        remote(block, block, s_send.at[i], s_recv.at[i], partner).wait_recv()
        if swapped:
            along_x(i, rep).start()
        to_partner(block, i, d_send, d_recv).start()
        return carry

    def pass_last(i, carry):
        along_x(i, theirs).wait_recv()
        to_partner(w1_ref.at[theirs, moved(i), core], i, n_send, n_recv).start()
        return carry

    def strips_on(stage):
        if stage == 0:
            local[0].wait()
            to_partner(w1_ref.at[:, chip, core], 0, d_send, d_recv).start()
            lax.fori_loop(1, chips, pass_on, 0)
        elif swapped:
            lax.fori_loop(1, chips, pass_last, 0)

    def last(i, carry):
        source = moved(i)

        @pl.when(i > 0)
        def _():
            to_partner(w1_ref.at[mine, source, core], i, d_send, d_recv).wait_send()
            to_partner(w1_ref.at[mine, source, 1 - core], i, d_send, d_recv).wait_recv()
            if swapped:
                to_partner(w1_ref.at[theirs, source, core], i, n_send, n_recv).wait_send()
                to_partner(w1_ref.at[theirs, source, 1 - core], i, n_send, n_recv).wait_recv()

        dup(source).wait_send()
        if shared:
            dup_end(source).wait_send()
        return carry

    def strips_here():
        to_partner(w1_ref.at[:, chip, core], 0, d_send, d_recv).wait_send()
        to_partner(w1_ref.at[:, chip, 1 - core], 0, d_send, d_recv).wait_recv()
        lax.fori_loop(0, chips, last, 0)
        local[1].wait()
        halves.wait()

    def sent(i, carry):
        block = w1_ref.at[mine, chip, core]
        remote(block, block, s_send.at[i], s_recv.at[i], partner).wait_send()
        if shared:
            give(moved(i), rep).wait_send()
        if swapped:
            along_x(i, rep).wait_send()
        return carry

    parts = []
    for h in range(heads):
        if h == 2 * heads // 3:
            more(1, strips_on)
        at = slice(h * head_size, (h + 1) * head_size)
        raw = dot(proj_ref[0, :, at], proj_ref[1, :, at], NT)
        spread = jnp.broadcast_to(bias[4 + h : 5 + h, :], (length, 2 * length))
        skewed = pltpu.roll(spread, length + 1, 1, stride=1, stride_axis=0)
        scores = jnp.where(allowed, raw * 0.125 + skewed[:, :length], -1e30)
        expo = jnp.exp(scores - jnp.max(scores, axis=1, keepdims=True))
        probs = expo / jnp.sum(expo, axis=1, keepdims=True)
        probs_ref[h] = probs
        parts.append(dot(probs.astype(LOW), proj_ref[2, :, at]))
    context = jnp.concatenate(parts, axis=1).astype(LOW)
    context_ref[...] = context
    hidden = inputs + dot(context, joined(whole_ref, spot_of(3, pad), rows, pad))
    hidden_ref[...] = hidden
    ffn_ref[...] = (hidden * rms_scale(hidden) * total[1:2]).astype(LOW)

    def finish():
        lax.fori_loop(1, chips, sent, 0)
        gather.finish()

    return strips_on, strips_here, finish


def expert_part(
    place,
    reps,
    rows,
    strips_on,
    strips_here,
    u_gather,
    x_ref,
    u_ref,
    w1_ref,
    w2_ref,
    sum_ref,
    route_ref,
    ret_ref,
    back_ref,
    router_ref,
    g1_ref,
    g2_ref,
    xs,
    us,
    act,
    slope,
    before_grad,
    ret_part,
    back_part,
    g1_own,
    g2_own,
    g2_all,
    p_send,
    p_recv,
    r_send,
    r_recv,
    own_sem,
    *rest,
):
    chips, outer, inner = place.chips, place.outer, place.inner
    core, chip = place.core, place.chip
    rep = lax.axis_index("rep")
    length, width = x_ref.shape
    strip = w1_ref.shape[4]
    cols = 2 * strip
    pad = g1_own.shape[2]
    partner = place.partner()
    x_gather = Gather(place, x_ref, xs, *rest[:5])
    back_scatter = Scatter(place, back_part, *rest[5:13])
    ret_scatter = Scatter(place, ret_part, *rest[13:16], rest[8], *rest[16:20])
    x_gather.start()
    strips_on(1)
    own = [
        pltpu.make_async_copy(x_ref, xs.at[chip], own_sem.at[0]),
        pltpu.make_async_copy(u_ref, us.at[chip], own_sem.at[1]),
    ]
    for copy in own:
        copy.start()
    for copy in own:
        copy.wait()
    for j in range(2, outer - 1):
        u_gather.arrive_z(j)
    strips_here()

    def w1_of(e):
        if rows == pad:
            return w1_ref[e].reshape(width, strip)
        parts = [w1_ref[e, j // 2, j % 2, :rows].astype(WIDE) for j in range(chips * 2)]
        return jnp.concatenate(parts, axis=0).astype(LOW)

    def w2_of():
        return w2_ref[...].reshape(cols, width)

    lane = lax.broadcasted_iota(jnp.int32, (length, length), 1)
    side = lax.broadcasted_iota(jnp.int32, (length, cols), 1) >= strip
    router = sum_ref[...].astype(LOW)

    def route_of(k):
        return jnp.sum(jnp.where(lane == k, route_ref[...], 0.0), axis=1, keepdims=True)

    def forward(i, carry):
        j, e = place.pair(i)
        k = x_gather.arrive(j, e)
        before = jnp.concatenate([dot(xs[k], w1_of(0)), dot(xs[k], w1_of(1))], axis=1)
        keep = jnp.logical_xor(side, route_of(k) < 0.5)
        square = before * before
        bent = jnp.tanh(0.7978845608 * before * (1.0 + 0.044715 * square))
        half = 0.5 * (1.0 + bent)
        rise = half + 0.5 * before * (1.0 - bent * bent) * 0.7978845608 * (
            1.0 + 0.134145 * square
        )
        active = jnp.where(keep, before * half, 0.0).astype(LOW)
        act[k] = active
        slope[k] = jnp.where(keep, rise, 0.0)
        ret_part[k] = dot(active, w2_of()).astype(LOW)
        return carry

    late = chips - 2 * (inner - 1)
    lax.fori_loop(0, late // 2, forward, 0)
    if outer > 2:
        u_gather.arrive_z(outer - 1)
    lax.fori_loop(late // 2, chips, forward, 0)

    def ret_term(k, at):
        return ret_part[k, at].astype(WIDE)

    def back_term(k, at):
        return back_part[k, at].astype(WIDE)

    def ret_give():
        ret_ref[...] = ret_scatter.acc[...]

    def back_give():
        back_ref[...] = back_scatter.acc[...]

    def ret_collect(j):
        ret_scatter.collect(j, j == 0, ret_term, ret_give)


    def backward(j, e):
        k = place.source(place.line(j), e)
        route = route_of(k)
        first, second, gate = gate_of(dot(xs[k], router, NT), route)
        pulled = dot(us[k], w2_of(), NT)
        us[k] = (gate * us[k].astype(WIDE)).astype(LOW)
        gate_grad = jnp.sum(act[k].astype(WIDE) * pulled, axis=1, keepdims=True)
        grad = (gate * pulled * slope[k]).astype(LOW)
        before_grad[k] = grad
        shared = gate * gate_grad
        first = first * (jnp.where(route > 0.5, 0.0, gate_grad) - shared)
        second = second * (jnp.where(route > 0.5, gate_grad, 0.0) - shared)
        tokens = xs[k].astype(WIDE)
        router_ref[0:1] += jnp.sum(tokens * first, axis=0, keepdims=True)
        router_ref[1:2] += jnp.sum(tokens * second, axis=0, keepdims=True)
        back_part[k] = (
            dot(grad[:, :strip], w1_of(0), NT)
            + dot(grad[:, strip:], w1_of(1), NT)
            + first * sum_ref[2:3, :]
            + second * sum_ref[3:4, :]
        ).astype(LOW)

    router_ref[...] = jnp.zeros_like(router_ref)

    def u_here(n, carry):
        for e in range(1, inner):
            u_gather.arrive_y(n, e)
        return carry

    early = outer - 1 if outer > 1 else 0
    for e in range(1, inner):
        ret_scatter.across(place.line(early), e).start()
    lax.fori_loop(0, outer, u_here, 0)
    u_gather.finish()

    def back_step(n, carry):
        j = outer - 1 - n
        for e in range(1, inner):
            backward(j, e)
            back_scatter.across(place.line(j), e).start()
        backward(j, 0)
        return carry

    lax.fori_loop(0, outer, back_step, 0)
    for j in range(early - 1, -1, -1):
        for e in range(1, inner):
            ret_scatter.across(place.line(j), e).start()

    def flat(ref):
        return ref[...].reshape(chips * length, ref.shape[2])

    g2 = dot(flat(act), flat(us), TN)
    g2_own[...] = g2.astype(LOW).reshape(g2_own.shape)
    g2_swap = remote(g2_own.at[:, 1 - core], g2_all.at[rep], p_send.at[0], p_recv.at[0], partner)
    g2_swap.start()
    for j in range(outer - 1, 1, -1):
        back_scatter.collect(j, False, back_term, None)
    g2_swap.wait()
    g2_all[rep] = (g2_own[:, core].astype(WIDE) + g2_all[rep].astype(WIDE)).astype(LOW)
    swaps = []
    for f in range(1, reps):
        swaps.append(
            remote(
                g2_all.at[rep],
                g2_all.at[rep],
                r_send.at[f - 1],
                r_recv.at[f - 1],
                {"rep": lax.rem(rep + f, reps)},
            )
        )
        swaps[-1].start()
    g1 = dot(flat(xs), flat(before_grad), TN)
    split(g1_own, 0, rows, pad, g1)
    g1_swap = remote(g1_own.at[:, 1 - core], g1_ref, p_send.at[1], p_recv.at[1], partner)
    g1_swap.start()
    if outer > 1:
        back_scatter.collect(1, False, back_term, None)
    back_scatter.collect(0, True, back_term, back_give)
    g1_swap.wait()
    g1_ref[...] = (g1_own[:, core].astype(WIDE) + g1_ref[...].astype(WIDE)).astype(LOW)

    def finish():
        for copy in swaps:
            copy.wait()
        value = g2_all[0].astype(WIDE)
        for r in range(1, reps):
            value = value + g2_all[r].astype(WIDE)
        g2_ref[...] = value
        x_gather.finish()
        ret_scatter.finish()
        back_scatter.finish()

    return ret_collect, finish


def back_part_of(
    place,
    reps,
    heads,
    rows,
    tok_ref,
    u_ref,
    hidden_ref,
    ffn_ref,
    normed_ref,
    proj_ref,
    probs_ref,
    context_ref,
    whole_ref,
    sum_ref,
    route_ref,
    bucket_ref,
    ret_collect,
    ret_ref,
    norm_ref,
    router_ref,
    g1_ref,
    layer_ref,
    input_ref,
    in_out_ref,
    out_out_ref,
    small_out_ref,
    g1_out_ref,
    got,
    x_got,
    g1_got,
    rep_all,
    strips,
    s_send,
    s_recv,
    t_send,
    t_recv,
    p_send,
    p_recv,
    r_send,
    r_recv,
    x_send,
    x_recv,
    own_sem,
    *rest,
):
    size = place.size
    chips, outer, inner = place.chips, place.outer, place.inner
    core, chip = place.core, place.chip
    rep = lax.axis_index("rep")
    length, width = tok_ref.shape
    head_size = width // heads
    depth = got.shape[1]
    pad = (depth - SMALL) // 4
    shared = 0
    lead = pl.multiple_of(shared * rep, 16) if shared else 0
    window = pl.ds(lead, depth - shared)
    partner = place.partner()
    grads = whole_ref
    strip = g1_ref.shape[2] // 2
    swapped = reps == 2 and strip % 128 == 0

    def half(which):
        return pl.ds(pl.multiple_of(which * strip, 128), strip)

    g1_swap = remote(
        g1_ref.at[:, :, half(1 - rep)] if swapped else g1_ref,
        g1_got if swapped else g1_ref,
        x_send.at[0],
        x_recv.at[0],
        {"rep": lax.rem(rep + 1, reps)},
    )
    if swapped:
        g1_swap.start()
    moves = []
    origin = g1_got if swapped else g1_ref
    own = pltpu.make_async_copy(origin.at[chip], strips.at[rep, chip], own_sem)
    for i, (d, e) in enumerate(place.pairs()):
        if i > 0:
            target = place.at(d, e)
            moves.append(
                remote(
                    origin.at[target],
                    strips.at[rep, chip],
                    s_send.at[i],
                    s_recv.at[i],
                    place.device(target),
                )
            )

    def strips_off():
        if swapped:
            g1_swap.wait()
            g1_got[...] = (
                g1_got[...].astype(WIDE) + g1_ref[:, :, half(rep)].astype(WIDE)
            ).astype(LOW)
        for copy in [own, *moves]:
            copy.start()

    upstream = u_ref[...].astype(WIDE)
    hidden = hidden_ref[...]
    route = column(route_ref[...].astype(WIDE))
    gate = gate_of(dot(ffn_ref[...], sum_ref[...].astype(LOW), NT), route)[2]
    norm_grad = norm_ref[...]
    scale = rms_scale(hidden)
    gain_ffn_grad = jnp.sum(norm_grad * hidden * scale, axis=0, keepdims=True)
    bent = norm_grad * sum_ref[1:2, :]
    hidden_grad = (
        upstream
        + scale * bent
        - hidden * (scale * scale * scale) * jnp.mean(bent * hidden, axis=1, keepdims=True)
    )
    attn_grad = hidden_grad.astype(LOW)
    context_grad = dot(attn_grad, joined(whole_ref, spot_of(3, pad), rows, pad), NT).astype(LOW)
    split(grads, spot_of(3, pad), rows, pad, dot(context_ref[...], attn_grad, TN))

    row = lax.broadcasted_iota(jnp.int32, (length, length), 0)
    col = lax.broadcasted_iota(jnp.int32, (length, length), 1)
    mirror = jnp.where(row + col == length - 1, 1.0, 0.0).astype(LOW)
    blank = jnp.zeros((length, length), WIDE)
    parts = [[], [], []]
    diagonals = []
    for h in range(heads):
        if h in (heads // 3, 5 * heads // 6) and outer > 2:
            ret_collect(outer - 1 if h == heads // 3 else outer - 2)
        at = slice(h * head_size, (h + 1) * head_size)
        grad = context_grad[:, at]
        probs = probs_ref[h]
        prob_grad = dot(grad, proj_ref[2, :, at], NT)
        summed = jnp.sum(probs * prob_grad, axis=1, keepdims=True)
        low = (probs * (prob_grad - summed)).astype(LOW)
        flipped = dot(mirror, low)
        skewed = pltpu.roll(
            jnp.concatenate([flipped, blank], axis=1), 0, 1, stride=1, stride_axis=0
        )
        diagonals.append(jnp.sum(skewed, axis=0, keepdims=True))
        parts[0].append(dot(low, proj_ref[1, :, at]) * 0.125)
        parts[1].append(dot(low, proj_ref[0, :, at], TN) * 0.125)
        parts[2].append(dot(probs.astype(LOW), grad, TN))
    diagonal = jnp.concatenate(diagonals, axis=0)
    spots = lax.broadcasted_iota(jnp.int32, (length, 2 * length), 0)
    onehot = jnp.where(padded(bucket_ref) == spots, 1.0, 0.0).astype(LOW)
    high = diagonal.astype(LOW)
    below = (diagonal - high.astype(WIDE)).astype(LOW)
    table_grad = dot(high, onehot, NT) + dot(below, onehot, NT)
    normed = normed_ref[...]
    normed_grad = jnp.zeros((length, width), WIDE)
    for k in range(3):
        projected = jnp.concatenate(parts[k], axis=1).astype(LOW)
        normed_grad = normed_grad + dot(projected, joined(whole_ref, spot_of(k, pad), rows, pad), NT)
        split(grads, spot_of(k, pad), rows, pad, dot(normed, projected, TN))
    inputs = tok_ref[...].astype(WIDE)
    scale = rms_scale(inputs)
    gain_attn_grad = jnp.sum(normed_grad * inputs * scale, axis=0, keepdims=True)
    small = jnp.concatenate(
        [
            gain_attn_grad,
            gain_ffn_grad,
            router_ref[0:2, :],
            jnp.concatenate(
                [table_grad, jnp.zeros((heads, width - length), WIDE)], axis=1
            ),
        ],
        axis=0,
    ).astype(LOW)
    for j in range(size):
        grads[j // 2, j % 2, 2 * pad : 2 * pad + SMALL, :] = small

    kept = got
    scatter = Scatter(place, kept.at[:, window], *rest)

    def swap(k):
        return remote(
            grads.at[k, 1 - core], got.at[k], p_send.at[k], p_recv.at[k], partner
        )

    order = [(j, e) for j in range(outer - 1, -1, -1) for e in range(1, inner)]
    order += [(j, 0) for j in range(outer - 1, -1, -1)]
    for j, e in order:
        swap(place.source(place.line(j), e)).start()
    bent = normed_grad * sum_ref[0:1, :]
    input_ref[...] = (
        hidden_grad
        + scale * bent
        - inputs * (scale * scale * scale) * jnp.mean(bent * inputs, axis=1, keepdims=True)
    )

    def item(n):
        side = max(inner - 1, 1)
        j = n - outer * (inner - 1)
        e = jnp.where(j < 0, 1 + lax.rem(n, side), 0)
        j = outer - 1 - jnp.where(j < 0, lax.div(n, side), j)
        return place.line(j), e

    def end(who):
        return pl.ds(pl.multiple_of((depth - shared) * who, 16), shared)

    def give(k):
        return remote(
            kept.at[k, end(1 - rep)], x_got.at[k], x_send.at[k], x_recv.at[k], {"rep": 1 - rep}
        )

    def cross(n, carry):
        @pl.when(n < chips)
        def _():
            far, e = item(n)
            k = place.source(far, e)
            swap(k).wait_recv()
            kept[k] = (grads[k, core].astype(WIDE) + got[k].astype(WIDE)).astype(LOW)
            if shared:
                give(k).start()

        @pl.when(n > 1)
        def _():
            far, e = item(n - 2)
            k = place.source(far, e)
            if shared:
                give(k).wait_recv()
                kept[k, end(rep)] = (
                    kept[k, end(rep)].astype(WIDE) + x_got[k].astype(WIDE)
                ).astype(LOW)

            @pl.when(e > 0)
            def _():
                scatter.across(far, e).start()

        return carry

    strips_off()
    lax.fori_loop(0, chips + 2, cross, 0)
    for j in range(outer - 3 if outer > 2 else outer - 1, -1, -1):
        ret_collect(j)
    layer_ref[...] = (hidden + gate * ret_ref[...]).astype(LOW)
    own.wait()
    for copy in moves:
        copy.wait_recv()
    turns = []
    for f in range(1, reps):
        turns.append(
            remote(
                strips.at[rep],
                strips.at[rep],
                t_send.at[f - 1],
                t_recv.at[f - 1],
                {"rep": lax.rem(rep + f, reps)},
            )
        )
        turns[-1].start()

    def term(k, at):
        at = pl.ds(pl.multiple_of(lead + at.start, 16), 16)
        return kept[k, at].astype(WIDE)

    def pass_on(n, carry):
        scatter.collect(outer - 1 - n, False, term, None)
        return carry

    lax.fori_loop(0, outer - 1, pass_on, 0)

    def give_sum():
        rep_all[rep] = scatter.acc[...].astype(LOW)

    scatter.collect(0, True, term, give_sum)
    swaps = []
    for f in range(1, reps):
        swaps.append(
            remote(
                rep_all.at[rep],
                rep_all.at[rep],
                r_send.at[f - 1],
                r_recv.at[f - 1],
                {"rep": lax.rem(rep + f, reps)},
            )
        )
        swaps[-1].start()
    for copy in turns:
        copy.wait()
    for k in range(chips):
        if swapped:
            for e in range(2):
                g1_out_ref[e, :, k * strip : (k + 1) * strip] = strips[e, k].astype(WIDE)
            continue
        value = strips[0, k].astype(WIDE)
        for r in range(1, reps):
            value = value + strips[r, k].astype(WIDE)
        for e in range(2):
            g1_out_ref[e, :, k * strip : (k + 1) * strip] = value[
                :rows, e * strip : (e + 1) * strip
            ]
    for copy in swaps:
        copy.wait()
    if shared:
        both = depth - 2 * shared
        value = jnp.concatenate(
            [
                rep_all[0, :shared].astype(WIDE),
                rep_all[0, shared:].astype(WIDE) + rep_all[1, :both].astype(WIDE),
                rep_all[1, both:].astype(WIDE),
            ],
            axis=0,
        )
    else:
        value = rep_all[0].astype(WIDE)
        for r in range(1, reps):
            value = value + rep_all[r].astype(WIDE)
    for k in range(3):
        in_out_ref[k] = value[spot_of(k, pad) : spot_of(k, pad) + rows]
    out_out_ref[...] = value[spot_of(3, pad) : spot_of(3, pad) + rows]
    small_out_ref[...] = value[2 * pad : 2 * pad + SMALL]
    for copy in moves:
        copy.wait_send()
    for k in range(chips):
        swap(k).wait_send()
        if shared:
            give(k).wait_send()
    scatter.finish()


def layer_kernel(size, reps, heads, counts, *refs):
    groups = []
    for count in counts:
        groups.append(refs[:count])
        refs = refs[count:]
    inputs, outputs, loads, load_sem, front, front_sems, expert, u_sems, back = groups
    tokens, cotangent, attn_in, attn_out, gains, router, table, routes = inputs[:8]
    strips, halves, buckets, lengths = inputs[8:]
    layer_out, input_grad, in_out, out_out, small_out, g1_out, g2_out = outputs
    whole, w1, w2, normed, proj, probs, context, hidden, ffn, totals, columns = front
    x_local, u_local, returned, norm_grad, router_grad, g1 = loads
    place = Place(size)
    rows = attn_out.shape[0]
    u_gather = Gather(place, u_local, expert[1], *u_sems)
    get = [
        pltpu.make_async_copy(cotangent, u_local, load_sem[0].at[0]),
        pltpu.make_async_copy(tokens, x_local, load_sem[0].at[1]),
    ]
    for copy in get:
        copy.start()

    def more(stage, strips_on=None):
        if stage == 0:
            for copy in get:
                copy.wait()
            u_gather.start()
        elif place.outer > 1:
            u_gather.arrive_z(1)
        if stage == 1:
            strips_on(0)

    strips_on, strips_here, front_finish = front_part(
        place,
        reps,
        heads,
        more,
        x_local,
        attn_in,
        attn_out,
        gains,
        router,
        table,
        routes,
        strips,
        halves,
        buckets,
        lengths,
        *front,
        *front_sems,
    )
    ret_collect, expert_finish = expert_part(
        place,
        reps,
        rows,
        strips_on,
        strips_here,
        u_gather,
        ffn,
        u_local,
        w1,
        w2,
        totals,
        columns,
        returned,
        norm_grad,
        router_grad,
        g1,
        g2_out,
        *expert,
    )
    front_finish()
    back_part_of(
        place,
        reps,
        heads,
        rows,
        x_local,
        u_local,
        hidden,
        ffn,
        normed,
        proj,
        probs,
        context,
        whole,
        totals,
        routes,
        buckets,
        ret_collect,
        returned,
        norm_grad,
        router_grad,
        g1,
        layer_out,
        input_grad,
        in_out,
        out_out,
        small_out,
        g1_out,
        *back,
    )
    expert_finish()


def layer(size, reps, heads, pad, strip, *operands):
    chips = size // 2
    length, width = operands[0].shape
    rows = operands[3].shape[0]
    half = operands[9].shape[1]
    cols = 2 * strip
    depth = 4 * pad + SMALL
    block = (chips, length, width)
    wide = (chips, length, cols)
    row = (length, width)
    weights = (chips, depth, width)
    others = max(reps - 1, 1)
    swapped = reps == 2 and strip % 128 == 0
    outputs = (
        jax.ShapeDtypeStruct(row, LOW),
        jax.ShapeDtypeStruct(row, WIDE),
        jax.ShapeDtypeStruct((3, rows, width), WIDE),
        jax.ShapeDtypeStruct((rows, width), WIDE),
        jax.ShapeDtypeStruct((SMALL, width), WIDE),
        jax.ShapeDtypeStruct((2, rows, chips * strip), WIDE),
        jax.ShapeDtypeStruct((2, half, width), WIDE),
    )
    loads = [
        pltpu.VMEM(row, LOW),
        pltpu.VMEM(row, LOW),
        pltpu.VMEM(row, WIDE),
        pltpu.VMEM(row, WIDE),
        pltpu.VMEM((8, width), WIDE),
        pltpu.VMEM((chips, pad, cols), LOW),
    ]
    front = [
        pltpu.VMEM((chips, 2, depth, width), LOW),
        pltpu.VMEM((2, chips, 2, pad, strip), LOW),
        pltpu.VMEM((2, 2, half, width), LOW),
        pltpu.VMEM(row, LOW),
        pltpu.VMEM((3,) + row, LOW),
        pltpu.VMEM((heads, length, length), WIDE),
        pltpu.VMEM(row, LOW),
        pltpu.VMEM(row, WIDE),
        pltpu.VMEM(row, LOW),
        pltpu.VMEM((SMALL, width), WIDE),
        pltpu.VMEM((length, length), WIDE),
    ]
    front_sems = [*Gather.sems(size), *[DMA((chips,))] * 14, DMA, DMA, DMA((2,))]
    expert = [
        pltpu.VMEM(block, LOW),
        pltpu.VMEM(block, LOW),
        pltpu.VMEM(wide, LOW),
        pltpu.VMEM(wide, WIDE),
        pltpu.VMEM(wide, LOW),
        pltpu.VMEM(block, LOW),
        pltpu.VMEM(block, LOW),
        pltpu.VMEM((chips, 2, pad, cols), LOW),
        pltpu.VMEM((2, 2, half, width), LOW),
        pltpu.VMEM((reps, 2, half, width), LOW),
        DMA((2,)),
        DMA((2,)),
        DMA((others,)),
        DMA((others,)),
        DMA((2,)),
        *Gather.sems(size),
        *Scatter.buffers(size, row),
        *[item for n, item in enumerate(Scatter.buffers(size, row)) if n != 3],
    ]
    back = [
        pltpu.VMEM(weights, LOW),
        pltpu.VMEM((1, 16, width), LOW),
        pltpu.VMEM((chips, pad, strip) if swapped else (1, 16, 128), LOW),
        pltpu.VMEM((reps, depth, width), LOW),
        pltpu.VMEM((reps, chips, pad, strip if swapped else cols), LOW),
        DMA((chips,)),
        DMA((chips,)),
        DMA((others,)),
        DMA((others,)),
        DMA((chips,)),
        DMA((chips,)),
        DMA((others,)),
        DMA((others,)),
        DMA((chips,)),
        DMA((chips,)),
        DMA,
        *Scatter.buffers(size, (depth, width)),
    ]
    load_sem = [DMA((2,))]
    scratch = [loads, load_sem, front, front_sems, expert, Gather.sems(size), back]
    counts = [len(operands), len(outputs), *[len(group) for group in scratch]]
    far = pl.BlockSpec(memory_space=pl.ANY)
    return pl.pallas_call(
        functools.partial(layer_kernel, size, reps, heads, counts),
        out_shape=outputs,
        in_specs=[far, far, *[VMEM] * 6, far, far, VMEM, SMEM],
        out_specs=[VMEM] * len(outputs),
        scratch_shapes=[item for group in scratch for item in group],
        compiler_params=pltpu.CompilerParams(
            collective_id=0, has_side_effects=True, vmem_limit_bytes=62 << 20
        ),
    )(*operands)


def shards(
    size,
    reps,
    tokens,
    cotangent,
    lengths,
    routes,
    bucket_ids,
    attn_in,
    attn_out,
    gains,
    router,
    rel_table,
    expert_in,
    expert_out,
):
    length, width = tokens.shape
    heads = rel_table.shape[1]
    table_rows = rel_table.shape[0]
    chips = size // 2
    rows = attn_out.shape[0]
    pad = rows + -rows % 16
    hidden_units = expert_in.shape[2]
    strip = hidden_units // chips
    half = expert_out.shape[1]
    me = lax.axis_index("shard")

    strips = expert_in
    if strip % 128 or pad != rows:
        strips = jnp.transpose(expert_in.reshape(2, rows, chips, strip), (2, 0, 1, 3))
        strips = jnp.pad(strips, ((0, 0), (0, 0), (0, pad - rows), (0, 0)))
    layer_out, input_grad, in_shard, out_shard, sums, expert_in_grad, expert_out_grad = layer(
        size,
        reps,
        heads,
        pad,
        strip,
        tokens,
        cotangent,
        attn_in,
        attn_out,
        gains,
        router.T,
        rel_table,
        routes.reshape(1, -1),
        strips,
        expert_out,
        bucket_ids.reshape(1, -1),
        lengths,
    )
    picked = lax.dynamic_slice(sums, (0, me * rows), (4, rows))
    table_shard = lax.dynamic_slice(sums, (4, me * table_rows), (heads, table_rows)).T
    return (
        layer_out,
        input_grad,
        in_shard,
        out_shard,
        picked[:2],
        picked[2:].T,
        table_shard,
        expert_in_grad,
        expert_out_grad,
    )


def solution(mesh):
    placed = (
        P(("rep", "shard"), None),
        P(("rep", "shard"), None),
        P(("rep", "shard"), None),
        P(("rep", "shard"), None),
        P(),
        P(None, "shard", None),
        P("shard", None),
        P(None, "shard"),
        P("shard", None),
        P("shard", None),
        P(None, "shard", None),
        P(None, "shard", None),
    )
    return jax.shard_map(
        functools.partial(shards, mesh.shape["shard"], mesh.shape["rep"]),
        mesh=mesh,
        in_specs=placed,
        out_specs=(
            P(("rep", "shard"), None),
            P(("rep", "shard"), None),
            P(None, "shard", None),
            P("shard", None),
            P(None, "shard"),
            P("shard", None),
            P("shard", None),
            P(None, "shard", None),
            P(None, "shard", None),
        ),
        check_vma=False,
    )
```

```python
import functools

import jax
import jax.numpy as jnp
from jax import lax
from jax.experimental import pallas as pl
from jax.experimental.pallas import tpu as pltpu
from jax.sharding import PartitionSpec as P

EPSILON = 1e-06
SMALL = 16
LOW = jnp.bfloat16
WIDE = jnp.float32
NT = (((1,), (1,)), ((), ()))
TN = (((0,), (0,)), ((), ()))
MESH = pl.DeviceIdType.MESH
VMEM = pl.BlockSpec(memory_space=pltpu.VMEM)
SMEM = pl.BlockSpec(memory_space=pltpu.SMEM)
DMA = pltpu.SemaphoreType.DMA


def grid_of(size):
    chips = size // 2
    outer = 4 if chips % 4 == 0 else 1
    return outer, chips // outer


class Place:
    def __init__(self, size):
        self.size = size
        self.outer, self.inner = grid_of(size)
        self.chips = size // 2
        me = lax.axis_index("shard")
        self.index = me
        self.core = lax.rem(me, 2)
        self.chip = lax.div(me, 2)
        self.z = lax.div(self.chip, self.inner)
        self.y = lax.rem(self.chip, self.inner)

    def at(self, dz, dy):
        far = lax.rem(self.z + dz + self.outer, self.outer)
        near = lax.rem(self.y + dy + self.inner, self.inner)
        return far * self.inner + near

    def device(self, chip):
        return {"shard": chip * 2 + self.core}

    def partner(self):
        return {"shard": self.chip * 2 + 1 - self.core}

    def pairs(self):
        return [(d, e) for d in range(self.outer) for e in range(self.inner)]

    def line(self, j):
        z, top = self.z, self.outer - 1
        short = jnp.minimum(z, top - z)
        t = lax.div(j + 1, 2)
        near = jnp.where(lax.rem(j, 2) == 1, z - t, z + t)
        far = jnp.where(z <= top - z, z + j - short, z - j + short)
        return jnp.where(j <= 2 * short, near, far)

    def source(self, far, e):
        return far * self.inner + lax.rem(self.y - e + self.inner, self.inner)

    def pair(self, i):
        q, r = lax.div(i + self.inner - 1, self.inner) - 1, lax.rem(i + self.inner - 1, self.inner)
        last = q == self.outer - 1
        e = jnp.where(last, r + 1, r)
        j = jnp.where(last, q, jnp.where(r == 0, q + 1, q))
        return jnp.where(i == 0, 0, j), jnp.where(i == 0, 0, e)

    def greet(self, chips, reps):
        barrier = pltpu.get_barrier_semaphore()
        count = 0

        def signal(target):
            pl.semaphore_signal(barrier, inc=1, device_id=target, device_id_type=MESH)

        for dz, dy in self.pairs()[1:]:
            if chips or dz == 0:
                signal(self.device(self.at(dz, dy)))
                count += 1
        signal(self.partner())
        count += 1
        if not chips:
            below = jnp.where(self.z > 0, 1, 0)
            above = jnp.where(self.z < self.outer - 1, 1, 0)

            @pl.when(self.z > 0)
            def _():
                signal(self.device(self.chip - self.inner))

            @pl.when(self.z < self.outer - 1)
            def _():
                signal(self.device(self.chip + self.inner))

            count = count + below + above
        for f in range(1, reps):
            signal({"rep": lax.rem(lax.axis_index("rep") + f, reps)})
            count += 1
        pl.semaphore_wait(barrier, count)


def remote(src, dst, send_sem, recv_sem, target):
    return pltpu.make_async_remote_copy(
        src_ref=src,
        dst_ref=dst,
        send_sem=send_sem,
        recv_sem=recv_sem,
        device_id=target,
        device_id_type=MESH,
    )


def dot(a, b, dims=None):
    if dims is None:
        return jnp.dot(a, b, preferred_element_type=WIDE)
    return lax.dot_general(a, b, dims, preferred_element_type=WIDE)


def joined(ref, first, rows, pad):
    chips, _, _, width = ref.shape
    if rows == pad:
        return ref[:, :, first : first + rows, :].reshape(chips * 2 * rows, width)
    parts = [ref[j // 2, j % 2, first : first + rows, :].astype(WIDE) for j in range(chips * 2)]
    return jnp.concatenate(parts, axis=0).astype(LOW)


def split(ref, first, rows, pad, values):
    chips, _, _, width = ref.shape
    if rows == pad:
        ref[:, :, first : first + rows, :] = values.reshape(chips, 2, rows, width).astype(LOW)
        return
    for j in range(chips * 2):
        ref[j // 2, j % 2, first : first + rows, :] = values[j * rows : (j + 1) * rows].astype(LOW)


def rms_scale(values):
    return lax.rsqrt(jnp.mean(values * values, axis=1, keepdims=True) + EPSILON)


def gate_of(logits, route):
    first, second = logits[:, 2:3], logits[:, 3:4]
    top = jnp.maximum(first, second)
    first, second = jnp.exp(first - top), jnp.exp(second - top)
    total = first + second
    first, second = first / total, second / total
    return first, second, jnp.where(route > 0.5, second, first)


class Gather:
    def __init__(self, place, own, slots, up_send, down_send, z_recv, y_send, y_recv):
        self.place, self.own, self.slots = place, own, slots
        self.up_send, self.down_send, self.z_recv = up_send, down_send, z_recv
        self.y_send, self.y_recv = y_send, y_recv

    @staticmethod
    def sems(size):
        outer, inner = grid_of(size)
        side = max(inner - 1, 1)
        return [DMA((outer,))] * 3 + [DMA((outer, side))] * 2

    def up(self, src, far):
        place = self.place
        slot = self.slots.at[place.source(far, 0)]
        target = place.device(place.chip + place.inner)
        return remote(src, slot, self.up_send.at[far], self.z_recv.at[far], target)

    def down(self, src, far):
        place = self.place
        slot = self.slots.at[place.source(far, 0)]
        target = place.device(place.chip - place.inner)
        return remote(src, slot, self.down_send.at[far], self.z_recv.at[far], target)

    def across(self, src, far, e):
        place = self.place
        slot = self.slots.at[place.source(far, 0)]
        target = place.device(place.at(0, e))
        return remote(
            src, slot, self.y_send.at[far, e - 1], self.y_recv.at[far, e - 1], target
        )

    def spread(self, src, far, own):
        place = self.place

        @pl.when(place.z < place.outer - 1 if own else jnp.logical_and(far < place.z, place.z < place.outer - 1))
        def _():
            self.up(src, far).start()

        @pl.when(place.z > 0 if own else jnp.logical_and(far > place.z, place.z > 0))
        def _():
            self.down(src, far).start()

        for e in range(1, place.inner):
            self.across(src, far, e).start()

    def start(self):
        self.spread(self.own, self.place.z, True)

    def arrive_z(self, j):
        far = self.place.line(j)
        source = self.place.source(far, 0)
        slot = self.slots.at[source]
        remote(
            self.own, slot, self.up_send.at[far], self.z_recv.at[far], self.place.partner()
        ).wait_recv()
        self.spread(slot, far, False)
        return source

    def arrive_y(self, j, e):
        far = self.place.line(j)
        source = self.place.source(far, e)
        remote(
            self.own,
            self.slots.at[source],
            self.y_send.at[far, e - 1],
            self.y_recv.at[far, e - 1],
            self.place.partner(),
        ).wait_recv()
        return source

    def arrive(self, j, e):
        @pl.when(jnp.logical_and(j > 0, e == 0))
        def _():
            self.arrive_z(j)

        @pl.when(e > 0)
        def _():
            self.arrive_y(j, e)

        return self.place.source(self.place.line(j), e)

    def finish(self):
        place = self.place

        def sent(far, carry):
            @pl.when(jnp.logical_and(far <= place.z, place.z < place.outer - 1))
            def _():
                self.up(self.own, far).wait_send()

            @pl.when(jnp.logical_and(far >= place.z, place.z > 0))
            def _():
                self.down(self.own, far).wait_send()

            for e in range(1, place.inner):
                self.across(self.own, far, e).wait_send()
            return carry

        lax.fori_loop(0, place.outer, sent, 0)


class Scatter:
    def __init__(self, place, part, y_buf, z_out, z_in, acc, y_send, y_recv, z_send, z_recv):
        self.place, self.part, self.acc = place, part, acc
        self.y_buf, self.z_out, self.z_in = y_buf, z_out, z_in
        self.y_send, self.y_recv, self.z_send, self.z_recv = y_send, y_recv, z_send, z_recv

    @staticmethod
    def buffers(size, block):
        outer, inner = grid_of(size)
        side = max(inner - 1, 1)
        return [
            pltpu.VMEM((outer, side) + block, LOW),
            pltpu.VMEM((max(outer - 1, 1),) + block, LOW),
            pltpu.VMEM((outer + 1,) + block, LOW),
            pltpu.VMEM(block, WIDE),
            DMA((outer, side)),
            DMA((outer, side)),
            DMA((outer,)),
            DMA((2, outer)),
        ]

    def across(self, far, e):
        place = self.place
        return remote(
            self.part.at[place.source(far, e)],
            self.y_buf.at[far, e - 1],
            self.y_send.at[far, e - 1],
            self.y_recv.at[far, e - 1],
            place.device(place.at(0, -e)),
        )

    def slot(self, far, way, z):
        return far if way == 0 else jnp.where(far == z, self.place.outer, far)

    def leave(self, far):
        return jnp.where(far < self.place.z, far, jnp.maximum(far - 1, 0))

    def along(self, far, way, z=None):
        place = self.place
        target = place.chip + (place.inner if way == 0 else -place.inner)
        if z is None:
            z = place.z + (1 if way == 0 else -1)
        return remote(
            self.z_out.at[self.leave(far)],
            self.z_in.at[self.slot(far, way, z)],
            self.z_send.at[far],
            self.z_recv.at[way, far],
            place.device(target),
        )

    def collect(self, j, last, first_term, give):
        place, acc = self.place, self.acc
        far = place.line(j)
        count = acc.shape[0] // 16
        for e in range(1, place.inner):
            self.across(far, e).wait_recv()

        def rows(n):
            return pl.ds(pl.multiple_of(n * 16, 16), 16)

        def begin(n, carry):
            value = first_term(place.source(far, 0), rows(n))
            for e in range(1, place.inner):
                value = value + self.y_buf[far, e - 1, rows(n)].astype(WIDE)
            acc[rows(n)] = value
            return carry

        lax.fori_loop(0, count, begin, 0, unroll=True)
        for way in range(2):
            more = place.z > 0 if way == 0 else place.z < place.outer - 1
            if not last:
                more = jnp.logical_and(more, far > place.z if way == 0 else far < place.z)

            @pl.when(more)
            def _(way=way):
                self.along(far, way, place.z).wait_recv()

                def add(n, carry):
                    acc[rows(n)] += self.z_in[self.slot(far, way, place.z), rows(n)].astype(WIDE)
                    return carry

                lax.fori_loop(0, count, add, 0, unroll=True)

        if last:
            give()
            return
        self.z_out[self.leave(far)] = acc[...].astype(LOW)

        @pl.when(far > place.z)
        def _():
            self.along(far, 0).start()

        @pl.when(far < place.z)
        def _():
            self.along(far, 1).start()

    def finish(self):
        place = self.place

        def sent(far, carry):
            for e in range(1, place.inner):
                self.across(far, e).wait_send()

            @pl.when(far != place.z)
            def _():
                self.along(far, 0).wait_send()

            return carry

        lax.fori_loop(0, place.outer, sent, 0)


def shared_rows(depth, reps):
    return depth * 5 // 256 * 16 if reps == 2 else 0


def spot_of(section, pad):
    return section * pad + (SMALL if section > 1 else 0)


def padded(ref):
    return jnp.concatenate([ref[...], jnp.full((1, 1), -1, jnp.int32)], axis=1)


def column(line):
    count = line.shape[1]
    return jnp.transpose(jnp.broadcast_to(line, (count, count)))[:, :1]


def placing(count, width, first):
    row = lax.broadcasted_iota(jnp.int32, (count, width), 0)
    col = lax.broadcasted_iota(jnp.int32, (count, width), 1)
    return jnp.where(col == row + first, 1.0, 0.0).astype(LOW)


def front_part(
    place,
    reps,
    heads,
    more,
    tok_ref,
    in_ref,
    out_ref,
    gain_ref,
    router_ref,
    table_ref,
    here_ref,
    strip_ref,
    half_ref,
    bucket_ref,
    length_ref,
    whole_ref,
    w1_ref,
    w2_ref,
    normed_ref,
    proj_ref,
    probs_ref,
    context_ref,
    hidden_ref,
    ffn_ref,
    sum_ref,
    route_ref,
    g_up,
    g_down,
    g_z,
    g_send,
    g_recv,
    c_send,
    c_recv,
    e_send,
    e_recv,
    x_send,
    x_recv,
    s_send,
    s_recv,
    f_send,
    f_recv,
    n_send,
    n_recv,
    d_send,
    d_recv,
    h_send,
    h_recv,
    own_sem,
):
    size, chips = place.size, place.chips
    core, chip = place.core, place.chip
    length, width = tok_ref.shape
    rows = out_ref.shape[0]
    pad = w1_ref.shape[3]
    strip = w1_ref.shape[4]
    head_size = width // heads
    depth = whole_ref.shape[2]
    shared = shared_rows(depth, reps)
    rep = lax.axis_index("rep") if shared else 0
    window = pl.ds(pl.multiple_of(shared * rep, 16), depth - shared)
    for k in range(3):
        whole_ref[chip, core, spot_of(k, pad) : spot_of(k, pad) + rows, :] = in_ref[k]
    whole_ref[chip, core, spot_of(3, pad) : spot_of(3, pad) + rows, :] = out_ref[...]
    spot = placing(rows, width, place.index * rows)
    table_rows = table_ref.shape[0]
    here = jnp.broadcast_to(here_ref[...].astype(WIDE), (heads, length))
    lower = jnp.concatenate(
        [
            dot(table_ref[...], placing(table_rows, length, place.index * table_rows), TN),
            here,
            jnp.zeros((heads, width - 2 * length), WIDE),
        ],
        axis=1,
    )
    small = jnp.concatenate(
        [dot(gain_ref[...], spot), dot(router_ref[...], spot), lower], axis=0
    )
    whole_ref[chip, core, 2 * pad : 2 * pad + SMALL, :] = small.astype(LOW)
    place.greet(True, reps)
    partner = place.partner()
    slots = whole_ref.at[:, core, window]
    gather = Gather(place, slots.at[chip], slots, g_up, g_down, g_z, g_send, g_recv)
    gather.start()

    def dup(source):
        block = whole_ref.at[source, core, window]
        return remote(block, block, c_send.at[source], c_recv.at[source], partner)

    def end(who):
        return pl.ds(pl.multiple_of((depth - shared) * who, 16), shared)

    def dup_end(source):
        block = whole_ref.at[source, core, end(1 - rep)]
        return remote(block, block, e_send.at[source], e_recv.at[source], partner)

    def give(source, who):
        block = whole_ref.at[source, core, end(who)]
        target = {"rep": 1 - rep}
        return remote(block, block, x_send.at[source], x_recv.at[source], target)

    swapped = shared and strip % 128 == 0 and rows == pad

    def strip_of(k, which):
        if strip % 128 == 0 and rows == pad:
            return strip_ref.at[which, :, pl.ds(pl.multiple_of(k * strip, 128), strip)]
        return strip_ref.at[k]

    mine = rep if swapped else slice(None)
    theirs = 1 - rep

    dup(chip).start()
    if shared:
        dup_end(chip).start()
    local = [
        pltpu.make_async_copy(strip_of(chip, slice(None)), w1_ref.at[:, chip, core], own_sem.at[0]),
        pltpu.make_async_copy(half_ref, w2_ref.at[:, core], own_sem.at[1]),
    ]
    for copy in local:
        copy.start()
    halves = remote(half_ref, w2_ref.at[:, core], h_send, h_recv, partner)
    halves.start()

    def arrive(i, carry):
        j, e = place.pair(i)
        source = gather.arrive(j, e)
        if shared:
            give(source, rep).start()
        dup(source).start()
        if shared:

            @pl.when(i > 2)
            def _():
                take(i - 2)

        return carry

    def take(i):
        j, e = place.pair(i)
        source = place.source(place.line(j), e)
        give(source, 1 - rep).wait_recv()
        dup_end(source).start()

    late = chips - 2 * (place.inner - 1)
    lax.fori_loop(1, late, arrive, 0)
    strips = []
    for i, (d, e) in enumerate(place.pairs()):
        if i > 0:
            target = place.at(d, e)
            copy = remote(
                strip_of(target, mine),
                w1_ref.at[mine, chip, core],
                s_send.at[i],
                s_recv.at[i],
                place.device(target),
            )
            copy.start()
            strips.append(copy)
    lax.fori_loop(late, chips, arrive, 0)
    if shared:
        for i in range(chips - 2, chips):
            take(i)

    def other(source, carry):
        block = whole_ref.at[source, 1 - core, window]
        remote(block, block, c_send.at[source], c_recv.at[source], partner).wait_recv()
        if shared:
            block = whole_ref.at[source, 1 - core, end(1 - rep)]
            remote(block, block, e_send.at[source], e_recv.at[source], partner).wait_recv()
        return carry

    more(0)
    lax.fori_loop(0, chips, other, 0)

    total = jnp.zeros((SMALL, width), WIDE)
    for j in range(size):
        total = total + whole_ref[j // 2, j % 2, 2 * pad : 2 * pad + SMALL, :].astype(WIDE)
    sum_ref[...] = total
    lines = [
        whole_ref[k, core, 2 * pad : 2 * pad + SMALL, length : 2 * length].astype(WIDE)[4:5]
        for k in range(chips)
    ]
    lines.append(jnp.zeros((length - chips, length), WIDE))
    route_ref[...] = jnp.transpose(jnp.concatenate(lines, axis=0))

    inputs = tok_ref[...].astype(WIDE)
    normed = (inputs * rms_scale(inputs) * total[0:1]).astype(LOW)
    normed_ref[...] = normed
    for k in range(3):
        proj_ref[k] = dot(normed, joined(whole_ref, spot_of(k, pad), rows, pad)).astype(LOW)
    spots = lax.broadcasted_iota(jnp.int32, (length, 2 * length), 0)
    onehot = jnp.where(padded(bucket_ref) == spots, 1.0, 0.0).astype(LOW)
    table = total[:, :length].astype(LOW)
    bias = dot(table, onehot)
    down = lax.broadcasted_iota(jnp.int32, (length, length), 0)
    across = lax.broadcasted_iota(jnp.int32, (length, length), 1)
    part_q = jnp.zeros((length, length), jnp.int32)
    part_k = jnp.zeros((length, length), jnp.int32)
    bound = jnp.int32(0)
    for s in range(length_ref.shape[1]):
        bound = bound + length_ref[0, s]
        part_q = part_q + jnp.where(down >= bound, 1, 0)
        part_k = part_k + jnp.where(across >= bound, 1, 0)
    allowed = part_q == part_k
    def moved(i):
        return place.at(-lax.div(i, place.inner), -lax.rem(i, place.inner))

    def along_x(i, which):
        block = w1_ref.at[which, moved(i), core]
        return remote(block, block, f_send.at[i], f_recv.at[i], {"rep": theirs})

    def to_partner(block, i, send, recv):
        return remote(block, block, send.at[i], recv.at[i], partner)

    def pass_on(i, carry):
        block = w1_ref.at[mine, moved(i), core]
        remote(block, block, s_send.at[i], s_recv.at[i], partner).wait_recv()
        if swapped:
            along_x(i, rep).start()
        to_partner(block, i, d_send, d_recv).start()
        return carry

    def pass_last(i, carry):
        along_x(i, theirs).wait_recv()
        to_partner(w1_ref.at[theirs, moved(i), core], i, n_send, n_recv).start()
        return carry

    def strips_on(stage):
        if stage == 0:
            local[0].wait()
            to_partner(w1_ref.at[:, chip, core], 0, d_send, d_recv).start()
            lax.fori_loop(1, chips, pass_on, 0)
        elif swapped:
            lax.fori_loop(1, chips, pass_last, 0)

    def last(i, carry):
        source = moved(i)

        @pl.when(i > 0)
        def _():
            to_partner(w1_ref.at[mine, source, core], i, d_send, d_recv).wait_send()
            to_partner(w1_ref.at[mine, source, 1 - core], i, d_send, d_recv).wait_recv()
            if swapped:
                to_partner(w1_ref.at[theirs, source, core], i, n_send, n_recv).wait_send()
                to_partner(w1_ref.at[theirs, source, 1 - core], i, n_send, n_recv).wait_recv()

        dup(source).wait_send()
        if shared:
            dup_end(source).wait_send()
        return carry

    def strips_here():
        to_partner(w1_ref.at[:, chip, core], 0, d_send, d_recv).wait_send()
        to_partner(w1_ref.at[:, chip, 1 - core], 0, d_send, d_recv).wait_recv()
        lax.fori_loop(0, chips, last, 0)
        local[1].wait()
        halves.wait()

    def sent(i, carry):
        block = w1_ref.at[mine, chip, core]
        remote(block, block, s_send.at[i], s_recv.at[i], partner).wait_send()
        if shared:
            give(moved(i), rep).wait_send()
        if swapped:
            along_x(i, rep).wait_send()
        return carry

    parts = []
    for h in range(heads):
        if h == 2 * heads // 3:
            more(1, strips_on)
        at = slice(h * head_size, (h + 1) * head_size)
        raw = dot(proj_ref[0, :, at], proj_ref[1, :, at], NT)
        spread = jnp.broadcast_to(bias[4 + h : 5 + h, :], (length, 2 * length))
        skewed = pltpu.roll(spread, length + 1, 1, stride=1, stride_axis=0)
        scores = jnp.where(allowed, raw * 0.125 + skewed[:, :length], -1e30)
        expo = jnp.exp(scores - jnp.max(scores, axis=1, keepdims=True))
        probs = expo / jnp.sum(expo, axis=1, keepdims=True)
        probs_ref[h] = probs
        parts.append(dot(probs.astype(LOW), proj_ref[2, :, at]))
    context = jnp.concatenate(parts, axis=1).astype(LOW)
    context_ref[...] = context
    hidden = inputs + dot(context, joined(whole_ref, spot_of(3, pad), rows, pad))
    hidden_ref[...] = hidden
    ffn_ref[...] = (hidden * rms_scale(hidden) * total[1:2]).astype(LOW)

    def finish():
        lax.fori_loop(1, chips, sent, 0)
        gather.finish()

    return strips_on, strips_here, finish


def expert_part(
    place,
    reps,
    rows,
    strips_on,
    strips_here,
    u_gather,
    x_ref,
    u_ref,
    w1_ref,
    w2_ref,
    sum_ref,
    route_ref,
    ret_ref,
    back_ref,
    router_ref,
    g1_ref,
    g2_ref,
    xs,
    us,
    act,
    slope,
    before_grad,
    ret_part,
    back_part,
    g1_own,
    g2_own,
    g2_all,
    p_send,
    p_recv,
    r_send,
    r_recv,
    own_sem,
    *rest,
):
    chips, outer, inner = place.chips, place.outer, place.inner
    core, chip = place.core, place.chip
    rep = lax.axis_index("rep")
    length, width = x_ref.shape
    strip = w1_ref.shape[4]
    cols = 2 * strip
    pad = g1_own.shape[2]
    partner = place.partner()
    x_gather = Gather(place, x_ref, xs, *rest[:5])
    back_scatter = Scatter(place, back_part, *rest[5:13])
    ret_scatter = Scatter(place, ret_part, *rest[13:16], rest[8], *rest[16:20])
    x_gather.start()
    strips_on(1)
    own = [
        pltpu.make_async_copy(x_ref, xs.at[chip], own_sem.at[0]),
        pltpu.make_async_copy(u_ref, us.at[chip], own_sem.at[1]),
    ]
    for copy in own:
        copy.start()
    for copy in own:
        copy.wait()
    for j in range(2, outer - 1):
        u_gather.arrive_z(j)
    strips_here()

    def w1_of(e):
        if rows == pad:
            return w1_ref[e].reshape(width, strip)
        parts = [w1_ref[e, j // 2, j % 2, :rows].astype(WIDE) for j in range(chips * 2)]
        return jnp.concatenate(parts, axis=0).astype(LOW)

    def w2_of():
        return w2_ref[...].reshape(cols, width)

    lane = lax.broadcasted_iota(jnp.int32, (length, length), 1)
    side = lax.broadcasted_iota(jnp.int32, (length, cols), 1) >= strip
    router = sum_ref[...].astype(LOW)

    def route_of(k):
        return jnp.sum(jnp.where(lane == k, route_ref[...], 0.0), axis=1, keepdims=True)

    def forward(i, carry):
        j, e = place.pair(i)
        k = x_gather.arrive(j, e)
        before = jnp.concatenate([dot(xs[k], w1_of(0)), dot(xs[k], w1_of(1))], axis=1)
        keep = jnp.logical_xor(side, route_of(k) < 0.5)
        square = before * before
        bent = jnp.tanh(0.7978845608 * before * (1.0 + 0.044715 * square))
        half = 0.5 * (1.0 + bent)
        rise = half + 0.5 * before * (1.0 - bent * bent) * 0.7978845608 * (
            1.0 + 0.134145 * square
        )
        active = jnp.where(keep, before * half, 0.0).astype(LOW)
        act[k] = active
        slope[k] = jnp.where(keep, rise, 0.0)
        ret_part[k] = dot(active, w2_of()).astype(LOW)
        return carry

    late = chips - 2 * (inner - 1)
    lax.fori_loop(0, late // 2, forward, 0)
    if outer > 2:
        u_gather.arrive_z(outer - 1)
    lax.fori_loop(late // 2, chips, forward, 0)

    def ret_term(k, at):
        return ret_part[k, at].astype(WIDE)

    def back_term(k, at):
        return back_part[k, at].astype(WIDE)

    def ret_give():
        ret_ref[...] = ret_scatter.acc[...]

    def back_give():
        back_ref[...] = back_scatter.acc[...]

    def ret_collect(j):
        ret_scatter.collect(j, j == 0, ret_term, ret_give)


    def backward(j, e):
        k = place.source(place.line(j), e)
        route = route_of(k)
        first, second, gate = gate_of(dot(xs[k], router, NT), route)
        pulled = dot(us[k], w2_of(), NT)
        us[k] = (gate * us[k].astype(WIDE)).astype(LOW)
        gate_grad = jnp.sum(act[k].astype(WIDE) * pulled, axis=1, keepdims=True)
        grad = (gate * pulled * slope[k]).astype(LOW)
        before_grad[k] = grad
        shared = gate * gate_grad
        first = first * (jnp.where(route > 0.5, 0.0, gate_grad) - shared)
        second = second * (jnp.where(route > 0.5, gate_grad, 0.0) - shared)
        tokens = xs[k].astype(WIDE)
        router_ref[0:1] += jnp.sum(tokens * first, axis=0, keepdims=True)
        router_ref[1:2] += jnp.sum(tokens * second, axis=0, keepdims=True)
        back_part[k] = (
            dot(grad[:, :strip], w1_of(0), NT)
            + dot(grad[:, strip:], w1_of(1), NT)
            + first * sum_ref[2:3, :]
            + second * sum_ref[3:4, :]
        ).astype(LOW)

    router_ref[...] = jnp.zeros_like(router_ref)

    def u_here(n, carry):
        for e in range(1, inner):
            u_gather.arrive_y(n, e)
        return carry

    early = outer - 1 if outer > 1 else 0
    for e in range(1, inner):
        ret_scatter.across(place.line(early), e).start()
    lax.fori_loop(0, outer, u_here, 0)
    u_gather.finish()

    def back_step(n, carry):
        j = outer - 1 - n
        for e in range(1, inner):
            backward(j, e)
            back_scatter.across(place.line(j), e).start()
        backward(j, 0)
        return carry

    lax.fori_loop(0, outer, back_step, 0)
    for j in range(early - 1, -1, -1):
        for e in range(1, inner):
            ret_scatter.across(place.line(j), e).start()

    def flat(ref):
        return ref[...].reshape(chips * length, ref.shape[2])

    g2_swap = remote(g2_own.at[:, 1 - core], g2_all.at[rep], p_send.at[0], p_recv.at[0], partner)
    swaps = []

    def g2_start():
        g2 = dot(flat(act), flat(us), TN)
        g2_own[...] = g2.astype(LOW).reshape(g2_own.shape)
        g2_swap.start()

    def g2_spread():
        g2_swap.wait()
        g2_all[rep] = (g2_own[:, core].astype(WIDE) + g2_all[rep].astype(WIDE)).astype(LOW)
        for f in range(1, reps):
            swaps.append(
                remote(
                    g2_all.at[rep],
                    g2_all.at[rep],
                    r_send.at[f - 1],
                    r_recv.at[f - 1],
                    {"rep": lax.rem(rep + f, reps)},
                )
            )
            swaps[-1].start()

    for j in range(outer - 1, 1, -1):
        back_scatter.collect(j, False, back_term, None)
    g1 = dot(flat(xs), flat(before_grad), TN)
    split(g1_own, 0, rows, pad, g1)
    g1_swap = remote(g1_own.at[:, 1 - core], g1_ref, p_send.at[1], p_recv.at[1], partner)
    g1_swap.start()
    if outer > 1:
        back_scatter.collect(1, False, back_term, None)
    back_scatter.collect(0, True, back_term, back_give)
    g1_swap.wait()
    g1_ref[...] = (g1_own[:, core].astype(WIDE) + g1_ref[...].astype(WIDE)).astype(LOW)

    def finish():
        for copy in swaps:
            copy.wait()
        value = g2_all[0].astype(WIDE)
        for r in range(1, reps):
            value = value + g2_all[r].astype(WIDE)
        g2_ref[...] = value
        x_gather.finish()
        ret_scatter.finish()
        back_scatter.finish()

    return ret_collect, (g2_start, g2_spread), finish


def back_part_of(
    place,
    reps,
    heads,
    rows,
    tok_ref,
    u_ref,
    hidden_ref,
    ffn_ref,
    normed_ref,
    proj_ref,
    probs_ref,
    context_ref,
    whole_ref,
    sum_ref,
    route_ref,
    bucket_ref,
    ret_collect,
    g2_steps,
    ret_ref,
    norm_ref,
    router_ref,
    g1_ref,
    layer_ref,
    input_ref,
    in_out_ref,
    out_out_ref,
    small_out_ref,
    g1_out_ref,
    got,
    x_got,
    g1_got,
    rep_all,
    strips,
    s_send,
    s_recv,
    t_send,
    t_recv,
    p_send,
    p_recv,
    r_send,
    r_recv,
    x_send,
    x_recv,
    own_sem,
    *rest,
):
    size = place.size
    chips, outer, inner = place.chips, place.outer, place.inner
    core, chip = place.core, place.chip
    rep = lax.axis_index("rep")
    length, width = tok_ref.shape
    head_size = width // heads
    depth = got.shape[1]
    pad = (depth - SMALL) // 4
    shared = 0
    lead = pl.multiple_of(shared * rep, 16) if shared else 0
    window = pl.ds(lead, depth - shared)
    partner = place.partner()
    grads = whole_ref
    strip = g1_ref.shape[2] // 2
    swapped = reps == 2 and strip % 128 == 0

    def half(which):
        return pl.ds(pl.multiple_of(which * strip, 128), strip)

    g1_swap = remote(
        g1_ref.at[:, :, half(1 - rep)] if swapped else g1_ref,
        g1_got if swapped else g1_ref,
        x_send.at[0],
        x_recv.at[0],
        {"rep": lax.rem(rep + 1, reps)},
    )
    if swapped:
        g1_swap.start()
    moves = []
    origin = g1_got if swapped else g1_ref
    own = pltpu.make_async_copy(origin.at[chip], strips.at[rep, chip], own_sem)
    for i, (d, e) in enumerate(place.pairs()):
        if i > 0:
            target = place.at(d, e)
            moves.append(
                remote(
                    origin.at[target],
                    strips.at[rep, chip],
                    s_send.at[i],
                    s_recv.at[i],
                    place.device(target),
                )
            )

    def strips_off():
        if swapped:
            g1_swap.wait()
            g1_got[...] = (
                g1_got[...].astype(WIDE) + g1_ref[:, :, half(rep)].astype(WIDE)
            ).astype(LOW)
        for copy in [own, *moves]:
            copy.start()

    upstream = u_ref[...].astype(WIDE)
    hidden = hidden_ref[...]
    route = column(route_ref[...].astype(WIDE))
    gate = gate_of(dot(ffn_ref[...], sum_ref[...].astype(LOW), NT), route)[2]
    norm_grad = norm_ref[...]
    scale = rms_scale(hidden)
    gain_ffn_grad = jnp.sum(norm_grad * hidden * scale, axis=0, keepdims=True)
    bent = norm_grad * sum_ref[1:2, :]
    hidden_grad = (
        upstream
        + scale * bent
        - hidden * (scale * scale * scale) * jnp.mean(bent * hidden, axis=1, keepdims=True)
    )
    attn_grad = hidden_grad.astype(LOW)
    context_grad = dot(attn_grad, joined(whole_ref, spot_of(3, pad), rows, pad), NT).astype(LOW)
    split(grads, spot_of(3, pad), rows, pad, dot(context_ref[...], attn_grad, TN))

    row = lax.broadcasted_iota(jnp.int32, (length, length), 0)
    col = lax.broadcasted_iota(jnp.int32, (length, length), 1)
    mirror = jnp.where(row + col == length - 1, 1.0, 0.0).astype(LOW)
    blank = jnp.zeros((length, length), WIDE)
    parts = [[], [], []]
    diagonals = []
    for h in range(heads):
        if h in (heads // 3, 5 * heads // 6) and outer > 2:
            ret_collect(outer - 1 if h == heads // 3 else outer - 2)
        at = slice(h * head_size, (h + 1) * head_size)
        grad = context_grad[:, at]
        probs = probs_ref[h]
        prob_grad = dot(grad, proj_ref[2, :, at], NT)
        summed = jnp.sum(probs * prob_grad, axis=1, keepdims=True)
        low = (probs * (prob_grad - summed)).astype(LOW)
        flipped = dot(mirror, low)
        skewed = pltpu.roll(
            jnp.concatenate([flipped, blank], axis=1), 0, 1, stride=1, stride_axis=0
        )
        diagonals.append(jnp.sum(skewed, axis=0, keepdims=True))
        parts[0].append(dot(low, proj_ref[1, :, at]) * 0.125)
        parts[1].append(dot(low, proj_ref[0, :, at], TN) * 0.125)
        parts[2].append(dot(probs.astype(LOW), grad, TN))
    diagonal = jnp.concatenate(diagonals, axis=0)
    spots = lax.broadcasted_iota(jnp.int32, (length, 2 * length), 0)
    onehot = jnp.where(padded(bucket_ref) == spots, 1.0, 0.0).astype(LOW)
    high = diagonal.astype(LOW)
    below = (diagonal - high.astype(WIDE)).astype(LOW)
    table_grad = dot(high, onehot, NT) + dot(below, onehot, NT)
    normed = normed_ref[...]
    normed_grad = jnp.zeros((length, width), WIDE)
    for k in range(3):
        projected = jnp.concatenate(parts[k], axis=1).astype(LOW)
        normed_grad = normed_grad + dot(projected, joined(whole_ref, spot_of(k, pad), rows, pad), NT)
        split(grads, spot_of(k, pad), rows, pad, dot(normed, projected, TN))
    inputs = tok_ref[...].astype(WIDE)
    scale = rms_scale(inputs)
    gain_attn_grad = jnp.sum(normed_grad * inputs * scale, axis=0, keepdims=True)
    small = jnp.concatenate(
        [
            gain_attn_grad,
            gain_ffn_grad,
            router_ref[0:2, :],
            jnp.concatenate(
                [table_grad, jnp.zeros((heads, width - length), WIDE)], axis=1
            ),
        ],
        axis=0,
    ).astype(LOW)
    for j in range(size):
        grads[j // 2, j % 2, 2 * pad : 2 * pad + SMALL, :] = small

    kept = got
    scatter = Scatter(place, kept.at[:, window], *rest)

    def swap(k):
        return remote(
            grads.at[k, 1 - core], got.at[k], p_send.at[k], p_recv.at[k], partner
        )

    order = [(j, e) for j in range(outer - 1, -1, -1) for e in range(1, inner)]
    order += [(j, 0) for j in range(outer - 1, -1, -1)]
    for j, e in order:
        swap(place.source(place.line(j), e)).start()
    bent = normed_grad * sum_ref[0:1, :]
    input_ref[...] = (
        hidden_grad
        + scale * bent
        - inputs * (scale * scale * scale) * jnp.mean(bent * inputs, axis=1, keepdims=True)
    )

    def item(n):
        side = max(inner - 1, 1)
        j = n - outer * (inner - 1)
        e = jnp.where(j < 0, 1 + lax.rem(n, side), 0)
        j = outer - 1 - jnp.where(j < 0, lax.div(n, side), j)
        return place.line(j), e

    def end(who):
        return pl.ds(pl.multiple_of((depth - shared) * who, 16), shared)

    def give(k):
        return remote(
            kept.at[k, end(1 - rep)], x_got.at[k], x_send.at[k], x_recv.at[k], {"rep": 1 - rep}
        )

    def cross(n, carry):
        @pl.when(n < chips)
        def _():
            far, e = item(n)
            k = place.source(far, e)
            swap(k).wait_recv()
            kept[k] = (grads[k, core].astype(WIDE) + got[k].astype(WIDE)).astype(LOW)
            if shared:
                give(k).start()

        @pl.when(n > 1)
        def _():
            far, e = item(n - 2)
            k = place.source(far, e)
            if shared:
                give(k).wait_recv()
                kept[k, end(rep)] = (
                    kept[k, end(rep)].astype(WIDE) + x_got[k].astype(WIDE)
                ).astype(LOW)

            @pl.when(e > 0)
            def _():
                scatter.across(far, e).start()

        return carry

    strips_off()
    lax.fori_loop(0, chips + 2, cross, 0)
    g2_steps[0]()
    for j in range(outer - 3 if outer > 2 else outer - 1, -1, -1):
        ret_collect(j)
    layer_ref[...] = (hidden + gate * ret_ref[...]).astype(LOW)
    g2_steps[1]()
    own.wait()
    for copy in moves:
        copy.wait_recv()
    turns = []
    for f in range(1, reps):
        turns.append(
            remote(
                strips.at[rep],
                strips.at[rep],
                t_send.at[f - 1],
                t_recv.at[f - 1],
                {"rep": lax.rem(rep + f, reps)},
            )
        )
        turns[-1].start()

    def term(k, at):
        at = pl.ds(pl.multiple_of(lead + at.start, 16), 16)
        return kept[k, at].astype(WIDE)

    def pass_on(n, carry):
        scatter.collect(outer - 1 - n, False, term, None)
        return carry

    lax.fori_loop(0, outer - 1, pass_on, 0)

    def give_sum():
        rep_all[rep] = scatter.acc[...].astype(LOW)

    scatter.collect(0, True, term, give_sum)
    swaps = []
    for f in range(1, reps):
        swaps.append(
            remote(
                rep_all.at[rep],
                rep_all.at[rep],
                r_send.at[f - 1],
                r_recv.at[f - 1],
                {"rep": lax.rem(rep + f, reps)},
            )
        )
        swaps[-1].start()
    for copy in turns:
        copy.wait()
    for k in range(chips):
        if swapped:
            for e in range(2):
                g1_out_ref[e, :, k * strip : (k + 1) * strip] = strips[e, k].astype(WIDE)
            continue
        value = strips[0, k].astype(WIDE)
        for r in range(1, reps):
            value = value + strips[r, k].astype(WIDE)
        for e in range(2):
            g1_out_ref[e, :, k * strip : (k + 1) * strip] = value[
                :rows, e * strip : (e + 1) * strip
            ]
    for copy in swaps:
        copy.wait()
    if shared:
        both = depth - 2 * shared
        value = jnp.concatenate(
            [
                rep_all[0, :shared].astype(WIDE),
                rep_all[0, shared:].astype(WIDE) + rep_all[1, :both].astype(WIDE),
                rep_all[1, both:].astype(WIDE),
            ],
            axis=0,
        )
    else:
        value = rep_all[0].astype(WIDE)
        for r in range(1, reps):
            value = value + rep_all[r].astype(WIDE)
    for k in range(3):
        in_out_ref[k] = value[spot_of(k, pad) : spot_of(k, pad) + rows]
    out_out_ref[...] = value[spot_of(3, pad) : spot_of(3, pad) + rows]
    small_out_ref[...] = value[2 * pad : 2 * pad + SMALL]
    for copy in moves:
        copy.wait_send()
    for k in range(chips):
        swap(k).wait_send()
        if shared:
            give(k).wait_send()
    scatter.finish()


def layer_kernel(size, reps, heads, counts, *refs):
    groups = []
    for count in counts:
        groups.append(refs[:count])
        refs = refs[count:]
    inputs, outputs, loads, load_sem, front, front_sems, expert, u_sems, back = groups
    tokens, cotangent, attn_in, attn_out, gains, router, table, routes = inputs[:8]
    strips, halves, buckets, lengths = inputs[8:]
    layer_out, input_grad, in_out, out_out, small_out, g1_out, g2_out = outputs
    whole, w1, w2, normed, proj, probs, context, hidden, ffn, totals, columns = front
    x_local, u_local, returned, norm_grad, router_grad, g1 = loads
    place = Place(size)
    rows = attn_out.shape[0]
    u_gather = Gather(place, u_local, expert[1], *u_sems)
    get = [
        pltpu.make_async_copy(cotangent, u_local, load_sem[0].at[0]),
        pltpu.make_async_copy(tokens, x_local, load_sem[0].at[1]),
    ]
    for copy in get:
        copy.start()

    def more(stage, strips_on=None):
        if stage == 0:
            for copy in get:
                copy.wait()
            u_gather.start()
        elif place.outer > 1:
            u_gather.arrive_z(1)
        if stage == 1:
            strips_on(0)

    strips_on, strips_here, front_finish = front_part(
        place,
        reps,
        heads,
        more,
        x_local,
        attn_in,
        attn_out,
        gains,
        router,
        table,
        routes,
        strips,
        halves,
        buckets,
        lengths,
        *front,
        *front_sems,
    )
    ret_collect, g2_steps, expert_finish = expert_part(
        place,
        reps,
        rows,
        strips_on,
        strips_here,
        u_gather,
        ffn,
        u_local,
        w1,
        w2,
        totals,
        columns,
        returned,
        norm_grad,
        router_grad,
        g1,
        g2_out,
        *expert,
    )
    front_finish()
    back_part_of(
        place,
        reps,
        heads,
        rows,
        x_local,
        u_local,
        hidden,
        ffn,
        normed,
        proj,
        probs,
        context,
        whole,
        totals,
        routes,
        buckets,
        ret_collect,
        g2_steps,
        returned,
        norm_grad,
        router_grad,
        g1,
        layer_out,
        input_grad,
        in_out,
        out_out,
        small_out,
        g1_out,
        *back,
    )
    expert_finish()


def layer(size, reps, heads, pad, strip, *operands):
    chips = size // 2
    length, width = operands[0].shape
    rows = operands[3].shape[0]
    half = operands[9].shape[1]
    cols = 2 * strip
    depth = 4 * pad + SMALL
    block = (chips, length, width)
    wide = (chips, length, cols)
    row = (length, width)
    weights = (chips, depth, width)
    others = max(reps - 1, 1)
    swapped = reps == 2 and strip % 128 == 0
    outputs = (
        jax.ShapeDtypeStruct(row, LOW),
        jax.ShapeDtypeStruct(row, WIDE),
        jax.ShapeDtypeStruct((3, rows, width), WIDE),
        jax.ShapeDtypeStruct((rows, width), WIDE),
        jax.ShapeDtypeStruct((SMALL, width), WIDE),
        jax.ShapeDtypeStruct((2, rows, chips * strip), WIDE),
        jax.ShapeDtypeStruct((2, half, width), WIDE),
    )
    loads = [
        pltpu.VMEM(row, LOW),
        pltpu.VMEM(row, LOW),
        pltpu.VMEM(row, WIDE),
        pltpu.VMEM(row, WIDE),
        pltpu.VMEM((8, width), WIDE),
        pltpu.VMEM((chips, pad, cols), LOW),
    ]
    front = [
        pltpu.VMEM((chips, 2, depth, width), LOW),
        pltpu.VMEM((2, chips, 2, pad, strip), LOW),
        pltpu.VMEM((2, 2, half, width), LOW),
        pltpu.VMEM(row, LOW),
        pltpu.VMEM((3,) + row, LOW),
        pltpu.VMEM((heads, length, length), WIDE),
        pltpu.VMEM(row, LOW),
        pltpu.VMEM(row, WIDE),
        pltpu.VMEM(row, LOW),
        pltpu.VMEM((SMALL, width), WIDE),
        pltpu.VMEM((length, length), WIDE),
    ]
    front_sems = [*Gather.sems(size), *[DMA((chips,))] * 14, DMA, DMA, DMA((2,))]
    expert = [
        pltpu.VMEM(block, LOW),
        pltpu.VMEM(block, LOW),
        pltpu.VMEM(wide, LOW),
        pltpu.VMEM(wide, WIDE),
        pltpu.VMEM(wide, LOW),
        pltpu.VMEM(block, LOW),
        pltpu.VMEM(block, LOW),
        pltpu.VMEM((chips, 2, pad, cols), LOW),
        pltpu.VMEM((2, 2, half, width), LOW),
        pltpu.VMEM((reps, 2, half, width), LOW),
        DMA((2,)),
        DMA((2,)),
        DMA((others,)),
        DMA((others,)),
        DMA((2,)),
        *Gather.sems(size),
        *Scatter.buffers(size, row),
        *[item for n, item in enumerate(Scatter.buffers(size, row)) if n != 3],
    ]
    back = [
        pltpu.VMEM(weights, LOW),
        pltpu.VMEM((1, 16, width), LOW),
        pltpu.VMEM((chips, pad, strip) if swapped else (1, 16, 128), LOW),
        pltpu.VMEM((reps, depth, width), LOW),
        pltpu.VMEM((reps, chips, pad, strip if swapped else cols), LOW),
        DMA((chips,)),
        DMA((chips,)),
        DMA((others,)),
        DMA((others,)),
        DMA((chips,)),
        DMA((chips,)),
        DMA((others,)),
        DMA((others,)),
        DMA((chips,)),
        DMA((chips,)),
        DMA,
        *Scatter.buffers(size, (depth, width)),
    ]
    load_sem = [DMA((2,))]
    scratch = [loads, load_sem, front, front_sems, expert, Gather.sems(size), back]
    counts = [len(operands), len(outputs), *[len(group) for group in scratch]]
    far = pl.BlockSpec(memory_space=pl.ANY)
    return pl.pallas_call(
        functools.partial(layer_kernel, size, reps, heads, counts),
        out_shape=outputs,
        in_specs=[far, far, *[VMEM] * 6, far, far, VMEM, SMEM],
        out_specs=[VMEM] * len(outputs),
        scratch_shapes=[item for group in scratch for item in group],
        compiler_params=pltpu.CompilerParams(
            collective_id=0, has_side_effects=True, vmem_limit_bytes=62 << 20
        ),
    )(*operands)


def shards(
    size,
    reps,
    tokens,
    cotangent,
    lengths,
    routes,
    bucket_ids,
    attn_in,
    attn_out,
    gains,
    router,
    rel_table,
    expert_in,
    expert_out,
):
    length, width = tokens.shape
    heads = rel_table.shape[1]
    table_rows = rel_table.shape[0]
    chips = size // 2
    rows = attn_out.shape[0]
    pad = rows + -rows % 16
    hidden_units = expert_in.shape[2]
    strip = hidden_units // chips
    half = expert_out.shape[1]
    me = lax.axis_index("shard")

    strips = expert_in
    if strip % 128 or pad != rows:
        strips = jnp.transpose(expert_in.reshape(2, rows, chips, strip), (2, 0, 1, 3))
        strips = jnp.pad(strips, ((0, 0), (0, 0), (0, pad - rows), (0, 0)))
    layer_out, input_grad, in_shard, out_shard, sums, expert_in_grad, expert_out_grad = layer(
        size,
        reps,
        heads,
        pad,
        strip,
        tokens,
        cotangent,
        attn_in,
        attn_out,
        gains,
        router.T,
        rel_table,
        routes.reshape(1, -1),
        strips,
        expert_out,
        bucket_ids.reshape(1, -1),
        lengths,
    )
    picked = lax.dynamic_slice(sums, (0, me * rows), (4, rows))
    table_shard = lax.dynamic_slice(sums, (4, me * table_rows), (heads, table_rows)).T
    return (
        layer_out,
        input_grad,
        in_shard,
        out_shard,
        picked[:2],
        picked[2:].T,
        table_shard,
        expert_in_grad,
        expert_out_grad,
    )


def solution(mesh):
    placed = (
        P(("rep", "shard"), None),
        P(("rep", "shard"), None),
        P(("rep", "shard"), None),
        P(("rep", "shard"), None),
        P(),
        P(None, "shard", None),
        P("shard", None),
        P(None, "shard"),
        P("shard", None),
        P("shard", None),
        P(None, "shard", None),
        P(None, "shard", None),
    )
    return jax.shard_map(
        functools.partial(shards, mesh.shape["shard"], mesh.shape["rep"]),
        mesh=mesh,
        in_specs=placed,
        out_specs=(
            P(("rep", "shard"), None),
            P(("rep", "shard"), None),
            P(None, "shard", None),
            P("shard", None),
            P(None, "shard"),
            P("shard", None),
            P("shard", None),
            P(None, "shard", None),
            P(None, "shard", None),
        ),
        check_vma=False,
    )
```
